256 devices in a mesh: dp: 128 (over x, z, y), pair: 2 (over core).
Axes of the slice: x: 4, y: 4, z: 8, core: 2. Of those that a mesh axis runs over, the one named last changes fastest.
Arguments:
- pool: bfloat16 [256, 2, 32768], P(None, None, 'dp'), may hold values from -20 to 20, as said below
- crop_ids: int32 [256, 3], replicated, may hold values from 0 to 255
- crop_corners: int32 [256, 3, 3], replicated, may hold values from 0 to 20
- counts: int32 [256], replicated, may hold values from 1 to 3, 512 in all
- conv_first: float32 [27, 32], replicated, may hold values from -1.25 to 1.25
- conv_second: float32 [27, 32, 32], replicated, may hold values from -0.21875 to 0.21875
- norm_gain: float32 [32], replicated, may hold values from 0.25 to 1.75
- head_weight: float32 [32], replicated, may hold values from -1 to 1
- momentum_first: float32 [27, 32], replicated, may hold values from -0.4375 to 0.4375
- momentum_second: float32 [27, 32, 32], replicated, may hold values from -0.0078125 to 0.0078125
- momentum_gain: float32 [32], replicated, may hold values from -0.4375 to 0.4375
- momentum_head: float32 [32], replicated, may hold values from -0.4375 to 0.4375
- variance_first: float32 [27, 32], replicated, may hold values from 0.0001 to 0.01
- variance_second: float32 [27, 32, 32], replicated, may hold values from 0.0001 to 0.01
- variance_gain: float32 [32], replicated, may hold values from 0.0001 to 0.01
- variance_head: float32 [32], replicated, may hold values from 0.0001 to 0.01
Outputs:
- update_first: float32 [27, 32], replicated
- update_second: float32 [27, 32, 32], replicated
- update_gain: float32 [32], replicated
- update_head: float32 [32], replicated
- next_momentum_first: float32 [27, 32], replicated
- next_momentum_second: float32 [27, 32, 32], replicated
- next_momentum_gain: float32 [32], replicated
- next_momentum_head: float32 [32], replicated
The draws below stay inside these ranges and needn't reach their ends.
Inputs may be any that keep to these rules, and one draw needn't show every extreme that they name: `pool`: channel 0 holds intensities, channel 1 boundary targets within 0 to 1. The counts sum to exactly 512, and some row requests 3 crops.
All inputs are finite; a program needn't handle non-finite values.
Results may differ from the reference program's by a relative error of at most 0.0041.
Values may be sent and summed in bfloat16 or wider, within the bound.
A program may use at most 64 MiB of HBM per device.

```python
import math
import jax
import jax.numpy as jnp
import numpy as np
from jax import lax

CH = 32
CROP = 12
BLOCK = 32
MOST = 3
POOL = 256
WORKERS = 256
TOTAL = 512


def draw_pool(key, part):
    key_image = jax.random.fold_in(key, 11)
    key_target = jax.random.fold_in(key, 12)
    intensity = jnp.clip(jax.random.normal(key_image, (POOL, 1, BLOCK ** 3), jnp.float32), -6.0, 6.0)
    target = jax.random.uniform(key_target, (POOL, 1, BLOCK ** 3), jnp.float32, 0.0, 1.0)
    return jnp.concatenate([intensity, target], axis=1).astype(jnp.bfloat16)


def touch_ends(values, key, smallest, top_value):
    longest = values.shape.index(max(values.shape))
    spots = []
    for shift in (0, 1):
        where = [jax.random.randint(jax.random.fold_in(key, axis), (), 0, length) for axis, length in enumerate(values.shape)]
        where[longest] = (where[longest] + shift) % values.shape[longest]
        spots.append(tuple(where))
    return values.at[spots[0]].set(smallest).at[spots[1]].set(top_value)


def length_profile(count, total, limit, slope):
    portions = [(1 << 20) // math.isqrt(grade ** slope) + 1 for grade in range(2, count + 1)]
    surplus, holding = total - limit - (count - 1), [1] * (count - 1)
    while surplus > 0:
        candidates = [i for i in range(count - 1) if holding[i] < limit]
        whole, budget = sum([portions[i] for i in candidates]), surplus
        for i in candidates:
            extra = min(limit - holding[i], max(1, budget * portions[i] // whole), surplus)
            holding[i] = holding[i] + extra
            surplus = surplus - extra
    return np.array([limit] + holding)


def uneven(rng, count, total, reach, skew):
    if count == 2:
        one = jax.random.randint(rng, (), max(1, total - reach), min(reach, total - 1) + 1)
        return jnp.stack([one, total - one])
    lengths = jnp.asarray(length_profile(count, total, reach, skew), jnp.int32)
    pairs = (count - 1) // 2
    donor, sink = lengths[1:1 + 2 * pairs:2], lengths[2:2 + 2 * pairs:2]
    room = jnp.minimum(donor - 1, reach - sink)
    passed = jax.random.randint(jax.random.fold_in(rng, 1), (pairs,), 0, 1 << 20) % (room + 1)
    lengths = lengths.at[1:1 + 2 * pairs:2].set(donor - passed).at[2:2 + 2 * pairs:2].set(sink + passed)
    return lengths[jax.random.permutation(jax.random.fold_in(rng, 2), count)]


def scatter_about(key, extent, scale, bound, kind=jnp.bfloat16):
    values = scale * jax.random.normal(key, extent, jnp.float32)
    return jnp.clip(values, min=-bound, max=bound).astype(kind)


def setup_inputs(seed: int = 0) -> dict:
    keys = jax.random.split(jax.random.key(seed), 17)
    pool = draw_pool(jax.random.fold_in(keys[16], 71), 0)
    crop_ids = touch_ends(jax.random.randint(keys[1], (WORKERS, MOST), 0, POOL), jax.random.fold_in(keys[1], 1), 0, POOL - 1).astype(jnp.int32)
    crop_corners = touch_ends(jax.random.randint(keys[2], (WORKERS, MOST, 3), 0, BLOCK - CROP + 1), jax.random.fold_in(keys[2], 1), 0, BLOCK - CROP).astype(jnp.int32)
    counts = uneven(keys[3], WORKERS, TOTAL, MOST, 2).astype(jnp.int32)
    conv_first = scatter_about(keys[4], (27, CH), 27 ** -0.5, 1.25, jnp.float32)
    conv_second = scatter_about(keys[5], (27, CH, CH), (27 * CH) ** -0.5, 0.21875, jnp.float32)
    norm_gain = jnp.clip(1.0 + 0.15 * jax.random.normal(keys[6], (CH,), jnp.float32), 0.25, 1.75)
    head_weight = scatter_about(keys[7], (CH,), CH ** -0.5, 1.0, jnp.float32)
    momentum_first = scatter_about(keys[8], (27, CH), 0.03, 0.4375, jnp.float32)
    momentum_second = scatter_about(keys[9], (27, CH, CH), 0.0005, 0.0078125, jnp.float32)
    momentum_gain = scatter_about(keys[10], (CH,), 0.03, 0.4375, jnp.float32)
    momentum_head = scatter_about(keys[11], (CH,), 0.03, 0.4375, jnp.float32)
    variance_first = jnp.clip(jnp.exp(jax.random.uniform(keys[12], (27, CH), jnp.float32, math.log(0.0001), math.log(0.01))), 0.0001, 0.01)
    variance_second = jnp.clip(jnp.exp(jax.random.uniform(keys[13], (27, CH, CH), jnp.float32, math.log(0.0001), math.log(0.01))), 0.0001, 0.01)
    variance_gain = jnp.clip(jnp.exp(jax.random.uniform(keys[14], (CH,), jnp.float32, math.log(0.0001), math.log(0.01))), 0.0001, 0.01)
    variance_head = jnp.clip(jnp.exp(jax.random.uniform(keys[15], (CH,), jnp.float32, math.log(0.0001), math.log(0.01))), 0.0001, 0.01)
    return dict(pool=pool, crop_ids=crop_ids, crop_corners=crop_corners, counts=counts, conv_first=conv_first, conv_second=conv_second, norm_gain=norm_gain, head_weight=head_weight, momentum_first=momentum_first, momentum_second=momentum_second, momentum_gain=momentum_gain, momentum_head=momentum_head, variance_first=variance_first, variance_second=variance_second, variance_gain=variance_gain, variance_head=variance_head)


beta_first = 0.9
beta_second = 0.999

def convolve(inputs, kernel, dilation):
    return lax.conv_general_dilated(inputs, kernel, (1, 1, 1), [(dilation, dilation)] * 3, rhs_dilation=(dilation, dilation, dilation), dimension_numbers=('NDHWC', 'DHWIO', 'NDHWC'), preferred_element_type=jnp.float32)

def crop_loss(params, volume, corner):
    conv_first, conv_second, norm_gain, head_weight = params
    window = lax.dynamic_slice(volume, (jnp.int32(0), corner[0], corner[1], corner[2]), (2, CROP, CROP, CROP))
    intensity = window[0].reshape(1, CROP, CROP, CROP, 1)
    target = window[1].astype(jnp.float32).reshape(CROP * CROP * CROP)
    first_map = convolve(intensity, conv_first.astype(jnp.bfloat16).reshape(3, 3, 3, 1, CH), 1)
    hidden = jax.nn.relu(first_map).astype(jnp.bfloat16)
    second = convolve(hidden, conv_second.astype(jnp.bfloat16).reshape(3, 3, 3, CH, CH), 2)
    center = lax.optimization_barrier(jnp.mean(second, axis=(0, 1, 2, 3)))
    spread = lax.optimization_barrier(jnp.mean(jnp.square(second - center), axis=(0, 1, 2, 3)))
    normed = (second - center) * lax.rsqrt(spread + 1e-05) * norm_gain
    joined = (jax.nn.relu(normed) + hidden.astype(jnp.float32)).astype(jnp.bfloat16)
    logits = jnp.dot(joined.reshape(CROP * CROP * CROP, CH), head_weight.astype(jnp.bfloat16), preferred_element_type=jnp.float32)
    return jnp.mean(jax.nn.softplus(logits) - target * logits)

def crop_order(counts, amount):
    starts = jnp.cumsum(counts, dtype=jnp.int32) - counts
    position = jnp.arange(amount, dtype=jnp.int32)
    crop_rows = lax.optimization_barrier(jnp.sum((starts[None, :] <= position[:, None]).astype(jnp.int32), axis=1, dtype=jnp.int32)) - 1
    crop_slots = position - starts[crop_rows]
    return (crop_rows, crop_slots)

def adam_update(gradient, momentum, variance):
    next_momentum = beta_first * momentum + (1.0 - beta_first) * gradient
    next_variance = beta_second * variance + (1.0 - beta_second) * gradient * gradient
    return (next_momentum / (jnp.sqrt(next_variance) + 1e-08), next_momentum)

def reference(pool, crop_ids, crop_corners, counts, conv_first, conv_second, norm_gain, head_weight, momentum_first, momentum_second, momentum_gain, momentum_head, variance_first, variance_second, variance_gain, variance_head):
    params = (conv_first, conv_second, norm_gain, head_weight)
    crop_rows, crop_slots = crop_order(counts, TOTAL)
    gradient_fn = jax.grad(crop_loss)

    def accumulate(summed, position):
        crop_row = crop_rows[position]
        crop_slot = crop_slots[position]
        volume = pool[crop_ids[crop_row, crop_slot]].reshape(2, BLOCK, BLOCK, BLOCK)
        crop_terms = gradient_fn(params, volume, crop_corners[crop_row, crop_slot])
        return (jax.tree.map(jnp.add, summed, crop_terms), None)
    start_sums = tuple((jnp.zeros(tensor.shape, jnp.float32) for tensor in params))
    summed, _ = lax.scan(accumulate, start_sums, jnp.arange(TOTAL, dtype=jnp.int32))
    averaged = tuple((tensor / jnp.float32(TOTAL) for tensor in summed))
    moments = (momentum_first, momentum_second, momentum_gain, momentum_head)
    variances = (variance_first, variance_second, variance_gain, variance_head)
    results = [adam_update(averaged[index], moments[index], variances[index]) for index in range(4)]
    return (results[0][0], results[1][0], results[2][0], results[3][0], results[0][1], results[1][1], results[2][1], results[3][1])
```

```python
import jax
import jax.numpy as jnp
from jax import lax
from jax.experimental import pallas as pl
from jax.experimental.pallas import tpu as pltpu
from jax.sharding import PartitionSpec as P

CH = 32
CROP = 12
BLOCK = 32
MOST = 3
SHARE = 2


beta_first = 0.9
beta_second = 0.999


def convolve(inputs, kernel, dilation):
    return lax.conv_general_dilated(
        inputs,
        kernel,
        (1, 1, 1),
        [(dilation, dilation)] * 3,
        rhs_dilation=(dilation, dilation, dilation),
        dimension_numbers=("NDHWC", "DHWIO", "NDHWC"),
        preferred_element_type=jnp.float32,
    )


def crop_loss(params, volume, corner):
    conv_first, conv_second, norm_gain, head_weight = params
    window = lax.dynamic_slice(
        volume, (jnp.int32(0), corner[0], corner[1], corner[2]), (2, CROP, CROP, CROP)
    )
    intensity = window[0].reshape(1, CROP, CROP, CROP, 1)
    target = window[1].astype(jnp.float32).reshape(CROP * CROP * CROP)
    first_map = convolve(intensity, conv_first.astype(jnp.bfloat16).reshape(3, 3, 3, 1, CH), 1)
    hidden = jax.nn.relu(first_map).astype(jnp.bfloat16)
    second = convolve(hidden, conv_second.astype(jnp.bfloat16).reshape(3, 3, 3, CH, CH), 2)
    center = jnp.mean(second, axis=(0, 1, 2, 3))
    spread = jnp.mean(jnp.square(second - center), axis=(0, 1, 2, 3))
    normed = (second - center) * lax.rsqrt(spread + 1e-05) * norm_gain
    joined = (jax.nn.relu(normed) + hidden.astype(jnp.float32)).astype(jnp.bfloat16)
    logits = jnp.dot(
        joined.reshape(CROP * CROP * CROP, CH),
        head_weight.astype(jnp.bfloat16),
        preferred_element_type=jnp.float32,
    )
    return jnp.mean(jax.nn.softplus(logits) - target * logits)


def adam_update(gradient, momentum, variance):
    next_momentum = beta_first * momentum + (1.0 - beta_first) * gradient
    next_variance = beta_second * variance + (1.0 - beta_second) * gradient * gradient
    return (next_momentum / (jnp.sqrt(next_variance) + 1e-08), next_momentum)


def local_gradients(params, arrived, corners, active):
    volumes = arrived.reshape(arrived.shape[0], 2, BLOCK, BLOCK, BLOCK)
    per_crop = jax.vmap(jax.grad(crop_loss), in_axes=(None, 0, 0))(params, volumes, corners)
    return tuple(
        (
            jnp.sum(stacked * active.reshape((-1,) + (1,) * (stacked.ndim - 1)), axis=0)
            for stacked in per_crop
        )
    )


MESH = pl.DeviceIdType.MESH
ROWS = 16


def plane_peer(k):
    dp = lax.axis_index("dp")
    x = lax.rem(dp // 32 + k // 4, 4)
    y = lax.rem(lax.rem(dp, 4) + k % 4, 4)
    z = lax.rem(dp // 4, 8)
    return (x * 32 + z * 4 + y, lax.axis_index("pair")), x * 4 + y


def column_peer(k):
    dp = lax.axis_index("dp")
    z = lax.rem(lax.rem(dp // 4, 8) + k // 2, 8)
    core = lax.rem(lax.axis_index("pair") + k % 2, 2)
    return ((dp // 32) * 32 + z * 4 + lax.rem(dp, 4), core), z * 2 + core


def sum_kernel(part, out, first, second, send, recv):
    barrier = pltpu.get_barrier_semaphore()
    for k in range(1, 16):
        pl.semaphore_signal(barrier, inc=1, device_id=plane_peer(k)[0], device_id_type=MESH)
        pl.semaphore_signal(barrier, inc=1, device_id=column_peer(k)[0], device_id_type=MESH)
    pl.semaphore_wait(barrier, 30)
    _, plane_me = plane_peer(0)
    _, column_me = column_peer(0)

    def rows(place):
        return pl.ds(pl.multiple_of(place * ROWS, ROWS), ROWS)

    def exchange(stage, peer, source, target):
        copies = []
        for k in range(1, 16):
            device, place = peer(k)
            copy = pltpu.make_async_remote_copy(
                src_ref=source(place), dst_ref=target,
                send_sem=send.at[stage, k], recv_sem=recv.at[stage, k],
                device_id=device, device_id_type=MESH,
            )
            copy.start()
            copies.append(copy)
        return copies

    copies = exchange(0, plane_peer, lambda place: part.at[rows(place)], first.at[plane_me])
    first[plane_me] = part[rows(plane_me)]
    for copy in copies:
        copy.wait()
    total = first[0]
    for k in range(1, 16):
        total = total + first[k]
    second[column_me] = total
    copies = exchange(1, column_peer, lambda place: second.at[column_me], second.at[column_me])
    for copy in copies:
        copy.wait()
    total = second[0]
    for k in range(1, 16):
        total = total + second[k]
    out[rows(plane_me)] = total
    copies = exchange(2, plane_peer, lambda place: out.at[rows(plane_me)], out.at[rows(plane_me)])
    for copy in copies:
        copy.wait()


def sum_everywhere(packed):
    return pl.pallas_call(
        sum_kernel,
        out_shape=jax.ShapeDtypeStruct((16 * ROWS, 128), jnp.float32),
        in_specs=[pl.BlockSpec(memory_space=pltpu.VMEM)],
        out_specs=pl.BlockSpec(memory_space=pltpu.VMEM),
        scratch_shapes=[
            pltpu.VMEM((16, ROWS, 128), jnp.float32),
            pltpu.VMEM((16, ROWS, 128), jnp.float32),
            pltpu.SemaphoreType.DMA((3, 16)),
            pltpu.SemaphoreType.DMA((3, 16)),
        ],
        compiler_params=pltpu.CompilerParams(collective_id=0, has_side_effects=True),
    )(packed)


def shards(
    pool,
    crop_ids,
    crop_corners,
    counts,
    conv_first,
    conv_second,
    norm_gain,
    head_weight,
    momentum_first,
    momentum_second,
    momentum_gain,
    momentum_head,
    variance_first,
    variance_second,
    variance_gain,
    variance_head,
):
    params = (conv_first, conv_second, norm_gain, head_weight)
    dp_count = lax.axis_size("dp")
    pair_count = lax.axis_size("pair")
    dp_index = lax.axis_index("dp")
    pair_index = lax.axis_index("pair")
    own_row = dp_index * pair_count + pair_index
    dest_rows = jnp.arange(dp_count, dtype=jnp.int32) * pair_count + pair_index
    batch_size = jnp.float32(counts.shape[0] * SHARE)
    wanted = crop_ids[dest_rows]
    outgoing = pool[wanted]
    arrived = lax.all_to_all(outgoing, "dp", split_axis=0, concat_axis=3, tiled=True)[0]
    corners = crop_corners[own_row]
    active = (jnp.arange(MOST, dtype=jnp.int32) < counts[own_row]).astype(jnp.float32)
    grad_first, grad_second, grad_gain, grad_head = local_gradients(
        params, arrived, corners, active
    )
    small = jnp.concatenate([grad_first.reshape(-1), grad_gain, grad_head])
    packed = jnp.concatenate(
        [grad_second.reshape(216, 128), jnp.pad(small, (0, 40 * 128 - small.size)).reshape(40, 128)]
    )
    total = sum_everywhere(packed)
    grad_second = total[:216].reshape(27, CH, CH)
    small = total[216:].reshape(-1)
    grad_first = small[: 27 * CH].reshape(27, CH)
    grad_gain = small[27 * CH : 28 * CH]
    grad_head = small[28 * CH : 29 * CH]
    update_second, next_second = adam_update(
        grad_second / batch_size, momentum_second, variance_second
    )
    update_first, next_first = adam_update(grad_first / batch_size, momentum_first, variance_first)
    update_gain, next_gain = adam_update(grad_gain / batch_size, momentum_gain, variance_gain)
    update_head, next_head = adam_update(grad_head / batch_size, momentum_head, variance_head)
    return (
        update_first,
        update_second,
        update_gain,
        update_head,
        next_first,
        next_second,
        next_gain,
        next_head,
    )


def solution(mesh):
    in_specs = (
        P(None, None, "dp"),
        P(),
        P(),
        P(),
        P(),
        P(),
        P(),
        P(),
        P(),
        P(),
        P(),
        P(),
        P(),
        P(),
        P(),
        P(),
    )
    out_specs = (P(), P(), P(), P(), P(), P(), P(), P())
    return jax.shard_map(shards, mesh=mesh, in_specs=in_specs, out_specs=out_specs, check_vma=False)
```

```python
import functools

import jax
import jax.numpy as jnp
from jax import lax
from jax.experimental import pallas as pl
from jax.experimental.pallas import tpu as pltpu
from jax.sharding import PartitionSpec as P

CH = 32
CROP = 12
BLOCK = 32


SIDE = 16
PLANE = SIDE * SIDE
LANES = 2 * PLANE
VOXELS = CROP * CROP * CROP
BAND = 6 * CH


def iota(shape, axis):
    return lax.broadcasted_iota(jnp.int32, shape, axis)


def nt(a, b):
    return lax.dot_general(a, b, (((1,), (1,)), ((), ())), preferred_element_type=jnp.float32)


def nn(a, b):
    return jnp.dot(a, b, preferred_element_type=jnp.float32)


def onehot(condition):
    return jnp.where(condition, 1.0, 0.0).astype(jnp.bfloat16)


def valid_lanes(rows):
    lane = iota((rows, PLANE), 1)
    return (lane % SIDE < CROP) & ((lane // SIDE) % SIDE < CROP)


def shifted(value, offset):
    amount = (-offset) % PLANE
    return pltpu.roll(value, amount, 1) if amount else value


def halves(ref, rows, crop):
    return ref[rows, crop * PLANE : (crop + 1) * PLANE]


def expand_first(conv_first, toeplitz_first):
    weights = conv_first[...].astype(jnp.bfloat16)
    repeat = onehot(iota((12 * CH, CH), 0) % CH == iota((12 * CH, CH), 1))
    row, column = iota((12 * CH, 144), 0), iota((12 * CH, 144), 1)
    place = row // CH
    step = column % 16 - (2 * (place % 6) + place // 6) + 1
    total = jnp.zeros((12 * CH, 144), jnp.float32)
    for dx in range(3):
        tap = onehot(iota((144, 27), 0) // 16 + 9 * dx == iota((144, 27), 1))
        spread = nn(tap, weights).astype(jnp.bfloat16)
        total = jnp.where(step == dx, nt(repeat, spread), total)
    toeplitz_first[...] = total.astype(jnp.bfloat16)


def expand_second(conv_second, forward, backward):
    eye = onehot(iota((CH, CH), 0) == iota((CH, CH), 1))
    for tap in range(9):
        blocks = [conv_second[9 * dx + tap] for dx in range(3)]
        zero = jnp.zeros((CH, 256 - 3 * CH), jnp.float32)
        group = slice(tap * 256, tap * 256 + 256)
        strip = jnp.concatenate([blocks[2], blocks[1], blocks[0], zero], axis=1)
        stacked = jnp.concatenate(blocks, axis=0).astype(jnp.bfloat16)
        turned = jnp.concatenate([nt(eye, stacked), zero], axis=1)
        for i in range(6):
            rows = slice(i * CH, i * CH + CH)
            amount = (CH * (i - 1)) % 256
            moved = pltpu.roll(strip, amount, 1) if amount else strip
            backward[rows, group] = moved.astype(jnp.bfloat16)
            moved = pltpu.roll(turned, amount, 1) if amount else turned
            forward[rows, group] = moved.astype(jnp.bfloat16)


def clear_ends(stack):
    for parity in range(2):
        for tap in range(9):
            stack[parity, tap * 256 + BAND : tap * 256 + 256, :] = jnp.zeros((256 - BAND, LANES), jnp.bfloat16)


def crop_gradients(
    x, t, gain_ref, head_ref, packed,
    toeplitz_first, forward, backward, patches, hidden, hidden_stack, second, logits, cotangent, cotangent_stack,
):
    valid = valid_lanes(1)
    for crop in range(2):
        half = slice(crop * PLANE, (crop + 1) * PLANE)
        source = x[:, half].astype(jnp.float32)
        for tap in range(9):
            offset = SIDE * (tap // 3 - 1) + tap % 3 - 1
            patches[tap * 16 : tap * 16 + 16, half] = shifted(source, offset).astype(jnp.bfloat16)
    for crop in range(2):
        half = slice(crop * PLANE, (crop + 1) * PLANE)
        for parity in range(2):
            rows = slice(parity * BAND, parity * BAND + BAND)
            first_map = nn(toeplitz_first[rows, :], patches[:, half])
            value = jnp.where(valid, jnp.maximum(first_map, 0.0), 0.0)
            hidden[rows, half] = value.astype(jnp.bfloat16)
            for tap in range(9):
                offset = 2 * (SIDE * (tap // 3 - 1) + tap % 3 - 1)
                hidden_stack[parity, tap * 256 : tap * 256 + BAND, half] = shifted(value, offset).astype(jnp.bfloat16)
    for parity in range(2):
        second[parity * BAND : parity * BAND + BAND, :] = nn(forward[...], hidden_stack[parity])
    gain = gain_ref[...]
    head = head_ref[...]
    scale = 1.0 / VOXELS
    columns = []
    for crop in range(2):
        half = slice(crop * PLANE, (crop + 1) * PLANE)
        total = jnp.zeros((CH, PLANE), jnp.float32)
        for m in range(12):
            total = total + second[m * CH : m * CH + CH, half]
        center = jnp.sum(jnp.where(valid, total, 0.0), axis=1, keepdims=True) * scale
        total = jnp.zeros((CH, PLANE), jnp.float32)
        for m in range(12):
            away = second[m * CH : m * CH + CH, half] - center
            total = total + away * away
        spread = jnp.sum(jnp.where(valid, total, 0.0), axis=1, keepdims=True) * scale
        inverse = lax.rsqrt(spread + 1e-05)
        columns.append(inverse)
        for m in range(12):
            rows = slice(m * CH, m * CH + CH)
            hat = (second[rows, half] - center) * inverse
            second[rows, half] = hat
            joined = (jnp.maximum(hat * gain, 0.0) + hidden[rows, half].astype(jnp.float32)).astype(jnp.bfloat16)
            logits[m : m + 1, half] = jnp.sum(joined.astype(jnp.float32) * head, axis=0, keepdims=True)
    slope = 1.0 / (1.0 + jnp.exp(-logits[0:12, :])) - t[...]
    both = jnp.concatenate([valid, valid], axis=1)
    logits[0:12, :] = jnp.where(both, slope * scale, 0.0)
    grad_gain = jnp.zeros((CH, 1), jnp.float32)
    grad_head = jnp.zeros((CH, 1), jnp.float32)
    for crop in range(2):
        half = slice(crop * PLANE, (crop + 1) * PLANE)
        sum_plain = jnp.zeros((CH, PLANE), jnp.float32)
        sum_hat = jnp.zeros((CH, PLANE), jnp.float32)
        sum_head = jnp.zeros((CH, PLANE), jnp.float32)
        for m in range(12):
            rows = slice(m * CH, m * CH + CH)
            hat = second[rows, half]
            normed = hat * gain
            slope = logits[m : m + 1, half]
            joined = (jnp.maximum(normed, 0.0) + hidden[rows, half].astype(jnp.float32)).astype(jnp.bfloat16)
            sum_head = sum_head + joined.astype(jnp.float32) * slope
            passed = jnp.where(normed > 0.0, slope, 0.0)
            sum_plain = sum_plain + passed
            sum_hat = sum_hat + passed * hat
        grad_head = grad_head + jnp.sum(sum_head, axis=1, keepdims=True)
        mean_plain = head * jnp.sum(sum_plain, axis=1, keepdims=True)
        mean_hat = head * jnp.sum(sum_hat, axis=1, keepdims=True)
        grad_gain = grad_gain + mean_hat
        mean_plain = mean_plain * scale
        mean_hat = mean_hat * scale
        factor = columns[crop] * gain
        for parity in range(2):
            for i in range(6):
                m = parity * 6 + i
                rows = slice(m * CH, m * CH + CH)
                hat = second[rows, half]
                slope = logits[m : m + 1, half]
                passed = jnp.where(hat * gain > 0.0, head * slope, 0.0)
                value = jnp.where(valid, factor * (passed - mean_plain - hat * mean_hat), 0.0)
                cotangent[parity, i * CH : i * CH + CH, half] = value.astype(jnp.bfloat16)
                for tap in range(9):
                    offset = -2 * (SIDE * (tap // 3 - 1) + tap % 3 - 1)
                    place = tap * 256 + i * CH
                    cotangent_stack[parity, place : place + CH, half] = shifted(value, offset).astype(jnp.bfloat16)
    for parity in range(2):
        cotangent[parity, BAND:256, :] = jnp.zeros((256 - BAND, LANES), jnp.bfloat16)
    lane = iota((CH, 128), 1)
    for tap in range(9):
        group = slice(tap * 256, tap * 256 + BAND)
        products = nt(hidden_stack[0, group, :], cotangent[0]) + nt(hidden_stack[1, group, :], cotangent[1])
        total = jnp.zeros((CH, 256), jnp.float32)
        for i in range(6):
            band = products[i * CH : i * CH + CH, :]
            amount = (-CH * (i - 1)) % 256
            total = total + (pltpu.roll(band, amount, 1) if amount else band)
        total = total[:, 0:128]
        at = tap * CH
        if at < 216:
            count = min(CH, 216 - at)
            packed[at : at + count, :] = jnp.where(lane < 96, total, 0.0)[0:count]
        if at + CH > 216:
            skip = max(0, 216 - at)
            for j in range(3):
                moved = pltpu.roll(total, 96 - CH * j, 1)
                moved = jnp.where(lane >= 96, moved, 0.0)[skip:CH]
                to = 72 * j + at + skip - 216
                packed[to : to + CH - skip, :] = packed[to : to + CH - skip, :] + moved
    for parity in range(2):
        rows = slice(parity * BAND, parity * BAND + BAND)
        for crop in range(2):
            half = slice(crop * PLANE, (crop + 1) * PLANE)
            back = nn(backward[...], cotangent_stack[parity, :, half])
            for i in range(6):
                m = parity * 6 + i
                at = slice(m * CH, m * CH + CH)
                whole = back[i * CH : i * CH + CH, :] + head * logits[m : m + 1, half]
                alive = hidden[at, half].astype(jnp.float32) > 0.0
                second[at, half] = jnp.where(alive, whole, 0.0)
    products = nt(patches[...], second[...].astype(jnp.bfloat16))
    row, column = iota((144, 12 * CH), 0), iota((144, 12 * CH), 1)
    place = column // CH
    step = row % 16 - (2 * (place % 6) + place // 6) + 1
    lane = iota((9, 128), 1)
    small = jnp.zeros((9, 128), jnp.float32)
    for dx in range(3):
        part = jnp.where(step == dx, products, 0.0)
        part = jnp.sum(part.reshape(9, 16, 12 * CH), axis=1)
        part = part[:, 0:128] + part[:, 128:256] + part[:, 256:384]
        part = part + pltpu.roll(part, 64, 1)
        part = part + pltpu.roll(part, 32, 1)
        small = jnp.where(lane // CH == dx, part, small)
    packed[216:225, :] = small
    pick = iota((CH, 128), 0) + 96 == iota((CH, 128), 1)
    packed[216:217, :] = packed[216:217, :] + jnp.sum(jnp.where(pick, grad_gain, 0.0), axis=0, keepdims=True)
    packed[217:218, :] = packed[217:218, :] + jnp.sum(jnp.where(pick, grad_head, 0.0), axis=0, keepdims=True)
    packed[225:256, :] = jnp.zeros((31, 128), jnp.float32)


def gradient_kernel(
    x, t, conv_first, conv_second, gain, head, packed,
    toeplitz_first, forward, backward, patches, hidden, hidden_stack, second, logits, cotangent, cotangent_stack,
):
    expand_first(conv_first, toeplitz_first)
    expand_second(conv_second, forward, backward)
    clear_ends(hidden_stack)
    clear_ends(cotangent_stack)
    crop_gradients(
        x, t, gain, head, packed,
        toeplitz_first, forward, backward, patches, hidden, hidden_stack, second, logits, cotangent, cotangent_stack,
    )


COMPUTE_SCRATCH = [
    pltpu.VMEM((12 * CH, 144), jnp.bfloat16),
    pltpu.VMEM((BAND, 9 * 256), jnp.bfloat16),
    pltpu.VMEM((BAND, 9 * 256), jnp.bfloat16),
    pltpu.VMEM((144, LANES), jnp.bfloat16),
    pltpu.VMEM((12 * CH, LANES), jnp.bfloat16),
    pltpu.VMEM((2, 9 * 256, LANES), jnp.bfloat16),
    pltpu.VMEM((12 * CH, LANES), jnp.float32),
    pltpu.VMEM((16, LANES), jnp.float32),
    pltpu.VMEM((2, 256, LANES), jnp.bfloat16),
    pltpu.VMEM((2, 9 * 256, LANES), jnp.bfloat16),
]


def gradients(x, t, conv_first, conv_second, norm_gain, head_weight):
    head = head_weight.astype(jnp.bfloat16).astype(jnp.float32)
    return pl.pallas_call(
        gradient_kernel,
        out_shape=jax.ShapeDtypeStruct((256, 128), jnp.float32),
        in_specs=[pl.BlockSpec(memory_space=pltpu.VMEM)] * 6,
        out_specs=pl.BlockSpec(memory_space=pltpu.VMEM),
        scratch_shapes=COMPUTE_SCRATCH,
        compiler_params=pltpu.CompilerParams(vmem_limit_bytes=40 * 1024 * 1024),
    )(x, t, conv_first, conv_second, norm_gain.reshape(CH, 1), head.reshape(CH, 1))


def unpack(total):
    second = []
    for dx in range(3):
        j = 2 - dx
        second.append(total[0:216, CH * j : CH * j + CH])
        second.append(total[72 * j : 72 * j + 72, 96:128])
    second = jnp.concatenate(second, axis=0).reshape(27, CH, CH)
    first = jnp.concatenate([total[216:225, CH * dx : CH * dx + CH] for dx in range(3)], axis=0)
    return first, second, total[216, 96:128], total[217, 96:128]


MESH = pl.DeviceIdType.MESH
ROWS = 16


def plane_peer(k):
    dp = lax.axis_index("dp")
    x = lax.rem(dp // 32 + k // 4, 4)
    y = lax.rem(lax.rem(dp, 4) + k % 4, 4)
    z = lax.rem(dp // 4, 8)
    return (x * 32 + z * 4 + y, lax.axis_index("pair")), x * 4 + y


def column_peer(k):
    dp = lax.axis_index("dp")
    z = lax.rem(lax.rem(dp // 4, 8) + k // 2, 8)
    core = lax.rem(lax.axis_index("pair") + k % 2, 2)
    return ((dp // 32) * 32 + z * 4 + lax.rem(dp, 4), core), z * 2 + core


def sum_kernel(part, out, first, second, send, recv):
    barrier = pltpu.get_barrier_semaphore()
    for k in range(1, 16):
        pl.semaphore_signal(barrier, inc=1, device_id=plane_peer(k)[0], device_id_type=MESH)
        pl.semaphore_signal(barrier, inc=1, device_id=column_peer(k)[0], device_id_type=MESH)
    pl.semaphore_wait(barrier, 30)
    _, plane_me = plane_peer(0)
    _, column_me = column_peer(0)

    def rows(place):
        return pl.ds(pl.multiple_of(place * ROWS, ROWS), ROWS)

    def exchange(stage, peer, source, target):
        copies = []
        for k in range(1, 16):
            device, place = peer(k)
            copy = pltpu.make_async_remote_copy(
                src_ref=source(place), dst_ref=target,
                send_sem=send.at[stage, k], recv_sem=recv.at[stage, k],
                device_id=device, device_id_type=MESH,
            )
            copy.start()
            copies.append(copy)
        return copies

    copies = exchange(0, plane_peer, lambda place: part.at[rows(place)], first.at[plane_me])
    first[plane_me] = part[rows(plane_me)]
    for copy in copies:
        copy.wait()
    total = first[0]
    for k in range(1, 16):
        total = total + first[k]
    second[column_me] = total
    copies = exchange(1, column_peer, lambda place: second.at[column_me], second.at[column_me])
    for copy in copies:
        copy.wait()
    total = second[0]
    for k in range(1, 16):
        total = total + second[k]
    out[rows(plane_me)] = total
    copies = exchange(2, plane_peer, lambda place: out.at[rows(plane_me)], out.at[rows(plane_me)])
    for copy in copies:
        copy.wait()


def sum_everywhere(packed):
    return pl.pallas_call(
        sum_kernel,
        out_shape=jax.ShapeDtypeStruct((16 * ROWS, 128), jnp.float32),
        in_specs=[pl.BlockSpec(memory_space=pltpu.VMEM)],
        out_specs=pl.BlockSpec(memory_space=pltpu.VMEM),
        scratch_shapes=[
            pltpu.VMEM((16, ROWS, 128), jnp.float32),
            pltpu.VMEM((16, ROWS, 128), jnp.float32),
            pltpu.SemaphoreType.DMA((3, 16)),
            pltpu.SemaphoreType.DMA((3, 16)),
        ],
        compiler_params=pltpu.CompilerParams(collective_id=0, has_side_effects=True),
    )(packed)


beta_first = 0.9
beta_second = 0.999


def adam_update(gradient, momentum, variance):
    next_momentum = beta_first * momentum + (1.0 - beta_first) * gradient
    next_variance = beta_second * variance + (1.0 - beta_second) * gradient * gradient
    return next_momentum / (jnp.sqrt(next_variance) + 1e-08), next_momentum


def adam_kernel(inverse_batch, total, *refs):
    moments, variances, updates, nexts = refs[0:4], refs[4:8], refs[8:12], refs[12:16]
    gradient = total[...] * inverse_batch
    for dx in range(3):
        j = 2 - dx
        part = jnp.concatenate(
            [gradient[0:216, CH * j : CH * j + CH], gradient[72 * j : 72 * j + 72, 96:128]], axis=0
        ).reshape(9, CH, CH)
        taps = slice(9 * dx, 9 * dx + 9)
        updates[1][taps], nexts[1][taps] = adam_update(part, moments[1][taps], variances[1][taps])
        part = gradient[216:225, CH * dx : CH * dx + CH]
        updates[0][taps], nexts[0][taps] = adam_update(part, moments[0][taps], variances[0][taps])
    for place in (2, 3):
        part = gradient[214 + place : 215 + place, 96:128]
        updates[place][...], nexts[place][...] = adam_update(part, moments[place][...], variances[place][...])


def adam(total, batch_size, moments, variances):
    rows = [value.reshape(1, CH) if value.ndim == 1 else value for value in (*moments, *variances)]
    shapes = [jax.ShapeDtypeStruct(value.shape, jnp.float32) for value in rows[0:4]]
    results = pl.pallas_call(
        functools.partial(adam_kernel, 1.0 / batch_size),
        out_shape=shapes + shapes,
        in_specs=[pl.BlockSpec(memory_space=pltpu.VMEM)] * 9,
        out_specs=[pl.BlockSpec(memory_space=pltpu.VMEM)] * 8,
    )(total, *rows)
    return tuple(value.reshape(CH) if value.shape == (1, CH) else value for value in results)


SHARE = 2


def crop_order(counts, position):
    starts = jnp.cumsum(counts, dtype=jnp.int32) - counts
    rows = jnp.sum((starts[None, :] <= position[:, None]).astype(jnp.int32), axis=1, dtype=jnp.int32) - 1
    return rows, position - starts[rows]


def shards(
    pool, crop_ids, crop_corners, counts, conv_first, conv_second, norm_gain, head_weight,
    momentum_first, momentum_second, momentum_gain, momentum_head,
    variance_first, variance_second, variance_gain, variance_head,
):
    dp_count = lax.axis_size("dp")
    pair_index = lax.axis_index("pair")
    batch_size = counts.shape[0] * SHARE
    position = pair_index * dp_count * SHARE + jnp.arange(dp_count * SHARE, dtype=jnp.int32)
    rows, slots = crop_order(counts, position)
    wanted = crop_ids[rows, slots].reshape(dp_count, SHARE)
    arrived = lax.all_to_all(pool[wanted], "dp", split_axis=0, concat_axis=3, tiled=True)[0]
    volumes = arrived.reshape(SHARE, 2, BLOCK, BLOCK, BLOCK)
    mine = lax.dynamic_slice_in_dim(rows, lax.axis_index("dp") * SHARE, SHARE)
    mine_slots = lax.dynamic_slice_in_dim(slots, lax.axis_index("dp") * SHARE, SHARE)
    corners = crop_corners[mine, mine_slots]
    windows = [
        lax.dynamic_slice(volumes[s], (0, corners[s, 0], corners[s, 1], corners[s, 2]), (2, CROP, CROP, CROP))
        for s in range(SHARE)
    ]
    windows = jnp.pad(jnp.stack(windows), ((0, 0), (0, 0), (0, 4), (0, 4), (0, 4)))
    windows = windows.transpose(1, 2, 0, 3, 4).reshape(2, SIDE, LANES)
    targets = jnp.concatenate([windows[1, 0:12:2], windows[1, 1:12:2]]).astype(jnp.float32)
    packed = gradients(windows[0], targets, conv_first, conv_second, norm_gain, head_weight)
    total = sum_everywhere(packed)
    return adam(
        total, batch_size,
        (momentum_first, momentum_second, momentum_gain, momentum_head),
        (variance_first, variance_second, variance_gain, variance_head),
    )


def solution(mesh):
    in_specs = (P(None, None, "dp"),) + (P(),) * 15
    return jax.shard_map(shards, mesh=mesh, in_specs=in_specs, out_specs=(P(),) * 8, check_vma=False)
```

```python
import functools

import jax
import jax.numpy as jnp
from jax import lax
from jax.experimental import pallas as pl
from jax.experimental.pallas import tpu as pltpu
from jax.sharding import PartitionSpec as P

CH = 32
CROP = 12
BLOCK = 32
MOST = 3


SIDE = 16
PLANE = SIDE * SIDE
LANES = 2 * PLANE
VOXELS = CROP * CROP * CROP
BAND = 6 * CH


def iota(shape, axis):
    return lax.broadcasted_iota(jnp.int32, shape, axis)


def nt(a, b):
    return lax.dot_general(a, b, (((1,), (1,)), ((), ())), preferred_element_type=jnp.float32)


def nn(a, b):
    return jnp.dot(a, b, preferred_element_type=jnp.float32)


def onehot(condition):
    return jnp.where(condition, 1.0, 0.0).astype(jnp.bfloat16)


def plane_of(m):
    return 2 * (m % 6) + m // 6


def valid_lanes(rows):
    lane = iota((rows, PLANE), 1)
    return (lane % SIDE < CROP) & ((lane // SIDE) % SIDE < CROP)


def shifted(value, offset):
    amount = (-offset) % PLANE
    return pltpu.roll(value, amount, 1) if amount else value


def halves(ref, rows, crop):
    return ref[rows, crop * PLANE : (crop + 1) * PLANE]


def expand_first(conv_first, toeplitz_first):
    weights = conv_first[...].astype(jnp.bfloat16)
    repeat = onehot(iota((12 * CH, CH), 0) % CH == iota((12 * CH, CH), 1))
    row, column = iota((12 * CH, 144), 0), iota((12 * CH, 144), 1)
    place = row // CH
    step = column % 16 - (2 * (place % 6) + place // 6) + 1
    total = jnp.zeros((12 * CH, 144), jnp.float32)
    for dx in range(3):
        tap = onehot(iota((144, 27), 0) // 16 + 9 * dx == iota((144, 27), 1))
        spread = nn(tap, weights).astype(jnp.bfloat16)
        total = jnp.where(step == dx, nt(repeat, spread), total)
    toeplitz_first[...] = total.astype(jnp.bfloat16)


def expand_second(conv_second, forward, backward):
    eye = onehot(iota((CH, CH), 0) == iota((CH, CH), 1))
    for tap in range(9):
        blocks = [conv_second[9 * dx + tap] for dx in range(3)]
        zero = jnp.zeros((CH, 256 - 3 * CH), jnp.float32)
        group = slice(tap * 256, tap * 256 + 256)
        strip = jnp.concatenate([blocks[2], blocks[1], blocks[0], zero], axis=1)
        stacked = jnp.concatenate(blocks, axis=0).astype(jnp.bfloat16)
        turned = jnp.concatenate([nt(eye, stacked), zero], axis=1)
        for i in range(6):
            rows = slice(i * CH, i * CH + CH)
            amount = (CH * (i - 1)) % 256
            moved = pltpu.roll(strip, amount, 1) if amount else strip
            backward[rows, group] = moved.astype(jnp.bfloat16)
            moved = pltpu.roll(turned, amount, 1) if amount else turned
            forward[rows, group] = moved.astype(jnp.bfloat16)


def clear_ends(stack):
    for parity in range(2):
        for tap in range(9):
            stack[parity, tap * 256 + BAND : tap * 256 + 256, :] = jnp.zeros((256 - BAND, LANES), jnp.bfloat16)


def crop_gradients(
    x, t, gain, head, packed,
    toeplitz_first, forward, backward, patches, hidden, hidden_stack, second, logits, cotangent, cotangent_stack,
):
    valid = valid_lanes(1)
    for crop in range(2):
        half = slice(crop * PLANE, (crop + 1) * PLANE)
        source = x[crop]
        for tap in range(9):
            offset = SIDE * (tap // 3 - 1) + tap % 3 - 1
            patches[tap * 16 : tap * 16 + 16, half] = shifted(source, offset).astype(jnp.bfloat16)
    for crop in range(2):
        half = slice(crop * PLANE, (crop + 1) * PLANE)
        for parity in range(2):
            rows = slice(parity * BAND, parity * BAND + BAND)
            first_map = nn(toeplitz_first[rows, :], patches[:, half])
            value = jnp.where(valid, jnp.maximum(first_map, 0.0), 0.0)
            hidden[rows, half] = value.astype(jnp.bfloat16)
            for tap in range(9):
                offset = 2 * (SIDE * (tap // 3 - 1) + tap % 3 - 1)
                hidden_stack[parity, tap * 256 : tap * 256 + BAND, half] = shifted(value, offset).astype(jnp.bfloat16)
    for parity in range(2):
        second[parity * BAND : parity * BAND + BAND, :] = nn(forward[...], hidden_stack[parity])
    scale = 1.0 / VOXELS
    columns = []
    for crop in range(2):
        half = slice(crop * PLANE, (crop + 1) * PLANE)
        total = jnp.zeros((CH, PLANE), jnp.float32)
        for m in range(12):
            total = total + second[m * CH : m * CH + CH, half]
        center = jnp.sum(jnp.where(valid, total, 0.0), axis=1, keepdims=True) * scale
        total = jnp.zeros((CH, PLANE), jnp.float32)
        for m in range(12):
            away = second[m * CH : m * CH + CH, half] - center
            total = total + away * away
        spread = jnp.sum(jnp.where(valid, total, 0.0), axis=1, keepdims=True) * scale
        inverse = lax.rsqrt(spread + 1e-05)
        columns.append(inverse)
        for m in range(12):
            rows = slice(m * CH, m * CH + CH)
            hat = (second[rows, half] - center) * inverse
            second[rows, half] = hat
            joined = (jnp.maximum(hat * gain, 0.0) + hidden[rows, half].astype(jnp.float32)).astype(jnp.bfloat16)
            logits[plane_of(m) : plane_of(m) + 1, half] = jnp.sum(joined.astype(jnp.float32) * head, axis=0, keepdims=True)
    slope = 1.0 / (1.0 + jnp.exp(-logits[0:12, :])) - t
    both = jnp.concatenate([valid, valid], axis=1)
    logits[0:12, :] = jnp.where(both, slope * scale, 0.0)
    grad_gain = jnp.zeros((CH, 1), jnp.float32)
    grad_head = jnp.zeros((CH, 1), jnp.float32)
    for crop in range(2):
        half = slice(crop * PLANE, (crop + 1) * PLANE)
        sum_plain = jnp.zeros((CH, PLANE), jnp.float32)
        sum_hat = jnp.zeros((CH, PLANE), jnp.float32)
        sum_head = jnp.zeros((CH, PLANE), jnp.float32)
        for m in range(12):
            rows = slice(m * CH, m * CH + CH)
            hat = second[rows, half]
            normed = hat * gain
            slope = logits[plane_of(m) : plane_of(m) + 1, half]
            joined = (jnp.maximum(normed, 0.0) + hidden[rows, half].astype(jnp.float32)).astype(jnp.bfloat16)
            sum_head = sum_head + joined.astype(jnp.float32) * slope
            passed = jnp.where(normed > 0.0, slope, 0.0)
            sum_plain = sum_plain + passed
            sum_hat = sum_hat + passed * hat
        grad_head = grad_head + jnp.sum(sum_head, axis=1, keepdims=True)
        mean_plain = head * jnp.sum(sum_plain, axis=1, keepdims=True)
        mean_hat = head * jnp.sum(sum_hat, axis=1, keepdims=True)
        grad_gain = grad_gain + mean_hat
        mean_plain = mean_plain * scale
        mean_hat = mean_hat * scale
        factor = columns[crop] * gain
        for parity in range(2):
            for i in range(6):
                m = parity * 6 + i
                rows = slice(m * CH, m * CH + CH)
                hat = second[rows, half]
                slope = logits[plane_of(m) : plane_of(m) + 1, half]
                passed = jnp.where(hat * gain > 0.0, head * slope, 0.0)
                value = jnp.where(valid, factor * (passed - mean_plain - hat * mean_hat), 0.0)
                cotangent[parity, i * CH : i * CH + CH, half] = value.astype(jnp.bfloat16)
                for tap in range(9):
                    offset = -2 * (SIDE * (tap // 3 - 1) + tap % 3 - 1)
                    place = tap * 256 + i * CH
                    cotangent_stack[parity, place : place + CH, half] = shifted(value, offset).astype(jnp.bfloat16)
    for parity in range(2):
        cotangent[parity, BAND:256, :] = jnp.zeros((256 - BAND, LANES), jnp.bfloat16)
    lane = iota((CH, 128), 1)
    for tap in range(9):
        group = slice(tap * 256, tap * 256 + BAND)
        products = nt(hidden_stack[0, group, :], cotangent[0]) + nt(hidden_stack[1, group, :], cotangent[1])
        total = jnp.zeros((CH, 256), jnp.float32)
        for i in range(6):
            band = products[i * CH : i * CH + CH, :]
            amount = (-CH * (i - 1)) % 256
            total = total + (pltpu.roll(band, amount, 1) if amount else band)
        total = total[:, 0:128]
        at = tap * CH
        if at < 216:
            count = min(CH, 216 - at)
            packed[at : at + count, :] = jnp.where(lane < 96, total, 0.0)[0:count]
        if at + CH > 216:
            skip = max(0, 216 - at)
            for j in range(3):
                moved = pltpu.roll(total, 96 - CH * j, 1)
                moved = jnp.where(lane >= 96, moved, 0.0)[skip:CH]
                to = 72 * j + at + skip - 216
                packed[to : to + CH - skip, :] = packed[to : to + CH - skip, :] + moved
    for parity in range(2):
        rows = slice(parity * BAND, parity * BAND + BAND)
        for crop in range(2):
            half = slice(crop * PLANE, (crop + 1) * PLANE)
            back = nn(backward[...], cotangent_stack[parity, :, half])
            for i in range(6):
                m = parity * 6 + i
                at = slice(m * CH, m * CH + CH)
                whole = back[i * CH : i * CH + CH, :] + head * logits[plane_of(m) : plane_of(m) + 1, half]
                alive = hidden[at, half].astype(jnp.float32) > 0.0
                second[at, half] = jnp.where(alive, whole, 0.0)
    products = nt(patches[...], second[...].astype(jnp.bfloat16))
    row, column = iota((144, 12 * CH), 0), iota((144, 12 * CH), 1)
    place = column // CH
    step = row % 16 - (2 * (place % 6) + place // 6) + 1
    lane = iota((9, 128), 1)
    small = jnp.zeros((9, 128), jnp.float32)
    for dx in range(3):
        part = jnp.where(step == dx, products, 0.0)
        part = jnp.sum(part.reshape(9, 16, 12 * CH), axis=1)
        part = part[:, 0:128] + part[:, 128:256] + part[:, 256:384]
        part = part + pltpu.roll(part, 64, 1)
        part = part + pltpu.roll(part, 32, 1)
        small = jnp.where(lane // CH == dx, part, small)
    packed[216:225, :] = small
    pick = iota((CH, 128), 0) + 96 == iota((CH, 128), 1)
    packed[216:217, :] = packed[216:217, :] + jnp.sum(jnp.where(pick, grad_gain, 0.0), axis=0, keepdims=True)
    packed[217:218, :] = packed[217:218, :] + jnp.sum(jnp.where(pick, grad_head, 0.0), axis=0, keepdims=True)
    packed[225:256, :] = jnp.zeros((31, 128), jnp.float32)


COMPUTE_SCRATCH = [
    pltpu.VMEM((12 * CH, 144), jnp.bfloat16),
    pltpu.VMEM((BAND, 9 * 256), jnp.bfloat16),
    pltpu.VMEM((BAND, 9 * 256), jnp.bfloat16),
    pltpu.VMEM((144, LANES), jnp.bfloat16),
    pltpu.VMEM((12 * CH, LANES), jnp.bfloat16),
    pltpu.VMEM((2, 9 * 256, LANES), jnp.bfloat16),
    pltpu.VMEM((12 * CH, LANES), jnp.float32),
    pltpu.VMEM((16, LANES), jnp.float32),
    pltpu.VMEM((2, 256, LANES), jnp.bfloat16),
    pltpu.VMEM((2, 9 * 256, LANES), jnp.bfloat16),
]


MESH = pl.DeviceIdType.MESH


def plane_peer(k):
    dp = lax.axis_index("dp")
    x = lax.rem(dp // 32 + k // 4, 4)
    y = lax.rem(lax.rem(dp, 4) + k % 4, 4)
    z = lax.rem(dp // 4, 8)
    return (x * 32 + z * 4 + y, lax.axis_index("pair")), x * 4 + y


def z_peer(k):
    dp = lax.axis_index("dp")
    z = lax.rem(lax.rem(dp // 4, 8) + k, 8)
    return ((dp // 32) * 32 + z * 4 + lax.rem(dp, 4), lax.axis_index("pair")), z


def core_peer(k):
    core = lax.rem(lax.axis_index("pair") + k, 2)
    return (lax.axis_index("dp"), core), core


PLANE_STEPS = (10, 6, 9, 11, 14, 2, 5, 7, 8, 13, 15, 1, 3, 4, 12)
Z_STEPS = (4, 3, 5, 2, 6, 1, 7)
GROUPS = ((plane_peer, PLANE_STEPS), (z_peer, Z_STEPS), (core_peer, (1,)))
CHIPS, COLUMN, CORES = GROUPS


def rows_at(place, count):
    return pl.ds(pl.multiple_of(place * count, count), count)


def greet():
    barrier = pltpu.get_barrier_semaphore()
    for peer, steps in GROUPS:
        for k in steps:
            pl.semaphore_signal(barrier, inc=1, device_id=peer(k)[0], device_id_type=MESH)
    return lambda: pl.semaphore_wait(barrier, sum(len(steps) for _, steps in GROUPS))


def exchange(stage, group, source, target, send, recv):
    peer, steps = group
    copies = []
    for k in steps:
        device, place = peer(k)
        copy = pltpu.make_async_remote_copy(
            src_ref=source(place), dst_ref=target, send_sem=send.at[stage, k], recv_sem=recv.at[stage, k],
            device_id=device, device_id_type=MESH,
        )
        copy.start()
        copies.append(copy)
    return copies


def finish(copies):
    for copy in copies:
        copy.wait()


def reduce_everywhere(packed, out, halves_in, first, second, send, recv):
    _, core = core_peer(0)
    _, place = plane_peer(0)
    _, z = z_peer(0)
    copies = exchange(2, CORES, lambda other: packed.at[rows_at(other, 128)], halves_in, send, recv)
    finish(copies)
    mine = rows_at(core, 128)
    packed[mine] = packed[mine] + halves_in[...]
    part = lambda other: pl.ds(pl.multiple_of(core * 128 + other * 8, 8), 8)
    copies = exchange(3, CHIPS, lambda other: packed.at[part(other)], first.at[place], send, recv)
    first[place] = packed[part(place)]
    finish(copies)
    total = first[0]
    for k in range(1, 16):
        total = total + first[k]
    second[z] = total
    copies = exchange(4, COLUMN, lambda other: second.at[z], second.at[z], send, recv)
    finish(copies)
    total = second[0]
    for k in range(1, 8):
        total = total + second[k]
    out[part(place)] = total
    copies = exchange(5, CHIPS, lambda other: out.at[part(place)], out.at[part(place)], send, recv)
    finish(copies)
    copies = exchange(6, CORES, lambda other: out.at[mine], out.at[mine], send, recv)
    finish(copies)


def crop_table(counts, ids, corners):
    shape = (256, 256)
    count = counts[...].astype(jnp.float32)
    before = onehot(iota(shape, 0) < iota(shape, 1))
    starts = nn(count.astype(jnp.bfloat16), before)
    number = (iota(shape, 0) + 256 * lax.axis_index("pair")).astype(jnp.float32)
    total = jnp.zeros((256, 4), jnp.float32)
    for s in range(MOST):
        chosen = onehot((number == starts + s) & (count > s))
        table = jnp.concatenate([ids[s : s + 1, :], corners[s]], axis=0)
        total = total + nt(chosen, table.astype(jnp.bfloat16))
    return total


def as_number(condition_shape, axis):
    return iota(condition_shape, axis).astype(jnp.float32)


def column(ref):
    eye = iota((CH, CH), 0) == iota((CH, CH), 1)
    return jnp.sum(jnp.where(eye, ref[...], 0.0), axis=1, keepdims=True)


def step_kernel(
    pool, counts, ids, corners, conv_first, conv_second, gain_ref, head_ref,
    out,
    gathered, arrived, leaving, landed, spots, packed, halves_in, first, second_sums, send, recv,
    toeplitz_first, forward, backward, patches, hidden, hidden_stack, second, logits, cotangent, cotangent_stack,
):
    wait_for_all = greet()
    _, place = plane_peer(0)
    _, z = z_peer(0)
    table = crop_table(counts, ids, corners)
    gathered[...] = nn(onehot(table[:, 0:1] == as_number((256, 256), 1)), pool[...]).astype(jnp.bfloat16)
    wait_for_all()
    copies = exchange(0, CHIPS, lambda other: gathered.at[rows_at(other, 16)], arrived.at[rows_at(place, 16)], send, recv)
    arrived[rows_at(place, 16)] = gathered[rows_at(place, 16)]
    expand_first(conv_first, toeplitz_first)
    expand_second(conv_second, forward, backward)
    table = table.astype(jnp.bfloat16)
    row = iota((128, 1), 0)
    crop = row // 16 * 2 + row % 16 // 8
    about = nn(onehot(iota((128, 256), 1) == place * 16 + crop), table)
    x = jnp.floor((about[:, 1:2] - z.astype(jnp.float32) + 7.0) * 0.125) + (row % 8 // 4).astype(jnp.float32)
    wanted = (x * 4.0 + (row % 4).astype(jnp.float32)) * 16.0 + crop.astype(jnp.float32)
    chosen = onehot(wanted == as_number((128, 256), 1))
    finish(copies)
    leaving[...] = nn(chosen, arrived[...]).astype(jnp.bfloat16)
    copies = exchange(1, COLUMN, lambda other: leaving.at[rows_at(other, 16)], landed.at[rows_at(z, 16)], send, recv)
    landed[rows_at(z, 16)] = leaving[rows_at(z, 16)]
    clear_ends(hidden_stack)
    clear_ends(cotangent_stack)
    gain = column(gain_ref)
    head = column(head_ref).astype(jnp.bfloat16).astype(jnp.float32)
    row = iota((128, 1), 0)
    s, p = row % 32 // 16, row % 16
    about = nn(onehot(iota((128, 256), 1) == place * 16 + z * 2 + s), table)
    x = about[:, 1:2] + p.astype(jnp.float32)
    wanted = (x - 8.0 * jnp.floor(x * 0.125)) * 16.0 + (s * 8 + p // 8 * 4 + row // 32).astype(jnp.float32)
    chosen = onehot((wanted == as_number((128, 128), 1)) & (p < CROP))
    lane = iota((1, 256), 1)
    inside = (lane % SIDE < CROP) & (lane // SIDE < CROP)
    for s in range(2):
        y = about[16 * s : 16 * s + 1, 2:3] + (lane // SIDE).astype(jnp.float32)
        spot = y * BLOCK + about[16 * s : 16 * s + 1, 3:4] + (lane % SIDE).astype(jnp.float32)
        spots[s] = onehot(jnp.where(inside, spot, -1.0) == as_number((1024, 256), 0))
    finish(copies)
    planes = nn(chosen, landed[...]).astype(jnp.bfloat16)
    images, targets = [], []
    for s in range(2):
        whole = jnp.concatenate(
            [
                jnp.concatenate([planes[32 * q + 16 * s : 32 * q + 16 * s + 16, 256 * c : 256 * c + 256] for q in range(4)], axis=1)
                for c in range(2)
            ],
            axis=0,
        )
        window = nn(whole, spots[s])
        images.append(window[0:16])
        targets.append(window[16:28])
    crop_gradients(
        images, jnp.concatenate(targets, axis=1), gain, head, packed,
        toeplitz_first, forward, backward, patches, hidden, hidden_stack, second, logits, cotangent, cotangent_stack,
    )
    reduce_everywhere(packed, out, halves_in, first, second_sums, send, recv)


SCRATCH = [
    pltpu.VMEM((256, 512), jnp.bfloat16),
    pltpu.VMEM((256, 512), jnp.bfloat16),
    pltpu.VMEM((128, 512), jnp.bfloat16),
    pltpu.VMEM((128, 512), jnp.bfloat16),
    pltpu.VMEM((2, 1024, 256), jnp.bfloat16),
    pltpu.VMEM((256, 128), jnp.float32),
    pltpu.VMEM((128, 128), jnp.float32),
    pltpu.VMEM((16, 8, 128), jnp.float32),
    pltpu.VMEM((8, 8, 128), jnp.float32),
    pltpu.SemaphoreType.DMA((7, 16)),
    pltpu.SemaphoreType.DMA((7, 16)),
]


def summed_gradients(pool, crop_ids, crop_corners, counts, conv_first, conv_second, norm_gain, head_weight):
    return pl.pallas_call(
        step_kernel,
        out_shape=jax.ShapeDtypeStruct((256, 128), jnp.float32),
        in_specs=[pl.BlockSpec(memory_space=pltpu.VMEM)] * 8,
        out_specs=pl.BlockSpec(memory_space=pltpu.VMEM),
        scratch_shapes=SCRATCH + COMPUTE_SCRATCH,
        compiler_params=pltpu.CompilerParams(
            collective_id=0, has_side_effects=True, vmem_limit_bytes=48 * 1024 * 1024
        ),
    )(
        pool.reshape(256, 512), counts.reshape(1, 256), crop_ids.T, crop_corners.transpose(1, 2, 0),
        conv_first, conv_second, norm_gain.reshape(1, CH), head_weight.reshape(1, CH),
    )


beta_first = 0.9
beta_second = 0.999


def adam_update(gradient, momentum, variance):
    next_momentum = beta_first * momentum + (1.0 - beta_first) * gradient
    next_variance = beta_second * variance + (1.0 - beta_second) * gradient * gradient
    return next_momentum / (jnp.sqrt(next_variance) + 1e-08), next_momentum


def adam_kernel(inverse_batch, total, *refs):
    moments, variances, updates, nexts = refs[0:4], refs[4:8], refs[8:12], refs[12:16]
    gradient = total[...] * inverse_batch
    for dx in range(3):
        j = 2 - dx
        part = jnp.concatenate(
            [gradient[0:216, CH * j : CH * j + CH], gradient[72 * j : 72 * j + 72, 96:128]], axis=0
        ).reshape(9, CH, CH)
        taps = slice(9 * dx, 9 * dx + 9)
        updates[1][taps], nexts[1][taps] = adam_update(part, moments[1][taps], variances[1][taps])
        part = gradient[216:225, CH * dx : CH * dx + CH]
        updates[0][taps], nexts[0][taps] = adam_update(part, moments[0][taps], variances[0][taps])
    for place in (2, 3):
        part = gradient[214 + place : 215 + place, 96:128]
        updates[place][...], nexts[place][...] = adam_update(part, moments[place][...], variances[place][...])


def adam(total, batch_size, moments, variances):
    rows = [value.reshape(1, CH) if value.ndim == 1 else value for value in (*moments, *variances)]
    shapes = [jax.ShapeDtypeStruct(value.shape, jnp.float32) for value in rows[0:4]]
    results = pl.pallas_call(
        functools.partial(adam_kernel, 1.0 / batch_size),
        out_shape=shapes + shapes,
        in_specs=[pl.BlockSpec(memory_space=pltpu.VMEM)] * 9,
        out_specs=[pl.BlockSpec(memory_space=pltpu.VMEM)] * 8,
    )(total, *rows)
    return tuple(value.reshape(CH) if value.shape == (1, CH) else value for value in results)


SHARE = 2


def shards(
    pool, crop_ids, crop_corners, counts, conv_first, conv_second, norm_gain, head_weight,
    momentum_first, momentum_second, momentum_gain, momentum_head,
    variance_first, variance_second, variance_gain, variance_head,
):
    total = summed_gradients(pool, crop_ids, crop_corners, counts, conv_first, conv_second, norm_gain, head_weight)
    return adam(
        total, counts.shape[0] * SHARE,
        (momentum_first, momentum_second, momentum_gain, momentum_head),
        (variance_first, variance_second, variance_gain, variance_head),
    )


def solution(mesh):
    in_specs = (P(None, None, "dp"),) + (P(),) * 15
    return jax.shard_map(shards, mesh=mesh, in_specs=in_specs, out_specs=(P(),) * 8, check_vma=False)
```

```python
import functools

import jax
import jax.numpy as jnp
from jax import lax
from jax.experimental import pallas as pl
from jax.experimental.pallas import tpu as pltpu
from jax.sharding import PartitionSpec as P

CH = 32
CROP = 12
BLOCK = 32
MOST = 3


SIDE = 16
PLANE = SIDE * SIDE
LANES = 2 * PLANE
VOXELS = CROP * CROP * CROP
BAND = 6 * CH


def iota(shape, axis):
    return lax.broadcasted_iota(jnp.int32, shape, axis)


def nt(a, b):
    return lax.dot_general(a, b, (((1,), (1,)), ((), ())), preferred_element_type=jnp.float32)


def nn(a, b):
    return jnp.dot(a, b, preferred_element_type=jnp.float32)


def onehot(condition):
    return jnp.where(condition, 1.0, 0.0).astype(jnp.bfloat16)


def plane_of(m):
    return 2 * (m % 6) + m // 6


def valid_lanes(rows):
    lane = iota((rows, PLANE), 1)
    return (lane % SIDE < CROP) & ((lane // SIDE) % SIDE < CROP)


def shifted(value, offset):
    amount = (-offset) % PLANE
    return pltpu.roll(value, amount, 1) if amount else value


def halves(ref, rows, crop):
    return ref[rows, crop * PLANE : (crop + 1) * PLANE]


def expand_first(conv_first, toeplitz_first):
    weights = conv_first[...].astype(jnp.bfloat16)
    repeat = onehot(iota((12 * CH, CH), 0) % CH == iota((12 * CH, CH), 1))
    row, column = iota((12 * CH, 144), 0), iota((12 * CH, 144), 1)
    place = row // CH
    step = column % 16 - (2 * (place % 6) + place // 6) + 1
    total = jnp.zeros((12 * CH, 144), jnp.float32)
    for dx in range(3):
        tap = onehot(iota((144, 27), 0) // 16 + 9 * dx == iota((144, 27), 1))
        spread = nn(tap, weights).astype(jnp.bfloat16)
        total = jnp.where(step == dx, nt(repeat, spread), total)
    toeplitz_first[...] = total.astype(jnp.bfloat16)


def expand_second(conv_second, forward, backward):
    eye = onehot(iota((CH, CH), 0) == iota((CH, CH), 1))
    for tap in range(9):
        blocks = [conv_second[9 * dx + tap] for dx in range(3)]
        zero = jnp.zeros((CH, 256 - 3 * CH), jnp.float32)
        group = slice(tap * 256, tap * 256 + 256)
        strip = jnp.concatenate([blocks[2], blocks[1], blocks[0], zero], axis=1)
        stacked = jnp.concatenate(blocks, axis=0).astype(jnp.bfloat16)
        turned = jnp.concatenate([nt(eye, stacked), zero], axis=1)
        for i in range(6):
            rows = slice(i * CH, i * CH + CH)
            amount = (CH * (i - 1)) % 256
            moved = pltpu.roll(strip, amount, 1) if amount else strip
            backward[rows, group] = moved.astype(jnp.bfloat16)
            moved = pltpu.roll(turned, amount, 1) if amount else turned
            forward[rows, group] = moved.astype(jnp.bfloat16)


def clear_ends(stack):
    for parity in range(2):
        for tap in range(9):
            stack[parity, tap * 256 + BAND : tap * 256 + 256, :] = jnp.zeros((256 - BAND, LANES), jnp.bfloat16)


def crop_gradients(
    x, t, gain, head, packed,
    toeplitz_first, forward, backward, patches, hidden, hidden_stack, second, logits, cotangent, cotangent_stack,
):
    valid = valid_lanes(1)
    for crop in range(2):
        half = slice(crop * PLANE, (crop + 1) * PLANE)
        source = x[crop]
        for tap in range(9):
            offset = SIDE * (tap // 3 - 1) + tap % 3 - 1
            patches[tap * 16 : tap * 16 + 16, half] = shifted(source, offset).astype(jnp.bfloat16)
    for crop in range(2):
        half = slice(crop * PLANE, (crop + 1) * PLANE)
        for parity in range(2):
            rows = slice(parity * BAND, parity * BAND + BAND)
            first_map = nn(toeplitz_first[rows, :], patches[:, half])
            value = jnp.where(valid, jnp.maximum(first_map, 0.0), 0.0)
            hidden[rows, half] = value.astype(jnp.bfloat16)
            for tap in range(9):
                offset = 2 * (SIDE * (tap // 3 - 1) + tap % 3 - 1)
                hidden_stack[parity, tap * 256 : tap * 256 + BAND, half] = shifted(value, offset).astype(jnp.bfloat16)
    for parity in range(2):
        second[parity * BAND : parity * BAND + BAND, :] = nn(forward[...], hidden_stack[parity])
    scale = 1.0 / VOXELS
    columns = []
    for crop in range(2):
        half = slice(crop * PLANE, (crop + 1) * PLANE)
        total = jnp.zeros((CH, PLANE), jnp.float32)
        for m in range(12):
            total = total + second[m * CH : m * CH + CH, half]
        center = jnp.sum(jnp.where(valid, total, 0.0), axis=1, keepdims=True) * scale
        total = jnp.zeros((CH, PLANE), jnp.float32)
        for m in range(12):
            away = second[m * CH : m * CH + CH, half] - center
            total = total + away * away
        spread = jnp.sum(jnp.where(valid, total, 0.0), axis=1, keepdims=True) * scale
        inverse = lax.rsqrt(spread + 1e-05)
        columns.append(inverse)
        for m in range(12):
            rows = slice(m * CH, m * CH + CH)
            hat = (second[rows, half] - center) * inverse
            second[rows, half] = hat
            joined = (jnp.maximum(hat * gain, 0.0) + hidden[rows, half].astype(jnp.float32)).astype(jnp.bfloat16)
            logits[plane_of(m) : plane_of(m) + 1, half] = jnp.sum(joined.astype(jnp.float32) * head, axis=0, keepdims=True)
    slope = 1.0 / (1.0 + jnp.exp(-logits[0:12, :])) - t
    both = jnp.concatenate([valid, valid], axis=1)
    logits[0:12, :] = jnp.where(both, slope * scale, 0.0)
    grad_gain = jnp.zeros((CH, 1), jnp.float32)
    grad_head = jnp.zeros((CH, 1), jnp.float32)
    for crop in range(2):
        half = slice(crop * PLANE, (crop + 1) * PLANE)
        sum_plain = jnp.zeros((CH, PLANE), jnp.float32)
        sum_hat = jnp.zeros((CH, PLANE), jnp.float32)
        sum_head = jnp.zeros((CH, PLANE), jnp.float32)
        for m in range(12):
            rows = slice(m * CH, m * CH + CH)
            hat = second[rows, half]
            normed = hat * gain
            slope = logits[plane_of(m) : plane_of(m) + 1, half]
            joined = (jnp.maximum(normed, 0.0) + hidden[rows, half].astype(jnp.float32)).astype(jnp.bfloat16)
            sum_head = sum_head + joined.astype(jnp.float32) * slope
            passed = jnp.where(normed > 0.0, slope, 0.0)
            sum_plain = sum_plain + passed
            sum_hat = sum_hat + passed * hat
        grad_head = grad_head + jnp.sum(sum_head, axis=1, keepdims=True)
        mean_plain = head * jnp.sum(sum_plain, axis=1, keepdims=True)
        mean_hat = head * jnp.sum(sum_hat, axis=1, keepdims=True)
        grad_gain = grad_gain + mean_hat
        mean_plain = mean_plain * scale
        mean_hat = mean_hat * scale
        factor = columns[crop] * gain
        for parity in range(2):
            for i in range(6):
                m = parity * 6 + i
                rows = slice(m * CH, m * CH + CH)
                hat = second[rows, half]
                slope = logits[plane_of(m) : plane_of(m) + 1, half]
                passed = jnp.where(hat * gain > 0.0, head * slope, 0.0)
                value = jnp.where(valid, factor * (passed - mean_plain - hat * mean_hat), 0.0)
                cotangent[parity, i * CH : i * CH + CH, half] = value.astype(jnp.bfloat16)
                for tap in range(9):
                    offset = -2 * (SIDE * (tap // 3 - 1) + tap % 3 - 1)
                    place = tap * 256 + i * CH
                    cotangent_stack[parity, place : place + CH, half] = shifted(value, offset).astype(jnp.bfloat16)
    for parity in range(2):
        cotangent[parity, BAND:256, :] = jnp.zeros((256 - BAND, LANES), jnp.bfloat16)
    lane = iota((CH, 128), 1)
    for tap in range(9):
        group = slice(tap * 256, tap * 256 + BAND)
        products = nt(hidden_stack[0, group, :], cotangent[0]) + nt(hidden_stack[1, group, :], cotangent[1])
        total = jnp.zeros((CH, 256), jnp.float32)
        for i in range(6):
            band = products[i * CH : i * CH + CH, :]
            amount = (-CH * (i - 1)) % 256
            total = total + (pltpu.roll(band, amount, 1) if amount else band)
        total = total[:, 0:128]
        at = tap * CH
        if at < 216:
            count = min(CH, 216 - at)
            packed[at : at + count, :] = jnp.where(lane < 96, total, 0.0)[0:count]
        if at + CH > 216:
            skip = max(0, 216 - at)
            for j in range(3):
                moved = pltpu.roll(total, 96 - CH * j, 1)
                moved = jnp.where(lane >= 96, moved, 0.0)[skip:CH]
                to = 72 * j + at + skip - 216
                packed[to : to + CH - skip, :] = packed[to : to + CH - skip, :] + moved
    for parity in range(2):
        rows = slice(parity * BAND, parity * BAND + BAND)
        for crop in range(2):
            half = slice(crop * PLANE, (crop + 1) * PLANE)
            back = nn(backward[...], cotangent_stack[parity, :, half])
            for i in range(6):
                m = parity * 6 + i
                at = slice(m * CH, m * CH + CH)
                whole = back[i * CH : i * CH + CH, :] + head * logits[plane_of(m) : plane_of(m) + 1, half]
                alive = hidden[at, half].astype(jnp.float32) > 0.0
                second[at, half] = jnp.where(alive, whole, 0.0)
    products = nt(patches[...], second[...].astype(jnp.bfloat16))
    row, column = iota((144, 12 * CH), 0), iota((144, 12 * CH), 1)
    place = column // CH
    step = row % 16 - (2 * (place % 6) + place // 6) + 1
    lane = iota((9, 128), 1)
    small = jnp.zeros((9, 128), jnp.float32)
    for dx in range(3):
        part = jnp.where(step == dx, products, 0.0)
        part = jnp.sum(part.reshape(9, 16, 12 * CH), axis=1)
        part = part[:, 0:128] + part[:, 128:256] + part[:, 256:384]
        part = part + pltpu.roll(part, 64, 1)
        part = part + pltpu.roll(part, 32, 1)
        small = jnp.where(lane // CH == dx, part, small)
    packed[216:225, :] = small
    pick = iota((CH, 128), 0) + 96 == iota((CH, 128), 1)
    packed[216:217, :] = packed[216:217, :] + jnp.sum(jnp.where(pick, grad_gain, 0.0), axis=0, keepdims=True)
    packed[217:218, :] = packed[217:218, :] + jnp.sum(jnp.where(pick, grad_head, 0.0), axis=0, keepdims=True)
    packed[225:256, :] = jnp.zeros((31, 128), jnp.float32)


COMPUTE_SCRATCH = [
    pltpu.VMEM((12 * CH, 144), jnp.bfloat16),
    pltpu.VMEM((BAND, 9 * 256), jnp.bfloat16),
    pltpu.VMEM((BAND, 9 * 256), jnp.bfloat16),
    pltpu.VMEM((144, LANES), jnp.bfloat16),
    pltpu.VMEM((12 * CH, LANES), jnp.bfloat16),
    pltpu.VMEM((2, 9 * 256, LANES), jnp.bfloat16),
    pltpu.VMEM((12 * CH, LANES), jnp.float32),
    pltpu.VMEM((16, LANES), jnp.float32),
    pltpu.VMEM((2, 256, LANES), jnp.bfloat16),
    pltpu.VMEM((2, 9 * 256, LANES), jnp.bfloat16),
]


MESH = pl.DeviceIdType.MESH


def plane_peer(k):
    dp = lax.axis_index("dp")
    x = lax.rem(dp // 32 + k // 4, 4)
    y = lax.rem(lax.rem(dp, 4) + k % 4, 4)
    z = lax.rem(dp // 4, 8)
    return (x * 32 + z * 4 + y, lax.axis_index("pair")), x * 4 + y


def z_peer(k):
    dp = lax.axis_index("dp")
    z = lax.rem(lax.rem(dp // 4, 8) + k, 8)
    return ((dp // 32) * 32 + z * 4 + lax.rem(dp, 4), lax.axis_index("pair")), z


def column_peer(k):
    (dp, _), z = z_peer(k // 2)
    core = lax.rem(lax.axis_index("pair") + k % 2, 2)
    return (dp, core), z * 2 + core


PLANE_STEPS = (10, 6, 9, 11, 14, 2, 5, 7, 8, 13, 15, 1, 3, 4, 12)
Z_STEPS = (4, 3, 5, 2, 6, 1, 7)
COLUMN_STEPS = (9, 8, 7, 6, 11, 10, 5, 4, 13, 12, 3, 2, 15, 14, 1)
CHIPS, DEPTH, COLUMN = (plane_peer, PLANE_STEPS), (z_peer, Z_STEPS), (column_peer, COLUMN_STEPS)
GROUPS = (CHIPS, COLUMN)


def rows_at(place, count):
    return pl.ds(pl.multiple_of(place * count, count), count)


def greet():
    barrier = pltpu.get_barrier_semaphore()
    for peer, steps in GROUPS:
        for k in steps:
            pl.semaphore_signal(barrier, inc=1, device_id=peer(k)[0], device_id_type=MESH)
    return lambda: pl.semaphore_wait(barrier, sum(len(steps) for _, steps in GROUPS))


def exchange(stage, group, source, target, send, recv):
    peer, steps = group
    copies = []
    for k in steps:
        device, place = peer(k)
        copy = pltpu.make_async_remote_copy(
            src_ref=source(place), dst_ref=target, send_sem=send.at[stage, k], recv_sem=recv.at[stage, k],
            device_id=device, device_id_type=MESH,
        )
        copy.start()
        copies.append(copy)
    return copies


def finish(copies):
    for copy in copies:
        copy.wait()


def reduce_everywhere(packed, out, first, second, send, recv):
    _, place = plane_peer(0)
    _, column = column_peer(0)
    copies = exchange(2, CHIPS, lambda other: packed.at[rows_at(other, 16)], first.at[place], send, recv)
    first[place] = packed[rows_at(place, 16)]
    finish(copies)
    total = first[0]
    for k in range(1, 16):
        total = total + first[k]
    second[column] = total
    copies = exchange(3, COLUMN, lambda other: second.at[column], second.at[column], send, recv)
    finish(copies)
    total = second[0]
    for k in range(1, 16):
        total = total + second[k]
    out[rows_at(place, 16)] = total
    copies = exchange(4, CHIPS, lambda other: out.at[rows_at(place, 16)], out.at[rows_at(place, 16)], send, recv)
    finish(copies)


def crop_table(counts, ids, corners):
    shape = (256, 256)
    count = counts[...].astype(jnp.float32)
    before = onehot(iota(shape, 0) < iota(shape, 1))
    starts = nn(count.astype(jnp.bfloat16), before)
    number = (iota(shape, 0) + 256 * lax.axis_index("pair")).astype(jnp.float32)
    total = jnp.zeros((256, 4), jnp.float32)
    for s in range(MOST):
        chosen = onehot((number == starts + s) & (count > s))
        table = jnp.concatenate([ids[s : s + 1, :], corners[s]], axis=0)
        total = total + nt(chosen, table.astype(jnp.bfloat16))
    return total


def as_number(condition_shape, axis):
    return iota(condition_shape, axis).astype(jnp.float32)


def column(ref):
    eye = iota((CH, CH), 0) == iota((CH, CH), 1)
    return jnp.sum(jnp.where(eye, ref[...], 0.0), axis=1, keepdims=True)


def step_kernel(
    pool_at, counts_at, ids_at, corners_at, conv_first_at, conv_second_at, gain_at, head_at,
    out,
    pool, counts, ids, corners, conv_first, conv_second, gain_ref, head_ref, loaded,
    gathered, arrived, leaving, landed, spots, packed, first, second_sums, send, recv,
    toeplitz_first, forward, backward, patches, hidden, hidden_stack, second, logits, cotangent, cotangent_stack,
):
    wait_for_all = greet()
    pairs = (
        (counts_at, counts), (ids_at, ids), (corners_at, corners), (pool_at, pool),
        (conv_first_at, conv_first), (conv_second_at, conv_second), (gain_at, gain_ref), (head_at, head_ref),
    )
    loads = [pltpu.make_async_copy(*pair, loaded.at[k]) for k, pair in enumerate(pairs)]
    for load in loads:
        load.start()
    _, place = plane_peer(0)
    _, z = z_peer(0)
    for load in loads[0:3]:
        load.wait()
    table = crop_table(counts, ids, corners)
    loads[3].wait()
    blocks = pool[...].reshape(512, 256)
    depth = table[:, 3:4].astype(jnp.int32)
    narrow = onehot(
        (iota((256, 128), 0) // BLOCK == iota((256, 128), 1) // SIDE)
        & (iota((256, 128), 0) % BLOCK == iota((256, 128), 1) % SIDE)
    )
    for c in range(2):
        chosen = onehot(2.0 * table[:, 0:1] + c == as_number((256, 512), 1))
        slab = nn(chosen, blocks)
        parts = []
        for part in (slab[:, 0:128], slab[:, 128:256]):
            for bit in (16, 8, 4, 2, 1):
                part = jnp.where((depth & bit) != 0, pltpu.roll(part, 128 - bit, 1), part)
            parts.append(part)
        cut = jnp.concatenate(parts, axis=1).astype(jnp.bfloat16)
        gathered[:, 128 * c : 128 * c + 128] = nn(cut, narrow).astype(jnp.bfloat16)
    wait_for_all()
    copies = exchange(0, CHIPS, lambda other: gathered.at[rows_at(other, 16)], arrived.at[rows_at(place, 16)], send, recv)
    arrived[rows_at(place, 16)] = gathered[rows_at(place, 16)]
    for load in loads[4:]:
        load.wait()
    expand_first(conv_first, toeplitz_first)
    expand_second(conv_second, forward, backward)
    table = table.astype(jnp.bfloat16)
    row = iota((128, 1), 0)
    crop = row // 16 * 2 + row % 16 // 8
    about = nn(onehot(iota((128, 256), 1) == place * 16 + crop), table)
    x = jnp.floor((about[:, 1:2] - z.astype(jnp.float32) + 7.0) * 0.125) + (row % 8 // 4).astype(jnp.float32)
    wanted = (x * 4.0 + (row % 4).astype(jnp.float32)) * 16.0 + crop.astype(jnp.float32)
    chosen = onehot(wanted == as_number((128, 256), 1))
    finish(copies)
    leaving[...] = nn(chosen, arrived[...]).astype(jnp.bfloat16)
    copies = exchange(1, DEPTH, lambda other: leaving.at[rows_at(other, 16)], landed.at[rows_at(z, 16)], send, recv)
    landed[rows_at(z, 16)] = leaving[rows_at(z, 16)]
    clear_ends(hidden_stack)
    clear_ends(cotangent_stack)
    gain = column(gain_ref)
    head = column(head_ref).astype(jnp.bfloat16).astype(jnp.float32)
    row = iota((128, 1), 0)
    s, p = row % 32 // 16, row % 16
    about = nn(onehot(iota((128, 256), 1) == place * 16 + z * 2 + s), table)
    x = about[:, 1:2] + p.astype(jnp.float32)
    wanted = (x - 8.0 * jnp.floor(x * 0.125)) * 16.0 + (s * 8 + p // 8 * 4 + row // 32).astype(jnp.float32)
    chosen = onehot((wanted == as_number((128, 128), 1)) & (p < CROP))
    lane = iota((1, 256), 1)
    inside = (lane % SIDE < CROP) & (lane // SIDE < CROP)
    for s in range(2):
        y = about[16 * s : 16 * s + 1, 2:3] + (lane // SIDE).astype(jnp.float32)
        spot = y * SIDE + (lane % SIDE).astype(jnp.float32)
        spots[s] = onehot(jnp.where(inside, spot, -1.0) == as_number((512, 256), 0))
    finish(copies)
    planes = nn(chosen, landed[...]).astype(jnp.bfloat16)
    images, targets = [], []
    for s in range(2):
        whole = jnp.concatenate(
            [
                jnp.concatenate([planes[32 * q + 16 * s : 32 * q + 16 * s + 16, 128 * c : 128 * c + 128] for q in range(4)], axis=1)
                for c in range(2)
            ],
            axis=0,
        )
        window = nn(whole, spots[s])
        images.append(window[0:16])
        targets.append(window[16:28])
    crop_gradients(
        images, jnp.concatenate(targets, axis=1), gain, head, packed,
        toeplitz_first, forward, backward, patches, hidden, hidden_stack, second, logits, cotangent, cotangent_stack,
    )
    reduce_everywhere(packed, out, first, second_sums, send, recv)


SCRATCH = [
    pltpu.VMEM((256, 2, 256), jnp.bfloat16),
    pltpu.VMEM((1, 256), jnp.int32),
    pltpu.VMEM((MOST, 256), jnp.int32),
    pltpu.VMEM((MOST, 3, 256), jnp.int32),
    pltpu.VMEM((27, CH), jnp.float32),
    pltpu.VMEM((27, CH, CH), jnp.float32),
    pltpu.VMEM((1, CH), jnp.float32),
    pltpu.VMEM((1, CH), jnp.float32),
    pltpu.SemaphoreType.DMA((8,)),
    pltpu.VMEM((256, 256), jnp.bfloat16),
    pltpu.VMEM((256, 256), jnp.bfloat16),
    pltpu.VMEM((128, 256), jnp.bfloat16),
    pltpu.VMEM((128, 256), jnp.bfloat16),
    pltpu.VMEM((2, 512, 256), jnp.bfloat16),
    pltpu.VMEM((256, 128), jnp.float32),
    pltpu.VMEM((16, 16, 128), jnp.float32),
    pltpu.VMEM((16, 16, 128), jnp.float32),
    pltpu.SemaphoreType.DMA((5, 16)),
    pltpu.SemaphoreType.DMA((5, 16)),
]


def summed_gradients(pool, crop_ids, crop_corners, counts, conv_first, conv_second, norm_gain, head_weight):
    return pl.pallas_call(
        step_kernel,
        out_shape=jax.ShapeDtypeStruct((256, 128), jnp.float32),
        in_specs=[pl.BlockSpec(memory_space=pltpu.HBM)] * 8,
        out_specs=pl.BlockSpec(memory_space=pltpu.VMEM),
        scratch_shapes=SCRATCH + COMPUTE_SCRATCH,
        compiler_params=pltpu.CompilerParams(
            collective_id=0, has_side_effects=True, vmem_limit_bytes=20 * 1024 * 1024
        ),
    )(*[
        pltpu.with_memory_space_constraint(value, pltpu.HBM)
        for value in (
            pool, counts.reshape(1, 256), crop_ids.T, crop_corners.transpose(1, 2, 0),
            conv_first, conv_second, norm_gain.reshape(1, CH), head_weight.reshape(1, CH),
        )
    ])


beta_first = 0.9
beta_second = 0.999


def adam_update(gradient, momentum, variance):
    next_momentum = beta_first * momentum + (1.0 - beta_first) * gradient
    next_variance = beta_second * variance + (1.0 - beta_second) * gradient * gradient
    return next_momentum / (jnp.sqrt(next_variance) + 1e-08), next_momentum


def adam_kernel(inverse_batch, total, *refs):
    moments, variances, updates, nexts = refs[0:4], refs[4:8], refs[8:12], refs[12:16]
    gradient = total[...] * inverse_batch
    for dx in range(3):
        j = 2 - dx
        part = jnp.concatenate(
            [gradient[0:216, CH * j : CH * j + CH], gradient[72 * j : 72 * j + 72, 96:128]], axis=0
        ).reshape(9, CH, CH)
        taps = slice(9 * dx, 9 * dx + 9)
        updates[1][taps], nexts[1][taps] = adam_update(part, moments[1][taps], variances[1][taps])
        part = gradient[216:225, CH * dx : CH * dx + CH]
        updates[0][taps], nexts[0][taps] = adam_update(part, moments[0][taps], variances[0][taps])
    for place in (2, 3):
        part = gradient[214 + place : 215 + place, 96:128]
        updates[place][...], nexts[place][...] = adam_update(part, moments[place][...], variances[place][...])


def adam(total, batch_size, moments, variances):
    rows = [value.reshape(1, CH) if value.ndim == 1 else value for value in (*moments, *variances)]
    shapes = [jax.ShapeDtypeStruct(value.shape, jnp.float32) for value in rows[0:4]]
    rows = [
        value if value.ndim == 3 else pltpu.with_memory_space_constraint(value, pltpu.HBM) for value in rows
    ]
    results = pl.pallas_call(
        functools.partial(adam_kernel, 1.0 / batch_size),
        out_shape=shapes + shapes,
        in_specs=[pl.BlockSpec(memory_space=pltpu.VMEM)] * 9,
        out_specs=[pl.BlockSpec(memory_space=pltpu.VMEM)] * 8,
        compiler_params=pltpu.CompilerParams(vmem_limit_bytes=8 * 1024 * 1024),
    )(total, *rows)
    return tuple(value.reshape(CH) if value.shape == (1, CH) else value for value in results)


SHARE = 2


def shards(
    pool, crop_ids, crop_corners, counts, conv_first, conv_second, norm_gain, head_weight,
    momentum_first, momentum_second, momentum_gain, momentum_head,
    variance_first, variance_second, variance_gain, variance_head,
):
    total = summed_gradients(pool, crop_ids, crop_corners, counts, conv_first, conv_second, norm_gain, head_weight)
    return adam(
        total, counts.shape[0] * SHARE,
        (momentum_first, momentum_second, momentum_gain, momentum_head),
        (variance_first, variance_second, variance_gain, variance_head),
    )


def solution(mesh):
    in_specs = (P(None, None, "dp"),) + (P(),) * 15
    return jax.shard_map(shards, mesh=mesh, in_specs=in_specs, out_specs=(P(),) * 8, check_vma=False)
```

```python
import functools

import jax
import jax.numpy as jnp
from jax import lax
from jax.experimental import pallas as pl
from jax.experimental.pallas import tpu as pltpu
from jax.sharding import PartitionSpec as P

CH = 32
CROP = 12
BLOCK = 32
MOST = 3


SIDE = 16
PLANE = CROP * CROP
PITCH = PLANE + 2 * CROP
PART = 384
LANES = 2 * PART
VOXELS = CROP * CROP * CROP
BAND = 6 * CH
TAPS = 9 * BAND


def iota(shape, axis):
    return lax.broadcasted_iota(jnp.int32, shape, axis)


def nt(a, b):
    return lax.dot_general(a, b, (((1,), (1,)), ((), ())), preferred_element_type=jnp.float32)


def nn(a, b):
    return jnp.dot(a, b, preferred_element_type=jnp.float32)


def onehot(condition):
    return jnp.where(condition, 1.0, 0.0).astype(jnp.bfloat16)


def in_crop():
    lane = iota((1, PART), 1)
    return (lane < 2 * PITCH) & (lane % PITCH < PLANE)


def edges(reach):
    z = iota((1, PART), 1) % PITCH % CROP
    return z < CROP - reach, None, z >= reach


def sources(value, masks):
    value = value.astype(jnp.bfloat16)
    return [value if mask is None else jnp.where(mask, value, jnp.zeros_like(value)) for mask in masks]


def moved(source, dy, dz):
    amount = (-(CROP * dy + dz)) % PART
    return (pltpu.roll(source, amount, 1) if amount else source).astype(jnp.bfloat16)


def by_crop(columns):
    return jnp.where(iota((1, PART), 1) < PITCH, columns[0], columns[1])


def crop_sums(value):
    lane = iota((1, PART), 1)
    value = jnp.where(in_crop(), value, 0.0)
    first = jnp.sum(jnp.where(lane < PITCH, value, 0.0), axis=1, keepdims=True)
    return first, jnp.sum(jnp.where(lane >= PITCH, value, 0.0), axis=1, keepdims=True)


def expand_first(conv_first, toeplitz_first):
    weights = conv_first[...].astype(jnp.bfloat16)
    repeat = onehot(iota((12 * CH, CH), 0) % CH == iota((12 * CH, CH), 1))
    row, column = iota((12 * CH, 144), 0), iota((12 * CH, 144), 1)
    place = row // CH
    step = column % 16 - (2 * (place % 6) + place // 6) + 1
    total = jnp.zeros((12 * CH, 144), jnp.float32)
    for dx in range(3):
        tap = onehot(iota((144, 27), 0) // 16 + 9 * dx == iota((144, 27), 1))
        spread = nn(tap, weights).astype(jnp.bfloat16)
        total = jnp.where(step == dx, nt(repeat, spread), total)
    toeplitz_first[...] = total.astype(jnp.bfloat16)


def expand_second(conv_second, forward, backward):
    eye = onehot(iota((CH, CH), 0) == iota((CH, CH), 1))
    zero = jnp.zeros((CH, 256 - 3 * CH), jnp.float32)
    plain, turned = [], []
    for tap in range(9):
        blocks = [conv_second[9 * dx + tap] for dx in range(3)]
        plain.append(jnp.concatenate([blocks[2], blocks[1], blocks[0], zero], axis=1))
        stacked = jnp.concatenate(blocks, axis=0).astype(jnp.bfloat16)
        turned.append(jnp.concatenate([nt(eye, stacked), zero], axis=1))
    for i in range(6):
        rows = slice(i * CH, i * CH + CH)
        amount = (CH * (i - 1)) % 256
        for strips, matrix in ((plain, backward), (turned, forward)):
            bands = [(pltpu.roll(strip, amount, 1) if amount else strip)[:, 0:BAND] for strip in strips]
            matrix[rows, :] = jnp.concatenate(bands, axis=1).astype(jnp.bfloat16)


def crop_gradients(
    image, target, gain, head, packed,
    toeplitz_first, forward, backward, patches, hidden, hidden_stack, second, logits, cotangent, cotangent_stack,
):
    halves = (slice(0, PART), slice(PART, LANES))
    places = [(parity, i) for parity in range(2) for i in range(6)]
    steps = [(tap // 3 - 1, tap % 3 - 1) for tap in range(9)]
    valid = in_crop()
    image = sources(image, edges(1))
    for tap, (dy, dz) in enumerate(steps):
        patches[tap * 16 : tap * 16 + 16, :] = moved(image[dz + 1], dy, dz)
    masks = edges(2)
    for parity, half in enumerate(halves):
        first_map = nn(toeplitz_first[parity * BAND : parity * BAND + BAND, :], patches[...])
        value = jnp.where(valid, jnp.maximum(first_map, 0.0), 0.0)
        hidden[:, half] = value.astype(jnp.bfloat16)
        value = sources(value, masks)
        for tap, (dy, dz) in enumerate(steps):
            hidden_stack[tap * BAND : tap * BAND + BAND, half] = moved(value[dz + 1], 2 * dy, 2 * dz)
    second[...] = nn(forward[...], hidden_stack[...])
    scale = 1.0 / VOXELS
    total = jnp.zeros((CH, PART), jnp.float32)
    for parity, i in places:
        total = total + second[i * CH : i * CH + CH, halves[parity]]
    center = by_crop([value * scale for value in crop_sums(total)])
    total = jnp.zeros((CH, PART), jnp.float32)
    for parity, i in places:
        away = second[i * CH : i * CH + CH, halves[parity]] - center
        total = total + away * away
    inverse = by_crop([lax.rsqrt(value * scale + 1e-05) for value in crop_sums(total)])
    for parity, i in places:
        rows, half, plane = slice(i * CH, i * CH + CH), halves[parity], 2 * i + parity
        hat = (second[rows, half] - center) * inverse
        second[rows, half] = hat
        joined = (jnp.maximum(hat * gain, 0.0) + hidden[rows, half].astype(jnp.float32)).astype(jnp.bfloat16)
        logits[plane : plane + 1, :] = jnp.sum(joined.astype(jnp.float32) * head, axis=0, keepdims=True)
    slope = 1.0 / (1.0 + jnp.exp(-logits[0:12, :])) - target
    logits[0:12, :] = jnp.where(valid, slope * scale, 0.0)
    sum_plain = jnp.zeros((CH, PART), jnp.float32)
    sum_hat = jnp.zeros((CH, PART), jnp.float32)
    sum_head = jnp.zeros((CH, PART), jnp.float32)
    for parity, i in places:
        rows, half, plane = slice(i * CH, i * CH + CH), halves[parity], 2 * i + parity
        hat = second[rows, half]
        normed = hat * gain
        slope = logits[plane : plane + 1, :]
        joined = (jnp.maximum(normed, 0.0) + hidden[rows, half].astype(jnp.float32)).astype(jnp.bfloat16)
        sum_head = sum_head + joined.astype(jnp.float32) * slope
        passed = jnp.where(normed > 0.0, slope, 0.0)
        sum_plain = sum_plain + passed
        sum_hat = sum_hat + passed * hat
    grad_head = sum(crop_sums(sum_head))
    sums_plain = [head * value for value in crop_sums(sum_plain)]
    sums_hat = [head * value for value in crop_sums(sum_hat)]
    grad_gain = sum(sums_hat)
    mean_plain = by_crop([value * scale for value in sums_plain])
    mean_hat = by_crop([value * scale for value in sums_hat])
    factor = jnp.where(valid, inverse * gain, 0.0)
    for parity, i in places:
        rows, half, plane = slice(i * CH, i * CH + CH), halves[parity], 2 * i + parity
        hat = second[rows, half]
        slope = logits[plane : plane + 1, :]
        passed = jnp.where(hat * gain > 0.0, head * slope, 0.0)
        value = factor * (passed - mean_plain - hat * mean_hat)
        cotangent[rows, half] = value.astype(jnp.bfloat16)
        value = sources(value, masks)
        for tap, (dy, dz) in enumerate(steps):
            place = tap * BAND + i * CH
            cotangent_stack[place : place + CH, half] = moved(value[1 - dz], -2 * dy, -2 * dz)
    cotangent[BAND:256, :] = jnp.zeros((256 - BAND, LANES), jnp.bfloat16)
    turned = cotangent[...].T
    lane = iota((CH, 128), 1)
    for tap in range(9):
        products = nn(hidden_stack[tap * BAND : tap * BAND + BAND, :], turned)
        total = jnp.zeros((CH, 256), jnp.float32)
        for i in range(6):
            band = products[i * CH : i * CH + CH, :]
            amount = (-CH * (i - 1)) % 256
            total = total + (pltpu.roll(band, amount, 1) if amount else band)
        total = total[:, 0:128]
        at = tap * CH
        if at < 216:
            count = min(CH, 216 - at)
            packed[at : at + count, :] = jnp.where(lane < 96, total, 0.0)[0:count]
        if at + CH > 216:
            skip = max(0, 216 - at)
            for j in range(3):
                shifted = pltpu.roll(total, 96 - CH * j, 1)
                shifted = jnp.where(lane >= 96, shifted, 0.0)[skip:CH]
                to = 72 * j + at + skip - 216
                packed[to : to + CH - skip, :] = packed[to : to + CH - skip, :] + shifted
    back = nn(backward[...], cotangent_stack[...])
    for parity, i in places:
        rows, half, plane = slice(i * CH, i * CH + CH), halves[parity], 2 * i + parity
        whole = back[rows, half] + head * logits[plane : plane + 1, :]
        alive = hidden[rows, half].astype(jnp.float32) > 0.0
        second[rows, half] = jnp.where(alive, whole, 0.0)
    lane = iota((9, 128), 1)
    small = jnp.zeros((9, 128), jnp.float32)
    products = jnp.concatenate([nt(patches[...], second[:, half].astype(jnp.bfloat16)) for half in halves], axis=1)
    row, column = iota((144, 2 * BAND), 0), iota((144, 2 * BAND), 1)
    place = column // CH
    step = row % 16 - (2 * (place % 6) + place // 6) + 1
    for dx in range(3):
        part = jnp.where(step == dx, products, 0.0)
        part = jnp.sum(part.reshape(9, 16, 2 * BAND), axis=1)
        part = part[:, 0:128] + part[:, 128:256] + part[:, 256:384]
        part = part + pltpu.roll(part, 64, 1)
        part = part + pltpu.roll(part, 32, 1)
        small = jnp.where(lane // CH == dx, part, small)
    packed[216:225, :] = small
    pick = iota((CH, 128), 0) + 96 == iota((CH, 128), 1)
    packed[216:217, :] = packed[216:217, :] + jnp.sum(jnp.where(pick, grad_gain, 0.0), axis=0, keepdims=True)
    packed[217:218, :] = packed[217:218, :] + jnp.sum(jnp.where(pick, grad_head, 0.0), axis=0, keepdims=True)
    packed[225:256, :] = jnp.zeros((31, 128), jnp.float32)


COMPUTE_SCRATCH = [
    pltpu.VMEM((12 * CH, 144), jnp.bfloat16),
    pltpu.VMEM((BAND, TAPS), jnp.bfloat16),
    pltpu.VMEM((BAND, TAPS), jnp.bfloat16),
    pltpu.VMEM((144, PART), jnp.bfloat16),
    pltpu.VMEM((BAND, LANES), jnp.bfloat16),
    pltpu.VMEM((TAPS, LANES), jnp.bfloat16),
    pltpu.VMEM((BAND, LANES), jnp.float32),
    pltpu.VMEM((16, PART), jnp.float32),
    pltpu.VMEM((256, LANES), jnp.bfloat16),
    pltpu.VMEM((TAPS, LANES), jnp.bfloat16),
]


MESH = pl.DeviceIdType.MESH


def plane_peer(k):
    dp = lax.axis_index("dp")
    x = lax.rem(dp // 32 + k // 4, 4)
    y = lax.rem(lax.rem(dp, 4) + k % 4, 4)
    z = lax.rem(dp // 4, 8)
    return (x * 32 + z * 4 + y, lax.axis_index("pair")), x * 4 + y


def z_peer(k):
    dp = lax.axis_index("dp")
    z = lax.rem(lax.rem(dp // 4, 8) + k, 8)
    return ((dp // 32) * 32 + z * 4 + lax.rem(dp, 4), lax.axis_index("pair")), z


def column_peer(k):
    (dp, _), z = z_peer(k // 2)
    core = lax.rem(lax.axis_index("pair") + k % 2, 2)
    return (dp, core), z * 2 + core


PLANE_STEPS = (10, 6, 9, 11, 14, 2, 5, 7, 8, 13, 15, 1, 3, 4, 12)
Z_STEPS = (4, 3, 5, 2, 6, 1, 7)
COLUMN_STEPS = (9, 8, 7, 6, 11, 10, 5, 4, 13, 12, 3, 2, 15, 14, 1)
CHIPS, DEPTH, COLUMN = (plane_peer, PLANE_STEPS), (z_peer, Z_STEPS), (column_peer, COLUMN_STEPS)
GROUPS = (CHIPS, COLUMN)


def rows_at(place, count):
    return pl.ds(pl.multiple_of(place * count, count), count)


def greet():
    barrier = pltpu.get_barrier_semaphore()
    for peer, steps in GROUPS:
        for k in steps:
            pl.semaphore_signal(barrier, inc=1, device_id=peer(k)[0], device_id_type=MESH)
    return lambda: pl.semaphore_wait(barrier, sum(len(steps) for _, steps in GROUPS))


def exchange(stage, group, source, target, send, recv):
    peer, steps = group
    copies = []
    for k in steps:
        device, place = peer(k)
        copy = pltpu.make_async_remote_copy(
            src_ref=source(place), dst_ref=target, send_sem=send.at[stage, k], recv_sem=recv.at[stage, k],
            device_id=device, device_id_type=MESH,
        )
        copy.start()
        copies.append(copy)
    return copies


def finish(copies):
    for copy in copies:
        copy.wait()


def reduce_everywhere(packed, out, first, second, send, recv):
    _, place = plane_peer(0)
    _, column = column_peer(0)
    copies = exchange(2, CHIPS, lambda other: packed.at[rows_at(other, 16)], first.at[place], send, recv)
    first[place] = packed[rows_at(place, 16)]
    finish(copies)
    total = first[0]
    for k in range(1, 16):
        total = total + first[k]
    second[column] = total
    copies = exchange(3, COLUMN, lambda other: second.at[column], second.at[column], send, recv)
    finish(copies)
    total = second[0]
    for k in range(1, 16):
        total = total + second[k]
    out[rows_at(place, 16)] = total
    copies = exchange(4, CHIPS, lambda other: out.at[rows_at(place, 16)], out.at[rows_at(place, 16)], send, recv)
    finish(copies)


def crop_table(counts, ids, corners):
    shape = (256, 256)
    count = counts[...].astype(jnp.float32)
    before = onehot(iota(shape, 0) < iota(shape, 1))
    starts = nn(count.astype(jnp.bfloat16), before)
    number = (iota(shape, 0) + 256 * lax.axis_index("pair")).astype(jnp.float32)
    total = jnp.zeros((256, 4), jnp.float32)
    for s in range(MOST):
        chosen = onehot((number == starts + s) & (count > s))
        table = jnp.concatenate([ids[s : s + 1, :], corners[s]], axis=0)
        total = total + nt(chosen, table.astype(jnp.bfloat16))
    return total


def as_number(condition_shape, axis):
    return iota(condition_shape, axis).astype(jnp.float32)


def column(ref):
    eye = iota((CH, CH), 0) == iota((CH, CH), 1)
    return jnp.sum(jnp.where(eye, ref[...], 0.0), axis=1, keepdims=True)


def step_kernel(
    pool_at, counts_at, ids_at, corners_at, conv_first_at, conv_second_at, gain_at, head_at, *refs
):
    small_at, moments_at, (out, small, *moments), refs = refs[0:6], refs[6:8], refs[8:12], refs[12:]
    (
    pool, counts, ids, corners, conv_first, conv_second, gain_ref, head_ref, loaded,
    gathered, arrived, leaving, landed, spots, packed, first, second_sums, send, recv,
    toeplitz_first, forward, backward, patches, hidden, hidden_stack, second, logits, cotangent, cotangent_stack,
    ) = refs
    wait_for_all = greet()
    pairs = (
        (counts_at, counts), (ids_at, ids), (corners_at, corners), (pool_at, pool),
        (conv_first_at, conv_first), (conv_second_at, conv_second), (gain_at, gain_ref), (head_at, head_ref),
    ) + tuple((source, small.at[k, 0 : source.shape[0]]) for k, source in enumerate(small_at)) + tuple(zip(moments_at, moments))
    loads = [pltpu.make_async_copy(*pair, loaded.at[k]) for k, pair in enumerate(pairs)]
    for load in loads:
        load.start()
    _, place = plane_peer(0)
    _, z = z_peer(0)
    for load in loads[0:3]:
        load.wait()
    table = crop_table(counts, ids, corners)
    loads[3].wait()
    blocks = pool[...].reshape(512, 256)
    depth = table[:, 3:4].astype(jnp.int32)
    narrow = onehot(
        (iota((256, 128), 0) // BLOCK == iota((256, 128), 1) // SIDE)
        & (iota((256, 128), 0) % BLOCK == iota((256, 128), 1) % SIDE)
    )
    for c in range(2):
        chosen = onehot(2.0 * table[:, 0:1] + c == as_number((256, 512), 1))
        slab = nn(chosen, blocks)
        parts = []
        for part in (slab[:, 0:128], slab[:, 128:256]):
            for bit in (16, 8, 4, 2, 1):
                part = jnp.where((depth & bit) != 0, pltpu.roll(part, 128 - bit, 1), part)
            parts.append(part)
        cut = jnp.concatenate(parts, axis=1).astype(jnp.bfloat16)
        gathered[:, 128 * c : 128 * c + 128] = nn(cut, narrow).astype(jnp.bfloat16)
    wait_for_all()
    copies = exchange(0, CHIPS, lambda other: gathered.at[rows_at(other, 16)], arrived.at[rows_at(place, 16)], send, recv)
    arrived[rows_at(place, 16)] = gathered[rows_at(place, 16)]
    for load in loads[4:]:
        load.wait()
    expand_first(conv_first, toeplitz_first)
    expand_second(conv_second, forward, backward)
    table = table.astype(jnp.bfloat16)
    row = iota((128, 1), 0)
    crop = row // 16 * 2 + row % 16 // 8
    about = nn(onehot(iota((128, 256), 1) == place * 16 + crop), table)
    x = jnp.floor((about[:, 1:2] - z.astype(jnp.float32) + 7.0) * 0.125) + (row % 8 // 4).astype(jnp.float32)
    wanted = (x * 4.0 + (row % 4).astype(jnp.float32)) * 16.0 + crop.astype(jnp.float32)
    chosen = onehot(wanted == as_number((128, 256), 1))
    finish(copies)
    leaving[...] = nn(chosen, arrived[...]).astype(jnp.bfloat16)
    copies = exchange(1, DEPTH, lambda other: leaving.at[rows_at(other, 16)], landed.at[rows_at(z, 16)], send, recv)
    landed[rows_at(z, 16)] = leaving[rows_at(z, 16)]
    gain = column(gain_ref)
    head = column(head_ref).astype(jnp.bfloat16).astype(jnp.float32)
    row = iota((128, 1), 0)
    s, p = row % 32 // 16, row % 16
    about = nn(onehot(iota((128, 256), 1) == place * 16 + z * 2 + s), table)
    x = about[:, 1:2] + p.astype(jnp.float32)
    wanted = (x - 8.0 * jnp.floor(x * 0.125)) * 16.0 + (s * 8 + p // 8 * 4 + row // 32).astype(jnp.float32)
    chosen = onehot((wanted == as_number((128, 128), 1)) & (p < CROP))
    lane = iota((1, PART), 1)
    for s in range(2):
        y = about[16 * s : 16 * s + 1, 2:3] + (lane % PITCH // CROP).astype(jnp.float32)
        spot = y * SIDE + (lane % PITCH % CROP).astype(jnp.float32)
        inside = in_crop() & (lane // PITCH == s)
        spots[s] = onehot(jnp.where(inside, spot, -1.0) == as_number((512, PART), 0))
    finish(copies)
    planes = nn(chosen, landed[...]).astype(jnp.bfloat16)
    window = jnp.zeros((32, PART), jnp.float32)
    for s in range(2):
        whole = jnp.concatenate(
            [
                jnp.concatenate([planes[32 * q + 16 * s : 32 * q + 16 * s + 16, 128 * c : 128 * c + 128] for q in range(4)], axis=1)
                for c in range(2)
            ],
            axis=0,
        )
        window = window + nn(whole, spots[s])
    crop_gradients(
        window[0:16], window[16:28], gain, head, packed,
        toeplitz_first, forward, backward, patches, hidden, hidden_stack, second, logits, cotangent, cotangent_stack,
    )
    reduce_everywhere(packed, out, first, second_sums, send, recv)


SCRATCH = [
    pltpu.VMEM((256, 2, 256), jnp.bfloat16),
    pltpu.VMEM((1, 256), jnp.int32),
    pltpu.VMEM((MOST, 256), jnp.int32),
    pltpu.VMEM((MOST, 3, 256), jnp.int32),
    pltpu.VMEM((27, CH), jnp.float32),
    pltpu.VMEM((27, CH, CH), jnp.float32),
    pltpu.VMEM((1, CH), jnp.float32),
    pltpu.VMEM((1, CH), jnp.float32),
    pltpu.SemaphoreType.DMA((16,)),
    pltpu.VMEM((256, 256), jnp.bfloat16),
    pltpu.VMEM((256, 256), jnp.bfloat16),
    pltpu.VMEM((128, 256), jnp.bfloat16),
    pltpu.VMEM((128, 256), jnp.bfloat16),
    pltpu.VMEM((2, 512, PART), jnp.bfloat16),
    pltpu.VMEM((256, 128), jnp.float32),
    pltpu.VMEM((16, 16, 128), jnp.float32),
    pltpu.VMEM((16, 16, 128), jnp.float32),
    pltpu.SemaphoreType.DMA((5, 16)),
    pltpu.SemaphoreType.DMA((5, 16)),
]


def summed_gradients(pool, crop_ids, crop_corners, counts, conv_first, conv_second, norm_gain, head_weight, small, large):
    return pl.pallas_call(
        step_kernel,
        out_shape=[jax.ShapeDtypeStruct((256, 128), jnp.float32), jax.ShapeDtypeStruct((6, 32, CH), jnp.float32)]
        + [jax.ShapeDtypeStruct((27, CH, CH), jnp.float32)] * 2,
        in_specs=[pl.BlockSpec(memory_space=pltpu.HBM)] * 16,
        out_specs=[pl.BlockSpec(memory_space=pltpu.VMEM)] * 4,
        scratch_shapes=SCRATCH + COMPUTE_SCRATCH,
        compiler_params=pltpu.CompilerParams(
            collective_id=0, has_side_effects=True, vmem_limit_bytes=20 * 1024 * 1024
        ),
    )(*[
        pltpu.with_memory_space_constraint(value, pltpu.HBM)
        for value in (
            pool, counts.reshape(1, 256), crop_ids.T, crop_corners.transpose(1, 2, 0),
            conv_first, conv_second, norm_gain.reshape(1, CH), head_weight.reshape(1, CH),
            *[value.reshape(-1, CH) for value in small],
            *large,
        )
    ])


beta_first = 0.9
beta_second = 0.999


def adam_update(gradient, momentum, variance):
    next_momentum = beta_first * momentum + (1.0 - beta_first) * gradient
    next_variance = beta_second * variance + (1.0 - beta_second) * gradient * gradient
    return next_momentum / (jnp.sqrt(next_variance) + 1e-08), next_momentum


def adam_kernel(inverse_batch, total, small, moment, variance, *refs):
    updates, nexts = refs[0:4], refs[4:8]
    gradient = total[...] * inverse_batch
    for dx in range(3):
        j = 2 - dx
        part = jnp.concatenate(
            [gradient[0:216, CH * j : CH * j + CH], gradient[72 * j : 72 * j + 72, 96:128]], axis=0
        ).reshape(9, CH, CH)
        taps = slice(9 * dx, 9 * dx + 9)
        updates[1][taps], nexts[1][taps] = adam_update(part, moment[taps], variance[taps])
        part = gradient[216:225, CH * dx : CH * dx + CH]
        updates[0][taps], nexts[0][taps] = adam_update(part, small[0, taps], small[3, taps])
    for k in (1, 2):
        part = gradient[215 + k : 216 + k, 96:128]
        updates[k + 1][...], nexts[k + 1][...] = adam_update(part, small[k, 0:1], small[k + 3, 0:1])


def adam(batch_size, total, small, moment, variance):
    shapes = [jax.ShapeDtypeStruct(shape, jnp.float32) for shape in ((27, CH), (27, CH, CH), (1, CH), (1, CH))]
    results = pl.pallas_call(
        functools.partial(adam_kernel, 1.0 / batch_size),
        out_shape=shapes + shapes,
        in_specs=[pl.BlockSpec(memory_space=pltpu.VMEM)] * 4,
        out_specs=[pl.BlockSpec(memory_space=pltpu.VMEM)] * 8,
        compiler_params=pltpu.CompilerParams(vmem_limit_bytes=8 * 1024 * 1024),
    )(total, small, moment, variance)
    return tuple(value.reshape(CH) if value.shape == (1, CH) else value for value in results)


SHARE = 2


def shards(
    pool, crop_ids, crop_corners, counts, conv_first, conv_second, norm_gain, head_weight,
    momentum_first, momentum_second, momentum_gain, momentum_head,
    variance_first, variance_second, variance_gain, variance_head,
):
    moved_on = summed_gradients(
        pool, crop_ids, crop_corners, counts, conv_first, conv_second, norm_gain, head_weight,
        (momentum_first, momentum_gain, momentum_head, variance_first, variance_gain, variance_head),
        (momentum_second, variance_second),
    )
    return adam(counts.shape[0] * SHARE, *moved_on)


def solution(mesh):
    in_specs = (P(None, None, "dp"),) + (P(),) * 15
    return jax.shard_map(shards, mesh=mesh, in_specs=in_specs, out_specs=(P(),) * 8, check_vma=False)
```

```python
import functools

import jax
import jax.numpy as jnp
from jax import lax
from jax.experimental import pallas as pl
from jax.experimental.pallas import tpu as pltpu
from jax.sharding import PartitionSpec as P

CH = 32
CROP = 12
BLOCK = 32
MOST = 3


SIDE = 16
PLANE = CROP * CROP
PITCH = PLANE + 2 * CROP
PART = 384
LANES = 2 * PART
VOXELS = CROP * CROP * CROP
BAND = 6 * CH
TAPS = 9 * BAND


def iota(shape, axis):
    return lax.broadcasted_iota(jnp.int32, shape, axis)


def nt(a, b):
    return lax.dot_general(a, b, (((1,), (1,)), ((), ())), preferred_element_type=jnp.float32)


def nn(a, b):
    return jnp.dot(a, b, preferred_element_type=jnp.float32)


def onehot(condition):
    return jnp.where(condition, 1.0, 0.0).astype(jnp.bfloat16)


def in_crop():
    lane = iota((1, PART), 1)
    return (lane < 2 * PITCH) & (lane % PITCH < PLANE)


def edges(reach):
    z = iota((1, PART), 1) % PITCH % CROP
    return z < CROP - reach, None, z >= reach


def sources(value, masks):
    value = value.astype(jnp.bfloat16)
    return [value if mask is None else jnp.where(mask, value, jnp.zeros_like(value)) for mask in masks]


def moved(source, dy, dz):
    amount = (-(CROP * dy + dz)) % PART
    return (pltpu.roll(source, amount, 1) if amount else source).astype(jnp.bfloat16)


def by_crop(columns):
    return jnp.where(iota((1, PART), 1) < PITCH, columns[0], columns[1])


def crop_sums(value):
    lane = iota((1, PART), 1)
    value = jnp.where(in_crop(), value, 0.0)
    first = jnp.sum(jnp.where(lane < PITCH, value, 0.0), axis=1, keepdims=True)
    return first, jnp.sum(jnp.where(lane >= PITCH, value, 0.0), axis=1, keepdims=True)


def expand_first(conv_first, toeplitz_first):
    weights = conv_first[...].astype(jnp.bfloat16)
    repeat = onehot(iota((12 * CH, CH), 0) % CH == iota((12 * CH, CH), 1))
    row, column = iota((12 * CH, 144), 0), iota((12 * CH, 144), 1)
    place = row // CH
    step = column % 16 - (2 * (place % 6) + place // 6) + 1
    total = jnp.zeros((12 * CH, 144), jnp.float32)
    for dx in range(3):
        tap = onehot(iota((144, 27), 0) // 16 + 9 * dx == iota((144, 27), 1))
        spread = nn(tap, weights).astype(jnp.bfloat16)
        total = jnp.where(step == dx, nt(repeat, spread), total)
    toeplitz_first[...] = total.astype(jnp.bfloat16)


def expand_second(conv_second, forward, backward):
    eye = onehot(iota((CH, CH), 0) == iota((CH, CH), 1))
    zero = jnp.zeros((CH, 256 - 3 * CH), jnp.float32)
    plain, turned = [], []
    for tap in range(9):
        blocks = [conv_second[9 * dx + tap] for dx in range(3)]
        plain.append(jnp.concatenate([blocks[2], blocks[1], blocks[0], zero], axis=1))
        stacked = jnp.concatenate(blocks, axis=0).astype(jnp.bfloat16)
        turned.append(jnp.concatenate([nt(eye, stacked), zero], axis=1))
    for i in range(6):
        rows = slice(i * CH, i * CH + CH)
        amount = (CH * (i - 1)) % 256
        for strips, matrix in ((plain, backward), (turned, forward)):
            bands = [(pltpu.roll(strip, amount, 1) if amount else strip)[:, 0:BAND] for strip in strips]
            matrix[rows, :] = jnp.concatenate(bands, axis=1).astype(jnp.bfloat16)


def crop_gradients(
    image, target, gain, head, packed,
    toeplitz_first, forward, backward, patches, hidden, hidden_stack, second, logits, cotangent, cotangent_stack,
):
    halves = (slice(0, PART), slice(PART, LANES))
    places = [(parity, i) for parity in range(2) for i in range(6)]
    steps = [(tap // 3 - 1, tap % 3 - 1) for tap in range(9)]
    valid = in_crop()
    image = sources(image, edges(1))
    for tap, (dy, dz) in enumerate(steps):
        patches[tap * 16 : tap * 16 + 16, :] = moved(image[dz + 1], dy, dz)
    masks = edges(2)
    for parity, half in enumerate(halves):
        first_map = nn(toeplitz_first[parity * BAND : parity * BAND + BAND, :], patches[...])
        value = jnp.where(valid, jnp.maximum(first_map, 0.0), 0.0)
        hidden[:, half] = value.astype(jnp.bfloat16)
        value = sources(value, masks)
        for tap, (dy, dz) in enumerate(steps):
            hidden_stack[tap * BAND : tap * BAND + BAND, half] = moved(value[dz + 1], 2 * dy, 2 * dz)
    second[...] = nn(forward[...], hidden_stack[...])
    scale = 1.0 / VOXELS
    total = jnp.zeros((CH, PART), jnp.float32)
    for parity, i in places:
        total = total + second[i * CH : i * CH + CH, halves[parity]]
    center = by_crop([value * scale for value in crop_sums(total)])
    total = jnp.zeros((CH, PART), jnp.float32)
    for parity, i in places:
        away = second[i * CH : i * CH + CH, halves[parity]] - center
        total = total + away * away
    inverse = by_crop([lax.rsqrt(value * scale + 1e-05) for value in crop_sums(total)])
    for parity, i in places:
        rows, half, plane = slice(i * CH, i * CH + CH), halves[parity], 2 * i + parity
        hat = (second[rows, half] - center) * inverse
        second[rows, half] = hat
        joined = (jnp.maximum(hat * gain, 0.0) + hidden[rows, half].astype(jnp.float32)).astype(jnp.bfloat16)
        logits[plane : plane + 1, :] = jnp.sum(joined.astype(jnp.float32) * head, axis=0, keepdims=True)
    slope = 1.0 / (1.0 + jnp.exp(-logits[0:12, :])) - target
    logits[0:12, :] = jnp.where(valid, slope * scale, 0.0)
    sum_plain = jnp.zeros((CH, PART), jnp.float32)
    sum_hat = jnp.zeros((CH, PART), jnp.float32)
    sum_head = jnp.zeros((CH, PART), jnp.float32)
    for parity, i in places:
        rows, half, plane = slice(i * CH, i * CH + CH), halves[parity], 2 * i + parity
        hat = second[rows, half]
        normed = hat * gain
        slope = logits[plane : plane + 1, :]
        joined = (jnp.maximum(normed, 0.0) + hidden[rows, half].astype(jnp.float32)).astype(jnp.bfloat16)
        sum_head = sum_head + joined.astype(jnp.float32) * slope
        passed = jnp.where(normed > 0.0, slope, 0.0)
        sum_plain = sum_plain + passed
        sum_hat = sum_hat + passed * hat
    grad_head = sum(crop_sums(sum_head))
    sums_plain = [head * value for value in crop_sums(sum_plain)]
    sums_hat = [head * value for value in crop_sums(sum_hat)]
    grad_gain = sum(sums_hat)
    mean_plain = by_crop([value * scale for value in sums_plain])
    mean_hat = by_crop([value * scale for value in sums_hat])
    factor = jnp.where(valid, inverse * gain, 0.0)
    for parity, i in places:
        rows, half, plane = slice(i * CH, i * CH + CH), halves[parity], 2 * i + parity
        hat = second[rows, half]
        slope = logits[plane : plane + 1, :]
        passed = jnp.where(hat * gain > 0.0, head * slope, 0.0)
        value = factor * (passed - mean_plain - hat * mean_hat)
        cotangent[rows, half] = value.astype(jnp.bfloat16)
        value = sources(value, masks)
        for tap, (dy, dz) in enumerate(steps):
            place = tap * BAND + i * CH
            cotangent_stack[place : place + CH, half] = moved(value[1 - dz], -2 * dy, -2 * dz)
    cotangent[BAND:256, :] = jnp.zeros((256 - BAND, LANES), jnp.bfloat16)
    turned = cotangent[...].T
    lane = iota((CH, 128), 1)
    for tap in range(9):
        products = nn(hidden_stack[tap * BAND : tap * BAND + BAND, :], turned)
        total = jnp.zeros((CH, 256), jnp.float32)
        for i in range(6):
            band = products[i * CH : i * CH + CH, :]
            amount = (-CH * (i - 1)) % 256
            total = total + (pltpu.roll(band, amount, 1) if amount else band)
        total = total[:, 0:128]
        at = tap * CH
        if at < 216:
            count = min(CH, 216 - at)
            packed[at : at + count, :] = jnp.where(lane < 96, total, 0.0)[0:count]
        if at + CH > 216:
            skip = max(0, 216 - at)
            for j in range(3):
                shifted = pltpu.roll(total, 96 - CH * j, 1)
                shifted = jnp.where(lane >= 96, shifted, 0.0)[skip:CH]
                to = 72 * j + at + skip - 216
                packed[to : to + CH - skip, :] = packed[to : to + CH - skip, :] + shifted
    return lambda small: first_gradients(
        small, gain, head, grad_gain, grad_head,
        backward, patches, hidden, second, logits, cotangent_stack,
    )


def first_gradients(
    small_sums, gain, head, grad_gain, grad_head, backward, patches, hidden, second, logits, cotangent_stack,
):
    halves = (slice(0, PART), slice(PART, LANES))
    places = [(parity, i) for parity in range(2) for i in range(6)]
    back = nn(backward[...], cotangent_stack[...])
    for parity, i in places:
        rows, half, plane = slice(i * CH, i * CH + CH), halves[parity], 2 * i + parity
        whole = back[rows, half] + head * logits[plane : plane + 1, :]
        alive = hidden[rows, half].astype(jnp.float32) > 0.0
        second[rows, half] = jnp.where(alive, whole, 0.0)
    lane = iota((9, 128), 1)
    small = jnp.zeros((9, 128), jnp.float32)
    products = jnp.concatenate([nt(patches[...], second[:, half].astype(jnp.bfloat16)) for half in halves], axis=1)
    row, column = iota((144, 2 * BAND), 0), iota((144, 2 * BAND), 1)
    place = column // CH
    step = row % 16 - (2 * (place % 6) + place // 6) + 1
    for dx in range(3):
        part = jnp.where(step == dx, products, 0.0)
        part = jnp.sum(part.reshape(9, 16, 2 * BAND), axis=1)
        part = part[:, 0:128] + part[:, 128:256] + part[:, 256:384]
        part = part + pltpu.roll(part, 64, 1)
        part = part + pltpu.roll(part, 32, 1)
        small = jnp.where(lane // CH == dx, part, small)
    small_sums[0:9, :] = small
    pick = iota((CH, 128), 0) + 96 == iota((CH, 128), 1)
    small_sums[0:1, :] = small_sums[0:1, :] + jnp.sum(jnp.where(pick, grad_gain, 0.0), axis=0, keepdims=True)
    small_sums[1:2, :] = small_sums[1:2, :] + jnp.sum(jnp.where(pick, grad_head, 0.0), axis=0, keepdims=True)
    small_sums[9:16, :] = jnp.zeros((7, 128), jnp.float32)


COMPUTE_SCRATCH = [
    pltpu.VMEM((12 * CH, 144), jnp.bfloat16),
    pltpu.VMEM((BAND, TAPS), jnp.bfloat16),
    pltpu.VMEM((BAND, TAPS), jnp.bfloat16),
    pltpu.VMEM((144, PART), jnp.bfloat16),
    pltpu.VMEM((BAND, LANES), jnp.bfloat16),
    pltpu.VMEM((TAPS, LANES), jnp.bfloat16),
    pltpu.VMEM((BAND, LANES), jnp.float32),
    pltpu.VMEM((16, PART), jnp.float32),
    pltpu.VMEM((256, LANES), jnp.bfloat16),
    pltpu.VMEM((TAPS, LANES), jnp.bfloat16),
]


MESH = pl.DeviceIdType.MESH


def plane_peer(k):
    dp = lax.axis_index("dp")
    x = lax.rem(dp // 32 + k // 4, 4)
    y = lax.rem(lax.rem(dp, 4) + k % 4, 4)
    z = lax.rem(dp // 4, 8)
    return (x * 32 + z * 4 + y, lax.axis_index("pair")), x * 4 + y


def z_peer(k):
    dp = lax.axis_index("dp")
    z = lax.rem(lax.rem(dp // 4, 8) + k, 8)
    return ((dp // 32) * 32 + z * 4 + lax.rem(dp, 4), lax.axis_index("pair")), z


def column_peer(k):
    (dp, _), z = z_peer(k // 2)
    core = lax.rem(lax.axis_index("pair") + k % 2, 2)
    return (dp, core), z * 2 + core


PLANE_STEPS = (10, 6, 9, 11, 14, 2, 5, 7, 8, 13, 15, 1, 3, 4, 12)
Z_STEPS = (4, 3, 5, 2, 6, 1, 7)
COLUMN_STEPS = (9, 8, 7, 6, 11, 10, 5, 4, 13, 12, 3, 2, 15, 14, 1)
CHIPS, DEPTH, COLUMN = (plane_peer, PLANE_STEPS), (z_peer, Z_STEPS), (column_peer, COLUMN_STEPS)
GROUPS = (CHIPS, COLUMN)


def rows_at(place, count):
    return pl.ds(pl.multiple_of(place * count, count), count)


def greet():
    barrier = pltpu.get_barrier_semaphore()
    for peer, steps in GROUPS:
        for k in steps:
            pl.semaphore_signal(barrier, inc=1, device_id=peer(k)[0], device_id_type=MESH)
    return lambda: pl.semaphore_wait(barrier, sum(len(steps) for _, steps in GROUPS))


def exchange(stage, group, source, target, send, recv):
    peer, steps = group
    copies = []
    for k in steps:
        device, place = peer(k)
        copy = pltpu.make_async_remote_copy(
            src_ref=source(place), dst_ref=target, send_sem=send.at[stage, k], recv_sem=recv.at[stage, k],
            device_id=device, device_id_type=MESH,
        )
        copy.start()
        copies.append(copy)
    return copies


def finish(copies):
    for copy in copies:
        copy.wait()


def added(slots):
    total = slots[0]
    for k in range(1, 16):
        total = total + slots[k]
    return total


def reduce_everywhere(packed, finish_gradients, out, small_out, first, second, small, small_first, small_second, send, recv):
    _, place = plane_peer(0)
    _, column = column_peer(0)
    parts = exchange(2, CHIPS, lambda other: packed.at[rows_at(other, 16)], first.at[place], send, recv)
    first[place] = packed[rows_at(place, 16)]
    finish_gradients(small)
    smalls = exchange(5, CHIPS, lambda other: small, small_first.at[place], send, recv)
    small_first[place] = small[...]
    finish(parts)
    second[column] = added(first)
    parts = exchange(3, COLUMN, lambda other: second.at[column], second.at[column], send, recv)
    finish(smalls)
    small_second[column] = added(small_first)
    smalls = exchange(6, COLUMN, lambda other: small_second.at[column], small_second.at[column], send, recv)
    finish(parts)
    out[rows_at(place, 16)] = added(second)
    parts = exchange(4, CHIPS, lambda other: out.at[rows_at(place, 16)], out.at[rows_at(place, 16)], send, recv)
    finish(smalls)
    small_out[...] = added(small_second)
    finish(parts)


def crop_table(counts, ids, corners):
    shape = (256, 256)
    count = counts[...].astype(jnp.float32)
    before = onehot(iota(shape, 0) < iota(shape, 1))
    starts = nn(count.astype(jnp.bfloat16), before)
    number = (iota(shape, 0) + 256 * lax.axis_index("pair")).astype(jnp.float32)
    total = jnp.zeros((256, 4), jnp.float32)
    for s in range(MOST):
        chosen = onehot((number == starts + s) & (count > s))
        table = jnp.concatenate([ids[s : s + 1, :], corners[s]], axis=0)
        total = total + nt(chosen, table.astype(jnp.bfloat16))
    return total


def as_number(condition_shape, axis):
    return iota(condition_shape, axis).astype(jnp.float32)


def column(ref):
    eye = iota((CH, CH), 0) == iota((CH, CH), 1)
    return jnp.sum(jnp.where(eye, ref[...], 0.0), axis=1, keepdims=True)


def step_kernel(
    pool_at, counts_at, ids_at, corners_at, conv_first_at, conv_second_at, gain_at, head_at, *refs
):
    small_at, moments_at, (out, small_out, small, *moments), refs = refs[0:6], refs[6:8], refs[8:13], refs[13:]
    (
    pool, counts, ids, corners, conv_first, conv_second, gain_ref, head_ref, loaded,
    gathered, arrived, leaving, landed, spots, packed, first, second_sums, small_sums, small_first, small_second, send, recv,
    toeplitz_first, forward, backward, patches, hidden, hidden_stack, second, logits, cotangent, cotangent_stack,
    ) = refs
    wait_for_all = greet()
    pairs = (
        (counts_at, counts), (ids_at, ids), (corners_at, corners), (pool_at, pool),
        (conv_first_at, conv_first), (conv_second_at, conv_second), (gain_at, gain_ref), (head_at, head_ref),
    ) + tuple((source, small.at[k, 0 : source.shape[0]]) for k, source in enumerate(small_at)) + tuple(zip(moments_at, moments))
    loads = [pltpu.make_async_copy(*pair, loaded.at[k]) for k, pair in enumerate(pairs)]
    for load in loads:
        load.start()
    _, place = plane_peer(0)
    _, z = z_peer(0)
    for load in loads[0:3]:
        load.wait()
    table = crop_table(counts, ids, corners)
    loads[3].wait()
    blocks = pool[...].reshape(512, 256)
    depth = table[:, 3:4].astype(jnp.int32)
    narrow = onehot(
        (iota((256, 128), 0) // BLOCK == iota((256, 128), 1) // SIDE)
        & (iota((256, 128), 0) % BLOCK == iota((256, 128), 1) % SIDE)
    )
    for c in range(2):
        chosen = onehot(2.0 * table[:, 0:1] + c == as_number((256, 512), 1))
        slab = nn(chosen, blocks)
        parts = []
        for part in (slab[:, 0:128], slab[:, 128:256]):
            for bit in (16, 8, 4, 2, 1):
                part = jnp.where((depth & bit) != 0, pltpu.roll(part, 128 - bit, 1), part)
            parts.append(part)
        cut = jnp.concatenate(parts, axis=1).astype(jnp.bfloat16)
        gathered[:, 128 * c : 128 * c + 128] = nn(cut, narrow).astype(jnp.bfloat16)
    wait_for_all()
    copies = exchange(0, CHIPS, lambda other: gathered.at[rows_at(other, 16)], arrived.at[rows_at(place, 16)], send, recv)
    arrived[rows_at(place, 16)] = gathered[rows_at(place, 16)]
    for load in loads[4:]:
        load.wait()
    expand_first(conv_first, toeplitz_first)
    expand_second(conv_second, forward, backward)
    table = table.astype(jnp.bfloat16)
    row = iota((128, 1), 0)
    crop = row // 16 * 2 + row % 16 // 8
    about = nn(onehot(iota((128, 256), 1) == place * 16 + crop), table)
    x = jnp.floor((about[:, 1:2] - z.astype(jnp.float32) + 7.0) * 0.125) + (row % 8 // 4).astype(jnp.float32)
    wanted = (x * 4.0 + (row % 4).astype(jnp.float32)) * 16.0 + crop.astype(jnp.float32)
    chosen = onehot(wanted == as_number((128, 256), 1))
    finish(copies)
    leaving[...] = nn(chosen, arrived[...]).astype(jnp.bfloat16)
    copies = exchange(1, DEPTH, lambda other: leaving.at[rows_at(other, 16)], landed.at[rows_at(z, 16)], send, recv)
    landed[rows_at(z, 16)] = leaving[rows_at(z, 16)]
    gain = column(gain_ref)
    head = column(head_ref).astype(jnp.bfloat16).astype(jnp.float32)
    row = iota((128, 1), 0)
    s, p = row % 32 // 16, row % 16
    about = nn(onehot(iota((128, 256), 1) == place * 16 + z * 2 + s), table)
    x = about[:, 1:2] + p.astype(jnp.float32)
    wanted = (x - 8.0 * jnp.floor(x * 0.125)) * 16.0 + (s * 8 + p // 8 * 4 + row // 32).astype(jnp.float32)
    chosen = onehot((wanted == as_number((128, 128), 1)) & (p < CROP))
    lane = iota((1, PART), 1)
    for s in range(2):
        y = about[16 * s : 16 * s + 1, 2:3] + (lane % PITCH // CROP).astype(jnp.float32)
        spot = y * SIDE + (lane % PITCH % CROP).astype(jnp.float32)
        inside = in_crop() & (lane // PITCH == s)
        spots[s] = onehot(jnp.where(inside, spot, -1.0) == as_number((512, PART), 0))
    finish(copies)
    planes = nn(chosen, landed[...]).astype(jnp.bfloat16)
    window = jnp.zeros((32, PART), jnp.float32)
    for s in range(2):
        whole = jnp.concatenate(
            [
                jnp.concatenate([planes[32 * q + 16 * s : 32 * q + 16 * s + 16, 128 * c : 128 * c + 128] for q in range(4)], axis=1)
                for c in range(2)
            ],
            axis=0,
        )
        window = window + nn(whole, spots[s])
    packed[216:256, :] = jnp.zeros((40, 128), jnp.float32)
    finish_gradients = crop_gradients(
        window[0:16], window[16:28], gain, head, packed,
        toeplitz_first, forward, backward, patches, hidden, hidden_stack, second, logits, cotangent, cotangent_stack,
    )
    reduce_everywhere(
        packed, finish_gradients, out, small_out, first, second_sums, small_sums, small_first, small_second, send, recv
    )


SCRATCH = [
    pltpu.VMEM((256, 2, 256), jnp.bfloat16),
    pltpu.VMEM((1, 256), jnp.int32),
    pltpu.VMEM((MOST, 256), jnp.int32),
    pltpu.VMEM((MOST, 3, 256), jnp.int32),
    pltpu.VMEM((27, CH), jnp.float32),
    pltpu.VMEM((27, CH, CH), jnp.float32),
    pltpu.VMEM((1, CH), jnp.float32),
    pltpu.VMEM((1, CH), jnp.float32),
    pltpu.SemaphoreType.DMA((16,)),
    pltpu.VMEM((256, 256), jnp.bfloat16),
    pltpu.VMEM((256, 256), jnp.bfloat16),
    pltpu.VMEM((128, 256), jnp.bfloat16),
    pltpu.VMEM((128, 256), jnp.bfloat16),
    pltpu.VMEM((2, 512, PART), jnp.bfloat16),
    pltpu.VMEM((256, 128), jnp.float32),
    pltpu.VMEM((16, 16, 128), jnp.float32),
    pltpu.VMEM((16, 16, 128), jnp.float32),
    pltpu.VMEM((16, 128), jnp.float32),
    pltpu.VMEM((16, 16, 128), jnp.float32),
    pltpu.VMEM((16, 16, 128), jnp.float32),
    pltpu.SemaphoreType.DMA((7, 16)),
    pltpu.SemaphoreType.DMA((7, 16)),
]


def summed_gradients(pool, crop_ids, crop_corners, counts, conv_first, conv_second, norm_gain, head_weight, small, large):
    return pl.pallas_call(
        step_kernel,
        out_shape=[jax.ShapeDtypeStruct(shape, jnp.float32) for shape in ((256, 128), (16, 128), (6, 32, CH))]
        + [jax.ShapeDtypeStruct((27, CH, CH), jnp.float32)] * 2,
        in_specs=[pl.BlockSpec(memory_space=pltpu.HBM)] * 16,
        out_specs=[pl.BlockSpec(memory_space=pltpu.VMEM)] * 5,
        scratch_shapes=SCRATCH + COMPUTE_SCRATCH,
        compiler_params=pltpu.CompilerParams(
            collective_id=0, has_side_effects=True, vmem_limit_bytes=20 * 1024 * 1024
        ),
    )(*[
        pltpu.with_memory_space_constraint(value, pltpu.HBM)
        for value in (
            pool, counts.reshape(1, 256), crop_ids.T, crop_corners.transpose(1, 2, 0),
            conv_first, conv_second, norm_gain.reshape(1, CH), head_weight.reshape(1, CH),
            *[value.reshape(-1, CH) for value in small],
            *large,
        )
    ])


beta_first = 0.9
beta_second = 0.999


def adam_update(gradient, momentum, variance):
    next_momentum = beta_first * momentum + (1.0 - beta_first) * gradient
    next_variance = beta_second * variance + (1.0 - beta_second) * gradient * gradient
    return next_momentum / (jnp.sqrt(next_variance) + 1e-08), next_momentum


def adam_kernel(inverse_batch, total, small_total, small, moment, variance, *refs):
    updates, nexts = refs[0:4], refs[4:8]
    gradient = total[...] * inverse_batch
    small_gradient = small_total[...] * inverse_batch
    for dx in range(3):
        j = 2 - dx
        part = jnp.concatenate(
            [gradient[0:216, CH * j : CH * j + CH], gradient[72 * j : 72 * j + 72, 96:128]], axis=0
        ).reshape(9, CH, CH)
        taps = slice(9 * dx, 9 * dx + 9)
        updates[1][taps], nexts[1][taps] = adam_update(part, moment[taps], variance[taps])
        part = small_gradient[0:9, CH * dx : CH * dx + CH]
        updates[0][taps], nexts[0][taps] = adam_update(part, small[0, taps], small[3, taps])
    for k in (1, 2):
        part = small_gradient[k - 1 : k, 96:128]
        updates[k + 1][...], nexts[k + 1][...] = adam_update(part, small[k, 0:1], small[k + 3, 0:1])


def adam(batch_size, total, small_total, small, moment, variance):
    shapes = [jax.ShapeDtypeStruct(shape, jnp.float32) for shape in ((27, CH), (27, CH, CH), (1, CH), (1, CH))]
    results = pl.pallas_call(
        functools.partial(adam_kernel, 1.0 / batch_size),
        out_shape=shapes + shapes,
        in_specs=[pl.BlockSpec(memory_space=pltpu.VMEM)] * 5,
        out_specs=[pl.BlockSpec(memory_space=pltpu.VMEM)] * 8,
        compiler_params=pltpu.CompilerParams(vmem_limit_bytes=8 * 1024 * 1024),
    )(total, small_total, small, moment, variance)
    return tuple(value.reshape(CH) if value.shape == (1, CH) else value for value in results)


SHARE = 2


def shards(
    pool, crop_ids, crop_corners, counts, conv_first, conv_second, norm_gain, head_weight,
    momentum_first, momentum_second, momentum_gain, momentum_head,
    variance_first, variance_second, variance_gain, variance_head,
):
    moved_on = summed_gradients(
        pool, crop_ids, crop_corners, counts, conv_first, conv_second, norm_gain, head_weight,
        (momentum_first, momentum_gain, momentum_head, variance_first, variance_gain, variance_head),
        (momentum_second, variance_second),
    )
    return adam(counts.shape[0] * SHARE, *moved_on)


def solution(mesh):
    in_specs = (P(None, None, "dp"),) + (P(),) * 15
    return jax.shard_map(shards, mesh=mesh, in_specs=in_specs, out_specs=(P(),) * 8, check_vma=False)
```

```python
import functools

import jax
import jax.numpy as jnp
from jax import lax
from jax.experimental import pallas as pl
from jax.experimental.pallas import tpu as pltpu
from jax.sharding import PartitionSpec as P

CH = 32
CROP = 12
BLOCK = 32
MOST = 3


SIDE = 16
PLANE = CROP * CROP
PITCH = PLANE + 2 * CROP
PART = 384
LANES = 2 * PART
VOXELS = CROP * CROP * CROP
BAND = 6 * CH
TAPS = 9 * BAND


def iota(shape, axis):
    return lax.broadcasted_iota(jnp.int32, shape, axis)


def nt(a, b):
    return lax.dot_general(a, b, (((1,), (1,)), ((), ())), preferred_element_type=jnp.float32)


def nn(a, b):
    return jnp.dot(a, b, preferred_element_type=jnp.float32)


def onehot(condition):
    return jnp.where(condition, 1.0, 0.0).astype(jnp.bfloat16)


def in_crop():
    lane = iota((1, PART), 1)
    return (lane < 2 * PITCH) & (lane % PITCH < PLANE)


def edges(reach):
    z = iota((1, PART), 1) % PITCH % CROP
    return z < CROP - reach, None, z >= reach


def sources(value, masks):
    value = value.astype(jnp.bfloat16)
    return [value if mask is None else jnp.where(mask, value, jnp.zeros_like(value)) for mask in masks]


def moved(source, dy, dz):
    amount = (-(CROP * dy + dz)) % PART
    return (pltpu.roll(source, amount, 1) if amount else source).astype(jnp.bfloat16)


def by_crop(columns):
    return jnp.where(iota((1, PART), 1) < PITCH, columns[0], columns[1])


def crop_sums(value):
    lane = iota((1, PART), 1)
    value = jnp.where(in_crop(), value, 0.0)
    first = jnp.sum(jnp.where(lane < PITCH, value, 0.0), axis=1, keepdims=True)
    return first, jnp.sum(jnp.where(lane >= PITCH, value, 0.0), axis=1, keepdims=True)


def expand_first(conv_first, toeplitz_first):
    weights = conv_first[...].astype(jnp.bfloat16)
    repeat = onehot(iota((12 * CH, CH), 0) % CH == iota((12 * CH, CH), 1))
    row, column = iota((12 * CH, 144), 0), iota((12 * CH, 144), 1)
    place = row // CH
    step = column % 16 - (2 * (place % 6) + place // 6) + 1
    total = jnp.zeros((12 * CH, 144), jnp.float32)
    for dx in range(3):
        tap = onehot(iota((144, 27), 0) // 16 + 9 * dx == iota((144, 27), 1))
        spread = nn(tap, weights).astype(jnp.bfloat16)
        total = jnp.where(step == dx, nt(repeat, spread), total)
    toeplitz_first[...] = total.astype(jnp.bfloat16)


def expand_second(conv_second, forward, backward):
    eye = onehot(iota((CH, CH), 0) == iota((CH, CH), 1))
    zero = jnp.zeros((CH, 256 - 3 * CH), jnp.float32)
    plain, turned = [], []
    for tap in range(9):
        blocks = [conv_second[9 * dx + tap] for dx in range(3)]
        plain.append(jnp.concatenate([blocks[2], blocks[1], blocks[0], zero], axis=1))
        stacked = jnp.concatenate(blocks, axis=0).astype(jnp.bfloat16)
        turned.append(jnp.concatenate([nt(eye, stacked), zero], axis=1))
    for i in range(6):
        rows = slice(i * CH, i * CH + CH)
        amount = (CH * (i - 1)) % 256
        for strips, matrix in ((plain, backward), (turned, forward)):
            bands = [(pltpu.roll(strip, amount, 1) if amount else strip)[:, 0:BAND] for strip in strips]
            matrix[rows, :] = jnp.concatenate(bands, axis=1).astype(jnp.bfloat16)


def crop_gradients(
    image, target, gain, head, packed,
    toeplitz_first, forward, backward, patches, hidden, hidden_stack, second, logits, cotangent, cotangent_stack,
):
    halves = (slice(0, PART), slice(PART, LANES))
    places = [(parity, i) for parity in range(2) for i in range(6)]
    steps = [(tap // 3 - 1, tap % 3 - 1) for tap in range(9)]
    valid = in_crop()
    image = sources(image, edges(1))
    for tap, (dy, dz) in enumerate(steps):
        patches[tap * 16 : tap * 16 + 16, :] = moved(image[dz + 1], dy, dz)
    masks = edges(2)
    for parity, half in enumerate(halves):
        first_map = nn(toeplitz_first[parity * BAND : parity * BAND + BAND, :], patches[...])
        value = jnp.where(valid, jnp.maximum(first_map, 0.0), 0.0)
        hidden[:, half] = value.astype(jnp.bfloat16)
        value = sources(value, masks)
        for tap, (dy, dz) in enumerate(steps):
            hidden_stack[tap * BAND : tap * BAND + BAND, half] = moved(value[dz + 1], 2 * dy, 2 * dz)
    second[...] = nn(forward[...], hidden_stack[...])
    scale = 1.0 / VOXELS
    total = jnp.zeros((CH, PART), jnp.float32)
    for parity, i in places:
        total = total + second[i * CH : i * CH + CH, halves[parity]]
    center = by_crop([value * scale for value in crop_sums(total)])
    total = jnp.zeros((CH, PART), jnp.float32)
    for parity, i in places:
        away = second[i * CH : i * CH + CH, halves[parity]] - center
        total = total + away * away
    inverse = by_crop([lax.rsqrt(value * scale + 1e-05) for value in crop_sums(total)])
    for parity, i in places:
        rows, half, plane = slice(i * CH, i * CH + CH), halves[parity], 2 * i + parity
        hat = (second[rows, half] - center) * inverse
        second[rows, half] = hat
        joined = (jnp.maximum(hat * gain, 0.0) + hidden[rows, half].astype(jnp.float32)).astype(jnp.bfloat16)
        logits[plane : plane + 1, :] = jnp.sum(joined.astype(jnp.float32) * head, axis=0, keepdims=True)
    slope = 1.0 / (1.0 + jnp.exp(-logits[0:12, :])) - target
    logits[0:12, :] = jnp.where(valid, slope * scale, 0.0)
    sum_plain = jnp.zeros((CH, PART), jnp.float32)
    sum_hat = jnp.zeros((CH, PART), jnp.float32)
    sum_head = jnp.zeros((CH, PART), jnp.float32)
    for parity, i in places:
        rows, half, plane = slice(i * CH, i * CH + CH), halves[parity], 2 * i + parity
        hat = second[rows, half]
        normed = hat * gain
        slope = logits[plane : plane + 1, :]
        joined = (jnp.maximum(normed, 0.0) + hidden[rows, half].astype(jnp.float32)).astype(jnp.bfloat16)
        sum_head = sum_head + joined.astype(jnp.float32) * slope
        passed = jnp.where(normed > 0.0, slope, 0.0)
        sum_plain = sum_plain + passed
        sum_hat = sum_hat + passed * hat
    grad_head = sum(crop_sums(sum_head))
    sums_plain = [head * value for value in crop_sums(sum_plain)]
    sums_hat = [head * value for value in crop_sums(sum_hat)]
    grad_gain = sum(sums_hat)
    mean_plain = by_crop([value * scale for value in sums_plain])
    mean_hat = by_crop([value * scale for value in sums_hat])
    factor = jnp.where(valid, inverse * gain, 0.0)
    for parity, i in places:
        rows, half, plane = slice(i * CH, i * CH + CH), halves[parity], 2 * i + parity
        hat = second[rows, half]
        slope = logits[plane : plane + 1, :]
        passed = jnp.where(hat * gain > 0.0, head * slope, 0.0)
        value = factor * (passed - mean_plain - hat * mean_hat)
        cotangent[rows, half] = value.astype(jnp.bfloat16)
        value = sources(value, masks)
        for tap, (dy, dz) in enumerate(steps):
            place = tap * BAND + i * CH
            cotangent_stack[place : place + CH, half] = moved(value[1 - dz], -2 * dy, -2 * dz)
    cotangent[BAND:256, :] = jnp.zeros((256 - BAND, LANES), jnp.bfloat16)
    turned = cotangent[...].T
    lane = iota((CH, 128), 1)
    for tap in range(9):
        products = nn(hidden_stack[tap * BAND : tap * BAND + BAND, :], turned)
        low, high = products[:, 0:128], products[:, 128:256]
        band = [slice(i * CH, i * CH + CH) for i in range(6)]
        total = low[band[1]] + high[band[5]] + jnp.where(lane >= CH, pltpu.roll(low[band[0]], CH, 1), 0.0)
        total = total + pltpu.roll(low[band[2]], 96, 1)
        for i, amount in ((3, 64), (4, 32)):
            total = total + pltpu.roll(jnp.where(lane < 128 - amount, high[band[i]], low[band[i]]), amount, 1)
        at = tap * CH
        if at < 216:
            count = min(CH, 216 - at)
            packed[at : at + count, :] = jnp.where(lane < 96, total, 0.0)[0:count]
        if at + CH > 216:
            skip = max(0, 216 - at)
            for j in range(3):
                shifted = pltpu.roll(total, 96 - CH * j, 1)
                shifted = jnp.where(lane >= 96, shifted, 0.0)[skip:CH]
                to = 72 * j + at + skip - 216
                packed[to : to + CH - skip, :] = packed[to : to + CH - skip, :] + shifted
    return lambda small: first_gradients(
        small, gain, head, grad_gain, grad_head,
        backward, patches, hidden, second, logits, cotangent_stack,
    )


def first_gradients(
    small_sums, gain, head, grad_gain, grad_head, backward, patches, hidden, second, logits, cotangent_stack,
):
    halves = (slice(0, PART), slice(PART, LANES))
    places = [(parity, i) for parity in range(2) for i in range(6)]
    back = nn(backward[...], cotangent_stack[...])
    for parity, i in places:
        rows, half, plane = slice(i * CH, i * CH + CH), halves[parity], 2 * i + parity
        whole = back[rows, half] + head * logits[plane : plane + 1, :]
        alive = hidden[rows, half].astype(jnp.float32) > 0.0
        second[rows, half] = jnp.where(alive, whole, 0.0)
    lane = iota((9, 128), 1)
    small = jnp.zeros((9, 128), jnp.float32)
    products = jnp.concatenate([nt(patches[...], second[:, half].astype(jnp.bfloat16)) for half in halves], axis=1)
    row, column = iota((144, 2 * BAND), 0), iota((144, 2 * BAND), 1)
    place = column // CH
    step = row % 16 - (2 * (place % 6) + place // 6) + 1
    for dx in range(3):
        part = jnp.where(step == dx, products, 0.0)
        part = jnp.sum(part.reshape(9, 16, 2 * BAND), axis=1)
        part = part[:, 0:128] + part[:, 128:256] + part[:, 256:384]
        part = part + pltpu.roll(part, 64, 1)
        part = part + pltpu.roll(part, 32, 1)
        small = jnp.where(lane // CH == dx, part, small)
    pick = iota((CH, 128), 0) + 96 == iota((CH, 128), 1)
    small = small + jnp.concatenate(
        [jnp.sum(jnp.where(pick, value, 0.0), axis=0, keepdims=True) for value in (grad_gain, grad_head)]
        + [jnp.where(lane[0:1] >= 96, pltpu.roll(small[8:9], 96 - CH * dx, 1), 0.0) for dx in range(3)]
        + [jnp.zeros((4, 128), jnp.float32)],
        axis=0,
    )
    small_sums[...] = small[0:8]


COMPUTE_SCRATCH = [
    pltpu.VMEM((12 * CH, 144), jnp.bfloat16),
    pltpu.VMEM((BAND, TAPS), jnp.bfloat16),
    pltpu.VMEM((BAND, TAPS), jnp.bfloat16),
    pltpu.VMEM((144, PART), jnp.bfloat16),
    pltpu.VMEM((BAND, LANES), jnp.bfloat16),
    pltpu.VMEM((TAPS, LANES), jnp.bfloat16),
    pltpu.VMEM((BAND, LANES), jnp.float32),
    pltpu.VMEM((16, PART), jnp.float32),
    pltpu.VMEM((256, LANES), jnp.bfloat16),
    pltpu.VMEM((TAPS, LANES), jnp.bfloat16),
]


MESH = pl.DeviceIdType.MESH


def plane_peer(k):
    dp = lax.axis_index("dp")
    x = lax.rem(dp // 32 + k // 4, 4)
    y = lax.rem(lax.rem(dp, 4) + k % 4, 4)
    z = lax.rem(dp // 4, 8)
    return (x * 32 + z * 4 + y, lax.axis_index("pair")), x * 4 + y


def z_peer(k):
    dp = lax.axis_index("dp")
    z = lax.rem(lax.rem(dp // 4, 8) + k, 8)
    return ((dp // 32) * 32 + z * 4 + lax.rem(dp, 4), lax.axis_index("pair")), z


def column_peer(k):
    (dp, _), z = z_peer(k // 2)
    core = lax.rem(lax.axis_index("pair") + k % 2, 2)
    return (dp, core), z * 2 + core


PLANE_STEPS = (10, 6, 9, 11, 14, 2, 5, 7, 8, 13, 15, 1, 3, 4, 12)
Z_STEPS = (4, 3, 5, 2, 6, 1, 7)
COLUMN_STEPS = (9, 8, 7, 6, 11, 10, 5, 4, 13, 12, 3, 2, 15, 14, 1)
CHIPS, DEPTH, COLUMN = (plane_peer, PLANE_STEPS), (z_peer, Z_STEPS), (column_peer, COLUMN_STEPS)
GROUPS = (CHIPS, COLUMN)


def rows_at(place, count):
    return pl.ds(pl.multiple_of(place * count, count), count)


def greet():
    barrier = pltpu.get_barrier_semaphore()
    for peer, steps in GROUPS:
        for k in steps:
            pl.semaphore_signal(barrier, inc=1, device_id=peer(k)[0], device_id_type=MESH)
    return lambda: pl.semaphore_wait(barrier, sum(len(steps) for _, steps in GROUPS))


def exchange(stage, group, source, target, send, recv):
    peer, steps = group
    copies = []
    for k in steps:
        device, place = peer(k)
        copy = pltpu.make_async_remote_copy(
            src_ref=source(place), dst_ref=target, send_sem=send.at[stage, k], recv_sem=recv.at[stage, k],
            device_id=device, device_id_type=MESH,
        )
        copy.start()
        copies.append(copy)
    return copies


def finish(copies):
    for copy in copies:
        copy.wait()


def added(slots):
    total = slots[0].astype(jnp.float32)
    for k in range(1, 16):
        total = total + slots[k].astype(jnp.float32)
    return total


def reduce_everywhere(packed, finish_gradients, out, first, second, small, send, recv):
    _, place = plane_peer(0)
    _, column = column_peer(0)
    copies = exchange(2, CHIPS, lambda other: packed.at[rows_at(other, 16)], first.at[place], send, recv)
    first[place] = packed[rows_at(place, 16)]
    finish_gradients(small)
    second[column, 16:32] = jnp.concatenate([small[...], jnp.zeros((8, 128), jnp.float32)], axis=0).astype(jnp.bfloat16)
    finish(copies)
    second[column, 0:16] = added(first).astype(jnp.bfloat16)
    copies = exchange(3, COLUMN, lambda other: second.at[column], second.at[column], send, recv)
    finish(copies)
    out[place] = added(second)[0:24]
    copies = exchange(4, CHIPS, lambda other: out.at[place], out.at[place], send, recv)
    finish(copies)


def crop_table(counts, ids, corners):
    shape = (256, 256)
    count = counts[...].astype(jnp.float32)
    before = onehot(iota(shape, 0) < iota(shape, 1))
    starts = nn(count.astype(jnp.bfloat16), before)
    number = (iota(shape, 0) + 256 * lax.axis_index("pair")).astype(jnp.float32)
    total = jnp.zeros((256, 4), jnp.float32)
    for s in range(MOST):
        chosen = onehot((number == starts + s) & (count > s))
        table = jnp.concatenate([ids[s : s + 1, :], corners[s]], axis=0)
        total = total + nt(chosen, table.astype(jnp.bfloat16))
    return total


def as_number(condition_shape, axis):
    return iota(condition_shape, axis).astype(jnp.float32)


def column(ref):
    eye = iota((CH, CH), 0) == iota((CH, CH), 1)
    return jnp.sum(jnp.where(eye, ref[...], 0.0), axis=1, keepdims=True)


def step_kernel(
    pool_at, counts_at, ids_at, corners_at, conv_first_at, conv_second_at, gain_at, head_at, *refs
):
    small_at, moments_at, (out, small, *moments), refs = refs[0:6], refs[6:8], refs[8:12], refs[12:]
    (
    pool, counts, ids, corners, conv_first, conv_second, gain_ref, head_ref, loaded,
    gathered, arrived, leaving, landed, spots, packed, first, second_sums, small_sums, send, recv,
    toeplitz_first, forward, backward, patches, hidden, hidden_stack, second, logits, cotangent, cotangent_stack,
    ) = refs
    wait_for_all = greet()
    pairs = (
        (counts_at, counts), (ids_at, ids), (corners_at, corners), (pool_at, pool),
        (conv_first_at, conv_first), (conv_second_at, conv_second), (gain_at, gain_ref), (head_at, head_ref),
    ) + tuple((source, small.at[k, 0 : source.shape[0]]) for k, source in enumerate(small_at)) + tuple(zip(moments_at, moments))
    loads = [pltpu.make_async_copy(*pair, loaded.at[k]) for k, pair in enumerate(pairs)]
    for load in loads:
        load.start()
    _, place = plane_peer(0)
    _, z = z_peer(0)
    for load in loads[0:3]:
        load.wait()
    table = crop_table(counts, ids, corners)
    loads[3].wait()
    blocks = pool[...].reshape(512, 256)
    depth = table[:, 3:4].astype(jnp.int32)
    narrow = onehot(
        (iota((256, 128), 0) // BLOCK == iota((256, 128), 1) // SIDE)
        & (iota((256, 128), 0) % BLOCK == iota((256, 128), 1) % SIDE)
    )
    for c in range(2):
        chosen = onehot(2.0 * table[:, 0:1] + c == as_number((256, 512), 1))
        slab = nn(chosen, blocks)
        parts = []
        for part in (slab[:, 0:128], slab[:, 128:256]):
            for bit in (16, 8, 4, 2, 1):
                part = jnp.where((depth & bit) != 0, pltpu.roll(part, 128 - bit, 1), part)
            parts.append(part)
        cut = jnp.concatenate(parts, axis=1).astype(jnp.bfloat16)
        gathered[:, 128 * c : 128 * c + 128] = nn(cut, narrow).astype(jnp.bfloat16)
    wait_for_all()
    copies = exchange(0, CHIPS, lambda other: gathered.at[rows_at(other, 16)], arrived.at[rows_at(place, 16)], send, recv)
    arrived[rows_at(place, 16)] = gathered[rows_at(place, 16)]
    for load in loads[4:]:
        load.wait()
    expand_first(conv_first, toeplitz_first)
    expand_second(conv_second, forward, backward)
    table = table.astype(jnp.bfloat16)
    row = iota((128, 1), 0)
    crop = row // 16 * 2 + row % 16 // 8
    about = nn(onehot(iota((128, 256), 1) == place * 16 + crop), table)
    x = jnp.floor((about[:, 1:2] - z.astype(jnp.float32) + 7.0) * 0.125) + (row % 8 // 4).astype(jnp.float32)
    wanted = (x * 4.0 + (row % 4).astype(jnp.float32)) * 16.0 + crop.astype(jnp.float32)
    chosen = onehot(wanted == as_number((128, 256), 1))
    finish(copies)
    leaving[...] = nn(chosen, arrived[...]).astype(jnp.bfloat16)
    copies = exchange(1, DEPTH, lambda other: leaving.at[rows_at(other, 16)], landed.at[rows_at(z, 16)], send, recv)
    landed[rows_at(z, 16)] = leaving[rows_at(z, 16)]
    gain = column(gain_ref)
    head = column(head_ref).astype(jnp.bfloat16).astype(jnp.float32)
    row = iota((128, 1), 0)
    s, p = row % 32 // 16, row % 16
    about = nn(onehot(iota((128, 256), 1) == place * 16 + z * 2 + s), table)
    x = about[:, 1:2] + p.astype(jnp.float32)
    wanted = (x - 8.0 * jnp.floor(x * 0.125)) * 16.0 + (s * 8 + p // 8 * 4 + row // 32).astype(jnp.float32)
    chosen = onehot((wanted == as_number((128, 128), 1)) & (p < CROP))
    lane = iota((1, PART), 1)
    for s in range(2):
        y = about[16 * s : 16 * s + 1, 2:3] + (lane % PITCH // CROP).astype(jnp.float32)
        spot = y * SIDE + (lane % PITCH % CROP).astype(jnp.float32)
        inside = in_crop() & (lane // PITCH == s)
        spots[s] = onehot(jnp.where(inside, spot, -1.0) == as_number((512, PART), 0))
    finish(copies)
    planes = nn(chosen, landed[...]).astype(jnp.bfloat16)
    window = jnp.zeros((32, PART), jnp.float32)
    for s in range(2):
        whole = jnp.concatenate(
            [
                jnp.concatenate([planes[32 * q + 16 * s : 32 * q + 16 * s + 16, 128 * c : 128 * c + 128] for q in range(4)], axis=1)
                for c in range(2)
            ],
            axis=0,
        )
        window = window + nn(whole, spots[s])
    packed[216:256, :] = jnp.zeros((40, 128), jnp.float32)
    finish_gradients = crop_gradients(
        window[0:16], window[16:28], gain, head, packed,
        toeplitz_first, forward, backward, patches, hidden, hidden_stack, second, logits, cotangent, cotangent_stack,
    )
    reduce_everywhere(
        packed, finish_gradients, out, first, second_sums, small_sums, send, recv
    )


SCRATCH = [
    pltpu.VMEM((256, 2, 256), jnp.bfloat16),
    pltpu.VMEM((1, 256), jnp.int32),
    pltpu.VMEM((MOST, 256), jnp.int32),
    pltpu.VMEM((MOST, 3, 256), jnp.int32),
    pltpu.VMEM((27, CH), jnp.float32),
    pltpu.VMEM((27, CH, CH), jnp.float32),
    pltpu.VMEM((1, CH), jnp.float32),
    pltpu.VMEM((1, CH), jnp.float32),
    pltpu.SemaphoreType.DMA((16,)),
    pltpu.VMEM((256, 256), jnp.bfloat16),
    pltpu.VMEM((256, 256), jnp.bfloat16),
    pltpu.VMEM((128, 256), jnp.bfloat16),
    pltpu.VMEM((128, 256), jnp.bfloat16),
    pltpu.VMEM((2, 512, PART), jnp.bfloat16),
    pltpu.VMEM((256, 128), jnp.float32),
    pltpu.VMEM((16, 16, 128), jnp.float32),
    pltpu.VMEM((16, 32, 128), jnp.bfloat16),
    pltpu.VMEM((8, 128), jnp.float32),
    pltpu.SemaphoreType.DMA((5, 16)),
    pltpu.SemaphoreType.DMA((5, 16)),
]


def summed_gradients(pool, crop_ids, crop_corners, counts, conv_first, conv_second, norm_gain, head_weight, small, large):
    return pl.pallas_call(
        step_kernel,
        out_shape=[jax.ShapeDtypeStruct(shape, jnp.float32) for shape in ((16, 24, 128), (6, 32, CH))]
        + [jax.ShapeDtypeStruct((27, CH, CH), jnp.float32)] * 2,
        in_specs=[pl.BlockSpec(memory_space=pltpu.HBM)] * 16,
        out_specs=[pl.BlockSpec(memory_space=pltpu.VMEM)] * 4,
        scratch_shapes=SCRATCH + COMPUTE_SCRATCH,
        compiler_params=pltpu.CompilerParams(
            collective_id=0, has_side_effects=True, vmem_limit_bytes=20 * 1024 * 1024
        ),
    )(*[
        pltpu.with_memory_space_constraint(value, pltpu.HBM)
        for value in (
            pool, counts.reshape(1, 256), crop_ids.T, crop_corners.transpose(1, 2, 0),
            conv_first, conv_second, norm_gain.reshape(1, CH), head_weight.reshape(1, CH),
            *[value.reshape(-1, CH) for value in small],
            *large,
        )
    ])


beta_first = 0.9
beta_second = 0.999


def adam_update(gradient, momentum, variance):
    next_momentum = beta_first * momentum + (1.0 - beta_first) * gradient
    next_variance = beta_second * variance + (1.0 - beta_second) * gradient * gradient
    return next_momentum / (jnp.sqrt(next_variance) + 1e-08), next_momentum


def adam_kernel(inverse_batch, total, small, moment, variance, *refs):
    updates, nexts = refs[0:4], refs[4:8]
    gradient = total[:, 0:16].reshape(256, 128) * inverse_batch
    small_gradient = added(total[:, 16:24]) * inverse_batch
    for dx in range(3):
        j = 2 - dx
        part = jnp.concatenate(
            [gradient[0:216, CH * j : CH * j + CH], gradient[72 * j : 72 * j + 72, 96:128]], axis=0
        ).reshape(9, CH, CH)
        taps = slice(9 * dx, 9 * dx + 9)
        updates[1][taps], nexts[1][taps] = adam_update(part, moment[taps], variance[taps])
        part = jnp.concatenate([small_gradient[:, CH * dx : CH * dx + CH], small_gradient[2 + dx : 3 + dx, 96:128]], axis=0)
        updates[0][taps], nexts[0][taps] = adam_update(part, small[0, taps], small[3, taps])
    for k in (1, 2):
        part = small_gradient[k - 1 : k, 96:128]
        updates[k + 1][...], nexts[k + 1][...] = adam_update(part, small[k, 0:1], small[k + 3, 0:1])


def adam(batch_size, total, small, moment, variance):
    shapes = [jax.ShapeDtypeStruct(shape, jnp.float32) for shape in ((27, CH), (27, CH, CH), (1, CH), (1, CH))]
    results = pl.pallas_call(
        functools.partial(adam_kernel, 1.0 / batch_size),
        out_shape=shapes + shapes,
        in_specs=[pl.BlockSpec(memory_space=pltpu.VMEM)] * 4,
        out_specs=[pl.BlockSpec(memory_space=pltpu.VMEM)] * 8,
        compiler_params=pltpu.CompilerParams(vmem_limit_bytes=8 * 1024 * 1024),
    )(total, small, moment, variance)
    return tuple(value.reshape(CH) if value.shape == (1, CH) else value for value in results)


SHARE = 2


def shards(
    pool, crop_ids, crop_corners, counts, conv_first, conv_second, norm_gain, head_weight,
    momentum_first, momentum_second, momentum_gain, momentum_head,
    variance_first, variance_second, variance_gain, variance_head,
):
    moved_on = summed_gradients(
        pool, crop_ids, crop_corners, counts, conv_first, conv_second, norm_gain, head_weight,
        (momentum_first, momentum_gain, momentum_head, variance_first, variance_gain, variance_head),
        (momentum_second, variance_second),
    )
    return adam(counts.shape[0] * SHARE, *moved_on)


def solution(mesh):
    in_specs = (P(None, None, "dp"),) + (P(),) * 15
    return jax.shard_map(shards, mesh=mesh, in_specs=in_specs, out_specs=(P(),) * 8, check_vma=False)
```

```python
import functools

import jax
import jax.numpy as jnp
from jax import lax
from jax.experimental import pallas as pl
from jax.experimental.pallas import tpu as pltpu
from jax.sharding import PartitionSpec as P

CH = 32
CROP = 12
BLOCK = 32
MOST = 3


SIDE = 16
PLANE = CROP * CROP
PITCH = PLANE + 2 * CROP
PART = 384
LANES = 2 * PART
VOXELS = CROP * CROP * CROP
BAND = 6 * CH
TAPS = 9 * BAND


def iota(shape, axis):
    return lax.broadcasted_iota(jnp.int32, shape, axis)


def nt(a, b):
    return lax.dot_general(a, b, (((1,), (1,)), ((), ())), preferred_element_type=jnp.float32)


def nn(a, b):
    return jnp.dot(a, b, preferred_element_type=jnp.float32)


def onehot(condition):
    return jnp.where(condition, 1.0, 0.0).astype(jnp.bfloat16)


def in_crop():
    lane = iota((1, PART), 1)
    return (lane < 2 * PITCH) & (lane % PITCH < PLANE)


def edges(reach):
    z = iota((1, PART), 1) % PITCH % CROP
    return z < CROP - reach, None, z >= reach


def sources(value, masks):
    value = value.astype(jnp.bfloat16)
    return [value if mask is None else jnp.where(mask, value, jnp.zeros_like(value)) for mask in masks]


def moved(source, dy, dz):
    amount = (-(CROP * dy + dz)) % PART
    return (pltpu.roll(source, amount, 1) if amount else source).astype(jnp.bfloat16)


def by_crop(columns):
    return jnp.where(iota((1, PART), 1) < PITCH, columns[0], columns[1])


def crop_sums(value):
    lane = iota((1, PART), 1)
    value = jnp.where(in_crop(), value, 0.0)
    first = jnp.sum(jnp.where(lane < PITCH, value, 0.0), axis=1, keepdims=True)
    return first, jnp.sum(jnp.where(lane >= PITCH, value, 0.0), axis=1, keepdims=True)


def expand_first(conv_first, toeplitz_first):
    weights = conv_first[...].astype(jnp.bfloat16)
    repeat = onehot(iota((12 * CH, CH), 0) % CH == iota((12 * CH, CH), 1))
    row, column = iota((12 * CH, 144), 0), iota((12 * CH, 144), 1)
    place = row // CH
    step = column % 16 - (2 * (place % 6) + place // 6) + 1
    total = jnp.zeros((12 * CH, 144), jnp.float32)
    for dx in range(3):
        tap = onehot(iota((144, 27), 0) // 16 + 9 * dx == iota((144, 27), 1))
        spread = nn(tap, weights).astype(jnp.bfloat16)
        total = jnp.where(step == dx, nt(repeat, spread), total)
    toeplitz_first[...] = total.astype(jnp.bfloat16)


def expand_second(conv_second, forward, backward):
    eye = onehot(iota((CH, CH), 0) == iota((CH, CH), 1))
    zero = jnp.zeros((CH, 256 - 3 * CH), jnp.float32)
    plain, turned = [], []
    for tap in range(9):
        blocks = [conv_second[9 * dx + tap] for dx in range(3)]
        plain.append(jnp.concatenate([blocks[2], blocks[1], blocks[0], zero], axis=1))
        stacked = jnp.concatenate(blocks, axis=0).astype(jnp.bfloat16)
        turned.append(jnp.concatenate([nt(eye, stacked), zero], axis=1))
    for i in range(6):
        rows = slice(i * CH, i * CH + CH)
        amount = (CH * (i - 1)) % 256
        for strips, matrix in ((plain, backward), (turned, forward)):
            bands = [(pltpu.roll(strip, amount, 1) if amount else strip)[:, 0:BAND] for strip in strips]
            matrix[rows, :] = jnp.concatenate(bands, axis=1).astype(jnp.bfloat16)


def crop_gradients(
    image, target, gain, head, packed,
    toeplitz_first, forward, backward, patches, hidden, hidden_stack, second, logits, cotangent, cotangent_stack,
):
    halves = (slice(0, PART), slice(PART, LANES))
    places = [(parity, i) for parity in range(2) for i in range(6)]
    steps = [(tap // 3 - 1, tap % 3 - 1) for tap in range(9)]
    valid = in_crop()
    image = sources(image, edges(1))
    for tap, (dy, dz) in enumerate(steps):
        patches[tap * 16 : tap * 16 + 16, :] = moved(image[dz + 1], dy, dz)
    masks = edges(2)
    for parity, half in enumerate(halves):
        first_map = nn(toeplitz_first[parity * BAND : parity * BAND + BAND, :], patches[...])
        value = jnp.where(valid, jnp.maximum(first_map, 0.0), 0.0)
        hidden[:, half] = value.astype(jnp.bfloat16)
        value = sources(value, masks)
        for tap, (dy, dz) in enumerate(steps):
            hidden_stack[tap * BAND : tap * BAND + BAND, half] = moved(value[dz + 1], 2 * dy, 2 * dz)
    second[...] = nn(forward[...], hidden_stack[...])
    scale = 1.0 / VOXELS
    total = jnp.zeros((CH, PART), jnp.float32)
    for parity, i in places:
        total = total + second[i * CH : i * CH + CH, halves[parity]]
    center = by_crop([value * scale for value in crop_sums(total)])
    total = jnp.zeros((CH, PART), jnp.float32)
    for parity, i in places:
        away = second[i * CH : i * CH + CH, halves[parity]] - center
        total = total + away * away
    inverse = by_crop([lax.rsqrt(value * scale + 1e-05) for value in crop_sums(total)])
    for parity, i in places:
        rows, half, plane = slice(i * CH, i * CH + CH), halves[parity], 2 * i + parity
        hat = (second[rows, half] - center) * inverse
        second[rows, half] = hat
        joined = (jnp.maximum(hat * gain, 0.0) + hidden[rows, half].astype(jnp.float32)).astype(jnp.bfloat16)
        logits[plane : plane + 1, :] = jnp.sum(joined.astype(jnp.float32) * head, axis=0, keepdims=True)
    slope = 1.0 / (1.0 + jnp.exp(-logits[0:12, :])) - target
    logits[0:12, :] = jnp.where(valid, slope * scale, 0.0)
    sum_plain = jnp.zeros((CH, PART), jnp.float32)
    sum_hat = jnp.zeros((CH, PART), jnp.float32)
    for parity, i in places:
        rows, half, plane = slice(i * CH, i * CH + CH), halves[parity], 2 * i + parity
        hat = second[rows, half]
        normed = hat * gain
        slope = logits[plane : plane + 1, :]
        passed = jnp.where(normed > 0.0, slope, 0.0)
        sum_plain = sum_plain + passed
        sum_hat = sum_hat + passed * hat
    sums_plain = [head * value for value in crop_sums(sum_plain)]
    sums_hat = [head * value for value in crop_sums(sum_hat)]
    grad_gain = sum(sums_hat)
    mean_plain = by_crop([value * scale for value in sums_plain])
    mean_hat = by_crop([value * scale for value in sums_hat])
    factor = jnp.where(valid, inverse * gain, 0.0)
    for parity, i in places:
        rows, half, plane = slice(i * CH, i * CH + CH), halves[parity], 2 * i + parity
        hat = second[rows, half]
        slope = logits[plane : plane + 1, :]
        passed = jnp.where(hat * gain > 0.0, head * slope, 0.0)
        cotangent[rows, half] = (factor * (passed - mean_plain - hat * mean_hat)).astype(jnp.bfloat16)
    cotangent[BAND:256, :] = jnp.zeros((256 - BAND, LANES), jnp.bfloat16)
    turned = cotangent[...].T
    lane = iota((CH, 128), 1)
    for tap in range(9):
        if tap % 3 == 0:
            three = nn(hidden_stack[tap * BAND : tap * BAND + 3 * BAND, :], turned)
        products = three[tap % 3 * BAND : tap % 3 * BAND + BAND]
        low, high = products[:, 0:128], products[:, 128:256]
        band = [slice(i * CH, i * CH + CH) for i in range(6)]
        total = low[band[1]] + high[band[5]] + jnp.where(lane >= CH, pltpu.roll(low[band[0]], CH, 1), 0.0)
        total = total + pltpu.roll(low[band[2]], 96, 1)
        for i, amount in ((3, 64), (4, 32)):
            total = total + pltpu.roll(jnp.where(lane < 128 - amount, high[band[i]], low[band[i]]), amount, 1)
        at = tap * CH
        if at < 216:
            count = min(CH, 216 - at)
            packed[at : at + count, :] = jnp.where(lane < 96, total, 0.0)[0:count]
        if at + CH > 216:
            skip = max(0, 216 - at)
            for j in range(3):
                shifted = pltpu.roll(total, 96 - CH * j, 1)
                shifted = jnp.where(lane >= 96, shifted, 0.0)[skip:CH]
                to = 72 * j + at + skip - 216
                packed[to : to + CH - skip, :] = packed[to : to + CH - skip, :] + shifted
    return lambda small: first_gradients(
        small, gain, head, grad_gain, backward, patches, hidden, second, logits, cotangent, cotangent_stack,
    )


def first_gradients(
    small_sums, gain, head, grad_gain, backward, patches, hidden, second, logits, cotangent, cotangent_stack,
):
    halves = (slice(0, PART), slice(PART, LANES))
    places = [(parity, i) for parity in range(2) for i in range(6)]
    masks = edges(2)
    for half in halves:
        value = sources(cotangent[0:BAND, half], masks)
        for tap in range(9):
            dy, dz = tap // 3 - 1, tap % 3 - 1
            cotangent_stack[tap * BAND : tap * BAND + BAND, half] = moved(value[1 - dz], -2 * dy, -2 * dz)
    back = nn(backward[...], cotangent_stack[...])
    sum_head = jnp.zeros((CH, PART), jnp.float32)
    for parity, i in places:
        rows, half, plane = slice(i * CH, i * CH + CH), halves[parity], 2 * i + parity
        slope = logits[plane : plane + 1, :]
        normed = second[rows, half] * gain
        joined = (jnp.maximum(normed, 0.0) + hidden[rows, half].astype(jnp.float32)).astype(jnp.bfloat16)
        sum_head = sum_head + joined.astype(jnp.float32) * slope
        whole = back[rows, half] + head * slope
        alive = hidden[rows, half].astype(jnp.float32) > 0.0
        second[rows, half] = jnp.where(alive, whole, 0.0)
    grad_head = sum(crop_sums(sum_head))
    lane = iota((9, 128), 1)
    small = jnp.zeros((9, 128), jnp.float32)
    products = jnp.concatenate([nt(patches[...], second[:, half].astype(jnp.bfloat16)) for half in halves], axis=1)
    row, column = iota((144, 2 * BAND), 0), iota((144, 2 * BAND), 1)
    place = column // CH
    step = row % 16 - (2 * (place % 6) + place // 6) + 1
    for dx in range(3):
        part = jnp.where(step == dx, products, 0.0)
        part = jnp.sum(part.reshape(9, 16, 2 * BAND), axis=1)
        part = part[:, 0:128] + part[:, 128:256] + part[:, 256:384]
        part = part + pltpu.roll(part, 64, 1)
        part = part + pltpu.roll(part, 32, 1)
        small = jnp.where(lane // CH == dx, part, small)
    pick = iota((CH, 128), 0) + 96 == iota((CH, 128), 1)
    small = small + jnp.concatenate(
        [jnp.sum(jnp.where(pick, value, 0.0), axis=0, keepdims=True) for value in (grad_gain, grad_head)]
        + [jnp.where(lane[0:1] >= 96, pltpu.roll(small[8:9], 96 - CH * dx, 1), 0.0) for dx in range(3)]
        + [jnp.zeros((4, 128), jnp.float32)],
        axis=0,
    )
    small_sums[...] = small[0:8]


COMPUTE_SCRATCH = [
    pltpu.VMEM((12 * CH, 144), jnp.bfloat16),
    pltpu.VMEM((BAND, TAPS), jnp.bfloat16),
    pltpu.VMEM((BAND, TAPS), jnp.bfloat16),
    pltpu.VMEM((144, PART), jnp.bfloat16),
    pltpu.VMEM((BAND, LANES), jnp.bfloat16),
    pltpu.VMEM((TAPS, LANES), jnp.bfloat16),
    pltpu.VMEM((BAND, LANES), jnp.float32),
    pltpu.VMEM((16, PART), jnp.float32),
    pltpu.VMEM((256, LANES), jnp.bfloat16),
    pltpu.VMEM((TAPS, LANES), jnp.bfloat16),
]


MESH = pl.DeviceIdType.MESH


def plane_peer(k):
    dp = lax.axis_index("dp")
    x = lax.rem(dp // 32 + k // 4, 4)
    y = lax.rem(lax.rem(dp, 4) + k % 4, 4)
    z = lax.rem(dp // 4, 8)
    return (x * 32 + z * 4 + y, lax.axis_index("pair")), x * 4 + y


def z_peer(k):
    dp = lax.axis_index("dp")
    z = lax.rem(lax.rem(dp // 4, 8) + k, 8)
    return ((dp // 32) * 32 + z * 4 + lax.rem(dp, 4), lax.axis_index("pair")), z


def column_peer(k):
    (dp, _), z = z_peer(k // 2)
    core = lax.rem(lax.axis_index("pair") + k % 2, 2)
    return (dp, core), z * 2 + core


PLANE_STEPS = (10, 6, 9, 11, 14, 2, 5, 7, 8, 13, 15, 1, 3, 4, 12)
Z_STEPS = (4, 3, 5, 2, 6, 1, 7)
COLUMN_STEPS = (9, 8, 7, 6, 11, 10, 5, 4, 13, 12, 3, 2, 15, 14, 1)
CHIPS, DEPTH, COLUMN = (plane_peer, PLANE_STEPS), (z_peer, Z_STEPS), (column_peer, COLUMN_STEPS)
GROUPS = (COLUMN, CHIPS)


def rows_at(place, count):
    return pl.ds(pl.multiple_of(place * count, count), count)


def greet():
    barrier = pltpu.get_barrier_semaphore()
    for peer, steps in GROUPS:
        for k in steps:
            pl.semaphore_signal(barrier, inc=1, device_id=peer(k)[0], device_id_type=MESH)
    return lambda: pl.semaphore_wait(barrier, sum(len(steps) for _, steps in GROUPS))


def exchange(stage, group, source, target, send, recv):
    peer, steps = group
    copies = []
    for k in steps:
        device, place = peer(k)
        copy = pltpu.make_async_remote_copy(
            src_ref=source(place), dst_ref=target, send_sem=send.at[stage, k], recv_sem=recv.at[stage, k],
            device_id=device, device_id_type=MESH,
        )
        copy.start()
        copies.append(copy)
    return copies


def finish(copies):
    for copy in copies:
        copy.wait()


def added(slots):
    total = slots[0].astype(jnp.float32)
    for k in range(1, 16):
        total = total + slots[k].astype(jnp.float32)
    return total


def reduce_everywhere(packed, finish_gradients, out, leaving, first, second, small, send, recv):
    _, place = plane_peer(0)
    _, column = column_peer(0)
    leaving[...] = packed[...].astype(jnp.bfloat16)
    copies = exchange(2, CHIPS, lambda other: leaving.at[rows_at(other, 16)], first.at[place], send, recv)
    first[place] = leaving[rows_at(place, 16)]
    finish_gradients(small)
    second[column, 16:32] = jnp.concatenate([small[...], jnp.zeros((8, 128), jnp.float32)], axis=0).astype(jnp.bfloat16)
    finish(copies)
    second[column, 0:16] = added(first).astype(jnp.bfloat16)
    copies = exchange(3, COLUMN, lambda other: second.at[column], second.at[column], send, recv)
    finish(copies)
    out[place] = added(second).astype(jnp.bfloat16)
    copies = exchange(4, CHIPS, lambda other: out.at[place], out.at[place], send, recv)
    finish(copies)


def crop_table(counts, ids, corners):
    shape = (256, 256)
    count = counts[...].astype(jnp.float32)
    before = onehot(iota(shape, 0) < iota(shape, 1))
    starts = nn(count.astype(jnp.bfloat16), before)
    number = (iota(shape, 0) + 256 * lax.axis_index("pair")).astype(jnp.float32)
    total = jnp.zeros((256, 4), jnp.float32)
    for s in range(MOST):
        chosen = onehot((number == starts + s) & (count > s))
        table = jnp.concatenate([ids[s : s + 1, :], corners[s]], axis=0)
        total = total + nt(chosen, table.astype(jnp.bfloat16))
    return total


def as_number(condition_shape, axis):
    return iota(condition_shape, axis).astype(jnp.float32)


def column(ref):
    eye = iota((CH, CH), 0) == iota((CH, CH), 1)
    return jnp.sum(jnp.where(eye, ref[...], 0.0), axis=1, keepdims=True)


def step_kernel(
    pool_at, counts_at, ids_at, corners_at, conv_first_at, conv_second_at, gain_at, head_at, *refs
):
    small_at, moments_at, (out, small, *moments), refs = refs[0:6], refs[6:8], refs[8:12], refs[12:]
    (
    pool, counts, ids, corners, conv_first, conv_second, gain_ref, head_ref, loaded,
    gathered, arrived, leaving, landed, spots, packed, summands, first, second_sums, small_sums, send, recv,
    toeplitz_first, forward, backward, patches, hidden, hidden_stack, second, logits, cotangent, cotangent_stack,
    ) = refs
    wait_for_all = greet()
    pairs = (
        (counts_at, counts), (ids_at, ids), (corners_at, corners), (pool_at, pool),
        (conv_first_at, conv_first), (conv_second_at, conv_second), (gain_at, gain_ref), (head_at, head_ref),
    ) + tuple((source, small.at[k, 0 : source.shape[0]]) for k, source in enumerate(small_at)) + tuple(zip(moments_at, moments))
    loads = [pltpu.make_async_copy(*pair, loaded.at[k]) for k, pair in enumerate(pairs)]
    for load in loads:
        load.start()
    _, place = plane_peer(0)
    _, z = z_peer(0)
    for load in loads[0:3]:
        load.wait()
    table = crop_table(counts, ids, corners)
    loads[3].wait()
    blocks = pool[...].reshape(512, 256)
    depth = table[:, 3:4].astype(jnp.int32)
    narrow = onehot(
        (iota((256, 128), 0) // BLOCK == iota((256, 128), 1) // SIDE)
        & (iota((256, 128), 0) % BLOCK == iota((256, 128), 1) % SIDE)
    )
    for c in range(2):
        chosen = onehot(2.0 * table[:, 0:1] + c == as_number((256, 512), 1))
        slab = nn(chosen, blocks)
        parts = []
        for part in (slab[:, 0:128], slab[:, 128:256]):
            for bit in (16, 8, 4, 2, 1):
                part = jnp.where((depth & bit) != 0, pltpu.roll(part, 128 - bit, 1), part)
            parts.append(part)
        cut = jnp.concatenate(parts, axis=1).astype(jnp.bfloat16)
        gathered[:, 128 * c : 128 * c + 128] = nn(cut, narrow).astype(jnp.bfloat16)
    wait_for_all()
    copies = exchange(0, CHIPS, lambda other: gathered.at[rows_at(other, 16)], arrived.at[rows_at(place, 16)], send, recv)
    arrived[rows_at(place, 16)] = gathered[rows_at(place, 16)]
    for load in loads[4:]:
        load.wait()
    expand_first(conv_first, toeplitz_first)
    expand_second(conv_second, forward, backward)
    table = table.astype(jnp.bfloat16)
    row = iota((128, 1), 0)
    crop = row // 16 * 2 + row % 16 // 8
    about = nn(onehot(iota((128, 256), 1) == place * 16 + crop), table)
    x = jnp.floor((about[:, 1:2] - z.astype(jnp.float32) + 7.0) * 0.125) + (row % 8 // 4).astype(jnp.float32)
    wanted = (x * 4.0 + (row % 4).astype(jnp.float32)) * 16.0 + crop.astype(jnp.float32)
    chosen = onehot(wanted == as_number((128, 256), 1))
    finish(copies)
    leaving[...] = nn(chosen, arrived[...]).astype(jnp.bfloat16)
    copies = exchange(1, DEPTH, lambda other: leaving.at[rows_at(other, 16)], landed.at[rows_at(z, 16)], send, recv)
    landed[rows_at(z, 16)] = leaving[rows_at(z, 16)]
    gain = column(gain_ref)
    head = column(head_ref).astype(jnp.bfloat16).astype(jnp.float32)
    row = iota((128, 1), 0)
    s, p = row % 32 // 16, row % 16
    about = nn(onehot(iota((128, 256), 1) == place * 16 + z * 2 + s), table)
    x = about[:, 1:2] + p.astype(jnp.float32)
    wanted = (x - 8.0 * jnp.floor(x * 0.125)) * 16.0 + (s * 8 + p // 8 * 4 + row // 32).astype(jnp.float32)
    chosen = onehot((wanted == as_number((128, 128), 1)) & (p < CROP))
    lane = iota((1, PART), 1)
    for s in range(2):
        y = about[16 * s : 16 * s + 1, 2:3] + (lane % PITCH // CROP).astype(jnp.float32)
        spot = y * SIDE + (lane % PITCH % CROP).astype(jnp.float32)
        inside = in_crop() & (lane // PITCH == s)
        spots[s] = onehot(jnp.where(inside, spot, -1.0) == as_number((512, PART), 0))
    finish(copies)
    planes = nn(chosen, landed[...]).astype(jnp.bfloat16)
    window = jnp.zeros((32, PART), jnp.float32)
    for s in range(2):
        whole = jnp.concatenate(
            [
                jnp.concatenate([planes[32 * q + 16 * s : 32 * q + 16 * s + 16, 128 * c : 128 * c + 128] for q in range(4)], axis=1)
                for c in range(2)
            ],
            axis=0,
        )
        window = window + nn(whole, spots[s])
    packed[216:256, :] = jnp.zeros((40, 128), jnp.float32)
    finish_gradients = crop_gradients(
        window[0:16], window[16:28], gain, head, packed,
        toeplitz_first, forward, backward, patches, hidden, hidden_stack, second, logits, cotangent, cotangent_stack,
    )
    reduce_everywhere(
        packed, finish_gradients, out, summands, first, second_sums, small_sums, send, recv
    )


SCRATCH = [
    pltpu.VMEM((256, 2, 256), jnp.bfloat16),
    pltpu.VMEM((1, 256), jnp.int32),
    pltpu.VMEM((MOST, 256), jnp.int32),
    pltpu.VMEM((MOST, 3, 256), jnp.int32),
    pltpu.VMEM((27, CH), jnp.float32),
    pltpu.VMEM((27, CH, CH), jnp.float32),
    pltpu.VMEM((1, CH), jnp.float32),
    pltpu.VMEM((1, CH), jnp.float32),
    pltpu.SemaphoreType.DMA((16,)),
    pltpu.VMEM((256, 256), jnp.bfloat16),
    pltpu.VMEM((256, 256), jnp.bfloat16),
    pltpu.VMEM((128, 256), jnp.bfloat16),
    pltpu.VMEM((128, 256), jnp.bfloat16),
    pltpu.VMEM((2, 512, PART), jnp.bfloat16),
    pltpu.VMEM((256, 128), jnp.float32),
    pltpu.VMEM((256, 128), jnp.bfloat16),
    pltpu.VMEM((16, 16, 128), jnp.bfloat16),
    pltpu.VMEM((16, 32, 128), jnp.bfloat16),
    pltpu.VMEM((8, 128), jnp.float32),
    pltpu.SemaphoreType.DMA((5, 16)),
    pltpu.SemaphoreType.DMA((5, 16)),
]


def summed_gradients(pool, crop_ids, crop_corners, counts, conv_first, conv_second, norm_gain, head_weight, small, large):
    return pl.pallas_call(
        step_kernel,
        out_shape=[jax.ShapeDtypeStruct((16, 32, 128), jnp.bfloat16), jax.ShapeDtypeStruct((6, 32, CH), jnp.float32)]
        + [jax.ShapeDtypeStruct((27, CH, CH), jnp.float32)] * 2,
        in_specs=[pl.BlockSpec(memory_space=pltpu.HBM)] * 16,
        out_specs=[pl.BlockSpec(memory_space=pltpu.VMEM)] * 4,
        scratch_shapes=SCRATCH + COMPUTE_SCRATCH,
        compiler_params=pltpu.CompilerParams(
            collective_id=0, has_side_effects=True, vmem_limit_bytes=20 * 1024 * 1024
        ),
    )(*[
        pltpu.with_memory_space_constraint(value, pltpu.HBM)
        for value in (
            pool, counts.reshape(1, 256), crop_ids.T, crop_corners.transpose(1, 2, 0),
            conv_first, conv_second, norm_gain.reshape(1, CH), head_weight.reshape(1, CH),
            *[value.reshape(-1, CH) for value in small],
            *large,
        )
    ])


beta_first = 0.9
beta_second = 0.999


def adam_update(gradient, momentum, variance):
    next_momentum = beta_first * momentum + (1.0 - beta_first) * gradient
    next_variance = beta_second * variance + (1.0 - beta_second) * gradient * gradient
    return next_momentum / (jnp.sqrt(next_variance) + 1e-08), next_momentum


def adam_kernel(inverse_batch, total, small, moment, variance, *refs):
    updates, nexts = refs[0:4], refs[4:8]
    gradient = total[:, 0:16].astype(jnp.float32).reshape(256, 128) * inverse_batch
    small_gradient = added(total[:, 16:32])[0:8] * inverse_batch
    for dx in range(3):
        j = 2 - dx
        part = jnp.concatenate(
            [gradient[0:216, CH * j : CH * j + CH], gradient[72 * j : 72 * j + 72, 96:128]], axis=0
        ).reshape(9, CH, CH)
        taps = slice(9 * dx, 9 * dx + 9)
        updates[1][taps], nexts[1][taps] = adam_update(part, moment[taps], variance[taps])
        part = jnp.concatenate([small_gradient[:, CH * dx : CH * dx + CH], small_gradient[2 + dx : 3 + dx, 96:128]], axis=0)
        updates[0][taps], nexts[0][taps] = adam_update(part, small[0, taps], small[3, taps])
    for k in (1, 2):
        part = small_gradient[k - 1 : k, 96:128]
        updates[k + 1][...], nexts[k + 1][...] = adam_update(part, small[k, 0:1], small[k + 3, 0:1])


def adam(batch_size, total, small, moment, variance):
    shapes = [jax.ShapeDtypeStruct(shape, jnp.float32) for shape in ((27, CH), (27, CH, CH), (1, CH), (1, CH))]
    results = pl.pallas_call(
        functools.partial(adam_kernel, 1.0 / batch_size),
        out_shape=shapes + shapes,
        in_specs=[pl.BlockSpec(memory_space=pltpu.VMEM)] * 4,
        out_specs=[pl.BlockSpec(memory_space=pltpu.VMEM)] * 8,
        compiler_params=pltpu.CompilerParams(vmem_limit_bytes=8 * 1024 * 1024),
    )(total, small, moment, variance)
    return tuple(value.reshape(CH) if value.shape == (1, CH) else value for value in results)


SHARE = 2


def shards(
    pool, crop_ids, crop_corners, counts, conv_first, conv_second, norm_gain, head_weight,
    momentum_first, momentum_second, momentum_gain, momentum_head,
    variance_first, variance_second, variance_gain, variance_head,
):
    moved_on = summed_gradients(
        pool, crop_ids, crop_corners, counts, conv_first, conv_second, norm_gain, head_weight,
        (momentum_first, momentum_gain, momentum_head, variance_first, variance_gain, variance_head),
        (momentum_second, variance_second),
    )
    return adam(counts.shape[0] * SHARE, *moved_on)


def solution(mesh):
    in_specs = (P(None, None, "dp"),) + (P(),) * 15
    return jax.shard_map(shards, mesh=mesh, in_specs=in_specs, out_specs=(P(),) * 8, check_vma=False)
```

```python
import functools

import jax
import jax.numpy as jnp
from jax import lax
from jax.experimental import pallas as pl
from jax.experimental.pallas import tpu as pltpu
from jax.sharding import PartitionSpec as P

CH = 32
CROP = 12
BLOCK = 32
MOST = 3


SIDE = 16
PLANE = CROP * CROP
PITCH = PLANE + 2 * CROP
PART = 384
LANES = 2 * PART
VOXELS = CROP * CROP * CROP
BAND = 6 * CH
TAPS = 9 * BAND


def iota(shape, axis):
    return lax.broadcasted_iota(jnp.int32, shape, axis)


def nt(a, b):
    return lax.dot_general(a, b, (((1,), (1,)), ((), ())), preferred_element_type=jnp.float32)


def nn(a, b):
    return jnp.dot(a, b, preferred_element_type=jnp.float32)


def onehot(condition):
    return jnp.where(condition, 1.0, 0.0).astype(jnp.bfloat16)


def in_crop():
    lane = iota((1, PART), 1)
    return (lane < 2 * PITCH) & (lane % PITCH < PLANE)


def edges(reach):
    z = iota((1, PART), 1) % PITCH % CROP
    return z < CROP - reach, None, z >= reach


def sources(value, masks):
    value = value.astype(jnp.bfloat16)
    return [value if mask is None else jnp.where(mask, value, jnp.zeros_like(value)) for mask in masks]


def moved(source, dy, dz):
    amount = (-(CROP * dy + dz)) % PART
    return (pltpu.roll(source, amount, 1) if amount else source).astype(jnp.bfloat16)


def by_crop(columns):
    return jnp.where(iota((1, PART), 1) < PITCH, columns[0], columns[1])


def crop_sums(value):
    lane = iota((1, PART), 1)
    value = jnp.where(in_crop(), value, 0.0)
    first = jnp.sum(jnp.where(lane < PITCH, value, 0.0), axis=1, keepdims=True)
    return first, jnp.sum(jnp.where(lane >= PITCH, value, 0.0), axis=1, keepdims=True)


def expand_first(conv_first, toeplitz_first):
    weights = conv_first[...].astype(jnp.bfloat16)
    repeat = onehot(iota((12 * CH, CH), 0) % CH == iota((12 * CH, CH), 1))
    row, column = iota((12 * CH, 144), 0), iota((12 * CH, 144), 1)
    place = row // CH
    step = column % 16 - (2 * (place % 6) + place // 6) + 1
    total = jnp.zeros((12 * CH, 144), jnp.float32)
    for dx in range(3):
        tap = onehot(iota((144, 27), 0) // 16 + 9 * dx == iota((144, 27), 1))
        spread = nn(tap, weights).astype(jnp.bfloat16)
        total = jnp.where(step == dx, nt(repeat, spread), total)
    toeplitz_first[...] = total.astype(jnp.bfloat16)


def expand_second(conv_second, forward, backward):
    eye = onehot(iota((CH, CH), 0) == iota((CH, CH), 1))
    zero = jnp.zeros((CH, 256 - 3 * CH), jnp.float32)
    plain, turned = [], []
    for tap in range(9):
        blocks = [conv_second[9 * dx + tap] for dx in range(3)]
        plain.append(jnp.concatenate([blocks[2], blocks[1], blocks[0], zero], axis=1))
        stacked = jnp.concatenate(blocks, axis=0).astype(jnp.bfloat16)
        turned.append(jnp.concatenate([nt(eye, stacked), zero], axis=1))
    for i in range(6):
        rows = slice(i * CH, i * CH + CH)
        amount = (CH * (i - 1)) % 256
        for strips, matrix in ((plain, backward), (turned, forward)):
            bands = [(pltpu.roll(strip, amount, 1) if amount else strip)[:, 0:BAND] for strip in strips]
            matrix[rows, :] = jnp.concatenate(bands, axis=1).astype(jnp.bfloat16)


def crop_gradients(
    image, target, gain, head, packed,
    toeplitz_first, forward, backward, patches, hidden, hidden_stack, second, logits, cotangent, cotangent_stack,
):
    halves = (slice(0, PART), slice(PART, LANES))
    places = [(parity, i) for parity in range(2) for i in range(6)]
    steps = [(tap // 3 - 1, tap % 3 - 1) for tap in range(9)]
    valid = in_crop()
    image = sources(image, edges(1))
    for tap, (dy, dz) in enumerate(steps):
        patches[tap * 16 : tap * 16 + 16, :] = moved(image[dz + 1], dy, dz)
    masks = edges(2)
    for parity, half in enumerate(halves):
        first_map = nn(toeplitz_first[parity * BAND : parity * BAND + BAND, :], patches[...])
        value = jnp.where(valid, jnp.maximum(first_map, 0.0), 0.0)
        hidden[:, half] = value.astype(jnp.bfloat16)
        value = sources(value, masks)
        for tap, (dy, dz) in enumerate(steps):
            hidden_stack[tap * BAND : tap * BAND + BAND, half] = moved(value[dz + 1], 2 * dy, 2 * dz)
    second[...] = nn(forward[...], hidden_stack[...])
    scale = 1.0 / VOXELS
    total = jnp.zeros((CH, PART), jnp.float32)
    for parity, i in places:
        total = total + second[i * CH : i * CH + CH, halves[parity]]
    center = by_crop([value * scale for value in crop_sums(total)])
    total = jnp.zeros((CH, PART), jnp.float32)
    for parity, i in places:
        away = second[i * CH : i * CH + CH, halves[parity]] - center
        total = total + away * away
    inverse = by_crop([lax.rsqrt(value * scale + 1e-05) for value in crop_sums(total)])
    for parity, i in places:
        rows, half, plane = slice(i * CH, i * CH + CH), halves[parity], 2 * i + parity
        hat = (second[rows, half] - center) * inverse
        second[rows, half] = hat
        joined = (jnp.maximum(hat * gain, 0.0) + hidden[rows, half].astype(jnp.float32)).astype(jnp.bfloat16)
        logits[plane : plane + 1, :] = jnp.sum(joined.astype(jnp.float32) * head, axis=0, keepdims=True)
    slope = 1.0 / (1.0 + jnp.exp(-logits[0:12, :])) - target
    logits[0:12, :] = jnp.where(valid, slope * scale, 0.0)
    sum_plain = jnp.zeros((CH, PART), jnp.float32)
    sum_hat = jnp.zeros((CH, PART), jnp.float32)
    for parity, i in places:
        rows, half, plane = slice(i * CH, i * CH + CH), halves[parity], 2 * i + parity
        hat = second[rows, half]
        normed = hat * gain
        slope = logits[plane : plane + 1, :]
        passed = jnp.where(normed > 0.0, slope, 0.0)
        sum_plain = sum_plain + passed
        sum_hat = sum_hat + passed * hat
    sums_plain = [head * value for value in crop_sums(sum_plain)]
    sums_hat = [head * value for value in crop_sums(sum_hat)]
    grad_gain = sum(sums_hat)
    mean_plain = by_crop([value * scale for value in sums_plain])
    mean_hat = by_crop([value * scale for value in sums_hat])
    factor = jnp.where(valid, inverse * gain, 0.0)
    for parity, i in places:
        rows, half, plane = slice(i * CH, i * CH + CH), halves[parity], 2 * i + parity
        hat = second[rows, half]
        slope = logits[plane : plane + 1, :]
        passed = jnp.where(hat * gain > 0.0, head * slope, 0.0)
        cotangent[rows, half] = (factor * (passed - mean_plain - hat * mean_hat)).astype(jnp.bfloat16)
    cotangent[BAND:256, :] = jnp.zeros((256 - BAND, LANES), jnp.bfloat16)
    turned = cotangent[...].T
    lane = iota((CH, 128), 1)
    for tap in range(9):
        if tap % 3 == 0:
            three = nn(hidden_stack[tap * BAND : tap * BAND + 3 * BAND, :], turned)
        products = three[tap % 3 * BAND : tap % 3 * BAND + BAND]
        low, high = products[:, 0:128], products[:, 128:256]
        band = [slice(i * CH, i * CH + CH) for i in range(6)]
        total = low[band[1]] + high[band[5]] + jnp.where(lane >= CH, pltpu.roll(low[band[0]], CH, 1), 0.0)
        total = total + pltpu.roll(low[band[2]], 96, 1)
        for i, amount in ((3, 64), (4, 32)):
            total = total + pltpu.roll(jnp.where(lane < 128 - amount, high[band[i]], low[band[i]]), amount, 1)
        at = tap * CH
        if at < 216:
            count = min(CH, 216 - at)
            packed[at : at + count, :] = jnp.where(lane < 96, total, 0.0)[0:count]
        if at + CH > 216:
            skip = max(0, 216 - at)
            for j in range(3):
                shifted = pltpu.roll(total, 96 - CH * j, 1)
                shifted = jnp.where(lane >= 96, shifted, 0.0)[skip:CH]
                to = 72 * j + at + skip - 216
                packed[to : to + CH - skip, :] = packed[to : to + CH - skip, :] + shifted
    return lambda small: first_gradients(
        small, gain, head, grad_gain, backward, patches, hidden, second, logits, cotangent, cotangent_stack,
    )


def first_gradients(
    small_sums, gain, head, grad_gain, backward, patches, hidden, second, logits, cotangent, cotangent_stack,
):
    halves = (slice(0, PART), slice(PART, LANES))
    places = [(parity, i) for parity in range(2) for i in range(6)]
    masks = edges(2)
    for half in halves:
        value = sources(cotangent[0:BAND, half], masks)
        for tap in range(9):
            dy, dz = tap // 3 - 1, tap % 3 - 1
            cotangent_stack[tap * BAND : tap * BAND + BAND, half] = moved(value[1 - dz], -2 * dy, -2 * dz)
    back = nn(backward[...], cotangent_stack[...])
    sum_head = jnp.zeros((CH, PART), jnp.float32)
    for parity, i in places:
        rows, half, plane = slice(i * CH, i * CH + CH), halves[parity], 2 * i + parity
        slope = logits[plane : plane + 1, :]
        normed = second[rows, half] * gain
        joined = (jnp.maximum(normed, 0.0) + hidden[rows, half].astype(jnp.float32)).astype(jnp.bfloat16)
        sum_head = sum_head + joined.astype(jnp.float32) * slope
        whole = back[rows, half] + head * slope
        alive = hidden[rows, half].astype(jnp.float32) > 0.0
        second[rows, half] = jnp.where(alive, whole, 0.0)
    grad_head = sum(crop_sums(sum_head))
    lane = iota((9, 128), 1)
    small = jnp.zeros((9, 128), jnp.float32)
    products = jnp.concatenate([nt(patches[...], second[:, half].astype(jnp.bfloat16)) for half in halves], axis=1)
    row, column = iota((144, 2 * BAND), 0), iota((144, 2 * BAND), 1)
    place = column // CH
    step = row % 16 - (2 * (place % 6) + place // 6) + 1
    for dx in range(3):
        part = jnp.where(step == dx, products, 0.0)
        part = jnp.sum(part.reshape(9, 16, 2 * BAND), axis=1)
        part = part[:, 0:128] + part[:, 128:256] + part[:, 256:384]
        part = part + pltpu.roll(part, 64, 1)
        part = part + pltpu.roll(part, 32, 1)
        small = jnp.where(lane // CH == dx, part, small)
    pick = iota((CH, 128), 0) + 96 == iota((CH, 128), 1)
    small = small + jnp.concatenate(
        [jnp.sum(jnp.where(pick, value, 0.0), axis=0, keepdims=True) for value in (grad_gain, grad_head)]
        + [jnp.where(lane[0:1] >= 96, pltpu.roll(small[8:9], 96 - CH * dx, 1), 0.0) for dx in range(3)]
        + [jnp.zeros((4, 128), jnp.float32)],
        axis=0,
    )
    small_sums[...] = small[0:8]


COMPUTE_SCRATCH = [
    pltpu.VMEM((12 * CH, 144), jnp.bfloat16),
    pltpu.VMEM((BAND, TAPS), jnp.bfloat16),
    pltpu.VMEM((BAND, TAPS), jnp.bfloat16),
    pltpu.VMEM((144, PART), jnp.bfloat16),
    pltpu.VMEM((BAND, LANES), jnp.bfloat16),
    pltpu.VMEM((TAPS, LANES), jnp.bfloat16),
    pltpu.VMEM((BAND, LANES), jnp.float32),
    pltpu.VMEM((16, PART), jnp.float32),
    pltpu.VMEM((256, LANES), jnp.bfloat16),
    pltpu.VMEM((TAPS, LANES), jnp.bfloat16),
]


MESH = pl.DeviceIdType.MESH


def plane_peer(k):
    dp = lax.axis_index("dp")
    x = lax.rem(dp // 32 + k // 4, 4)
    y = lax.rem(lax.rem(dp, 4) + k % 4, 4)
    z = lax.rem(dp // 4, 8)
    return (x * 32 + z * 4 + y, lax.axis_index("pair")), x * 4 + y


def z_peer(k):
    dp = lax.axis_index("dp")
    z = lax.rem(lax.rem(dp // 4, 8) + k, 8)
    return ((dp // 32) * 32 + z * 4 + lax.rem(dp, 4), lax.axis_index("pair")), z


def column_peer(k):
    (dp, _), z = z_peer(k // 2)
    core = lax.rem(lax.axis_index("pair") + k % 2, 2)
    return (dp, core), z * 2 + core


PLANE_STEPS = (10, 6, 9, 11, 14, 2, 5, 7, 8, 13, 15, 1, 3, 4, 12)
Z_STEPS = (4, 3, 5, 2, 6, 1, 7)
COLUMN_STEPS = (9, 8, 7, 6, 11, 10, 5, 4, 13, 12, 3, 2, 15, 14, 1)
CHIPS, DEPTH, COLUMN = (plane_peer, PLANE_STEPS), (z_peer, Z_STEPS), (column_peer, COLUMN_STEPS)
GROUPS = (COLUMN, CHIPS)


def rows_at(place, count):
    return pl.ds(pl.multiple_of(place * count, count), count)


def greet():
    barrier = pltpu.get_barrier_semaphore()
    for peer, steps in GROUPS:
        for k in steps:
            pl.semaphore_signal(barrier, inc=1, device_id=peer(k)[0], device_id_type=MESH)
    return lambda: pl.semaphore_wait(barrier, sum(len(steps) for _, steps in GROUPS))


def exchange(stage, group, source, target, send, recv):
    peer, steps = group
    copies = []
    for k in steps:
        device, place = peer(k)
        copy = pltpu.make_async_remote_copy(
            src_ref=source(place), dst_ref=target, send_sem=send.at[stage, k], recv_sem=recv.at[stage, k],
            device_id=device, device_id_type=MESH,
        )
        copy.start()
        copies.append(copy)
    return copies


def finish(copies):
    for copy in copies:
        copy.wait()


def added(slots):
    total = slots[0].astype(jnp.float32)
    for k in range(1, 16):
        total = total + slots[k].astype(jnp.float32)
    return total


def in_two(value):
    high = value.astype(jnp.bfloat16)
    return jnp.concatenate([high, (value - high.astype(jnp.float32)).astype(jnp.bfloat16)], axis=0)


def reduce_everywhere(packed, finish_gradients, out, leaving, first, second, small, send, recv):
    _, place = plane_peer(0)
    _, column = column_peer(0)
    leaving[...] = packed[...].astype(jnp.bfloat16)
    copies = exchange(2, CHIPS, lambda other: leaving.at[rows_at(other, 16)], first.at[place], send, recv)
    first[place] = leaving[rows_at(place, 16)]
    finish_gradients(small)
    second[column, 16:32] = in_two(small[...])
    finish(copies)
    second[column, 0:16] = added(first).astype(jnp.bfloat16)
    copies = exchange(3, COLUMN, lambda other: second.at[column], second.at[column], send, recv)
    finish(copies)
    total = added(second)
    out[place, 0:16] = total[0:16].astype(jnp.bfloat16)
    out[place, 16:32] = in_two(total[16:24] + total[24:32])
    copies = exchange(4, CHIPS, lambda other: out.at[place], out.at[place], send, recv)
    finish(copies)


def crop_table(counts, ids, corners):
    shape = (256, 256)
    count = counts[...].astype(jnp.float32)
    before = onehot(iota(shape, 0) < iota(shape, 1))
    starts = nn(count.astype(jnp.bfloat16), before)
    number = (iota(shape, 0) + 256 * lax.axis_index("pair")).astype(jnp.float32)
    total = jnp.zeros((256, 4), jnp.float32)
    for s in range(MOST):
        chosen = onehot((number == starts + s) & (count > s))
        table = jnp.concatenate([ids[s : s + 1, :], corners[s]], axis=0)
        total = total + nt(chosen, table.astype(jnp.bfloat16))
    return total


def as_number(condition_shape, axis):
    return iota(condition_shape, axis).astype(jnp.float32)


def column(ref):
    eye = iota((CH, CH), 0) == iota((CH, CH), 1)
    return jnp.sum(jnp.where(eye, ref[...], 0.0), axis=1, keepdims=True)


def step_kernel(
    pool_at, counts_at, ids_at, corners_at, conv_first_at, conv_second_at, gain_at, head_at, *refs
):
    small_at, moments_at, (out, small, *moments), refs = refs[0:6], refs[6:8], refs[8:12], refs[12:]
    (
    pool, counts, ids, corners, conv_first, conv_second, gain_ref, head_ref, loaded,
    gathered, arrived, leaving, landed, spots, packed, summands, first, second_sums, small_sums, send, recv,
    toeplitz_first, forward, backward, patches, hidden, hidden_stack, second, logits, cotangent, cotangent_stack,
    ) = refs
    wait_for_all = greet()
    pairs = (
        (counts_at, counts), (ids_at, ids), (corners_at, corners), (pool_at, pool),
        (conv_first_at, conv_first), (conv_second_at, conv_second), (gain_at, gain_ref), (head_at, head_ref),
    ) + tuple((source, small.at[k, 0 : source.shape[0]]) for k, source in enumerate(small_at)) + tuple(zip(moments_at, moments))
    loads = [pltpu.make_async_copy(*pair, loaded.at[k]) for k, pair in enumerate(pairs)]
    for load in loads:
        load.start()
    _, place = plane_peer(0)
    _, z = z_peer(0)
    for load in loads[0:3]:
        load.wait()
    table = crop_table(counts, ids, corners)
    loads[3].wait()
    blocks = pool[...].reshape(512, 256)
    depth = table[:, 3:4].astype(jnp.int32)
    narrow = onehot(
        (iota((256, 128), 0) // BLOCK == iota((256, 128), 1) // SIDE)
        & (iota((256, 128), 0) % BLOCK == iota((256, 128), 1) % SIDE)
    )
    for c in range(2):
        chosen = onehot(2.0 * table[:, 0:1] + c == as_number((256, 512), 1))
        slab = nn(chosen, blocks)
        parts = []
        for part in (slab[:, 0:128], slab[:, 128:256]):
            for bit in (16, 8, 4, 2, 1):
                part = jnp.where((depth & bit) != 0, pltpu.roll(part, 128 - bit, 1), part)
            parts.append(part)
        cut = jnp.concatenate(parts, axis=1).astype(jnp.bfloat16)
        gathered[:, 128 * c : 128 * c + 128] = nn(cut, narrow).astype(jnp.bfloat16)
    wait_for_all()
    copies = exchange(0, CHIPS, lambda other: gathered.at[rows_at(other, 16)], arrived.at[rows_at(place, 16)], send, recv)
    arrived[rows_at(place, 16)] = gathered[rows_at(place, 16)]
    for load in loads[4:]:
        load.wait()
    expand_first(conv_first, toeplitz_first)
    expand_second(conv_second, forward, backward)
    table = table.astype(jnp.bfloat16)
    row = iota((128, 1), 0)
    crop = row // 16 * 2 + row % 16 // 8
    about = nn(onehot(iota((128, 256), 1) == place * 16 + crop), table)
    x = jnp.floor((about[:, 1:2] - z.astype(jnp.float32) + 7.0) * 0.125) + (row % 8 // 4).astype(jnp.float32)
    wanted = (x * 4.0 + (row % 4).astype(jnp.float32)) * 16.0 + crop.astype(jnp.float32)
    chosen = onehot(wanted == as_number((128, 256), 1))
    finish(copies)
    leaving[...] = nn(chosen, arrived[...]).astype(jnp.bfloat16)
    copies = exchange(1, DEPTH, lambda other: leaving.at[rows_at(other, 16)], landed.at[rows_at(z, 16)], send, recv)
    landed[rows_at(z, 16)] = leaving[rows_at(z, 16)]
    gain = column(gain_ref)
    head = column(head_ref).astype(jnp.bfloat16).astype(jnp.float32)
    row = iota((128, 1), 0)
    s, p = row % 32 // 16, row % 16
    about = nn(onehot(iota((128, 256), 1) == place * 16 + z * 2 + s), table)
    x = about[:, 1:2] + p.astype(jnp.float32)
    wanted = (x - 8.0 * jnp.floor(x * 0.125)) * 16.0 + (s * 8 + p // 8 * 4 + row // 32).astype(jnp.float32)
    chosen = onehot((wanted == as_number((128, 128), 1)) & (p < CROP))
    lane = iota((1, PART), 1)
    for s in range(2):
        y = about[16 * s : 16 * s + 1, 2:3] + (lane % PITCH // CROP).astype(jnp.float32)
        spot = y * SIDE + (lane % PITCH % CROP).astype(jnp.float32)
        inside = in_crop() & (lane // PITCH == s)
        spots[s] = onehot(jnp.where(inside, spot, -1.0) == as_number((512, PART), 0))
    finish(copies)
    planes = nn(chosen, landed[...]).astype(jnp.bfloat16)
    window = jnp.zeros((32, PART), jnp.float32)
    for s in range(2):
        whole = jnp.concatenate(
            [
                jnp.concatenate([planes[32 * q + 16 * s : 32 * q + 16 * s + 16, 128 * c : 128 * c + 128] for q in range(4)], axis=1)
                for c in range(2)
            ],
            axis=0,
        )
        window = window + nn(whole, spots[s])
    packed[216:256, :] = jnp.zeros((40, 128), jnp.float32)
    finish_gradients = crop_gradients(
        window[0:16], window[16:28], gain, head, packed,
        toeplitz_first, forward, backward, patches, hidden, hidden_stack, second, logits, cotangent, cotangent_stack,
    )
    reduce_everywhere(
        packed, finish_gradients, out, summands, first, second_sums, small_sums, send, recv
    )


SCRATCH = [
    pltpu.VMEM((256, 2, 256), jnp.bfloat16),
    pltpu.VMEM((1, 256), jnp.int32),
    pltpu.VMEM((MOST, 256), jnp.int32),
    pltpu.VMEM((MOST, 3, 256), jnp.int32),
    pltpu.VMEM((27, CH), jnp.float32),
    pltpu.VMEM((27, CH, CH), jnp.float32),
    pltpu.VMEM((1, CH), jnp.float32),
    pltpu.VMEM((1, CH), jnp.float32),
    pltpu.SemaphoreType.DMA((16,)),
    pltpu.VMEM((256, 256), jnp.bfloat16),
    pltpu.VMEM((256, 256), jnp.bfloat16),
    pltpu.VMEM((128, 256), jnp.bfloat16),
    pltpu.VMEM((128, 256), jnp.bfloat16),
    pltpu.VMEM((2, 512, PART), jnp.bfloat16),
    pltpu.VMEM((256, 128), jnp.float32),
    pltpu.VMEM((256, 128), jnp.bfloat16),
    pltpu.VMEM((16, 16, 128), jnp.bfloat16),
    pltpu.VMEM((16, 32, 128), jnp.bfloat16),
    pltpu.VMEM((8, 128), jnp.float32),
    pltpu.SemaphoreType.DMA((5, 16)),
    pltpu.SemaphoreType.DMA((5, 16)),
]


def summed_gradients(pool, crop_ids, crop_corners, counts, conv_first, conv_second, norm_gain, head_weight, small, large):
    return pl.pallas_call(
        step_kernel,
        out_shape=[jax.ShapeDtypeStruct((16, 32, 128), jnp.bfloat16), jax.ShapeDtypeStruct((6, 32, CH), jnp.float32)]
        + [jax.ShapeDtypeStruct((27, CH, CH), jnp.float32)] * 2,
        in_specs=[pl.BlockSpec(memory_space=pltpu.HBM)] * 16,
        out_specs=[pl.BlockSpec(memory_space=pltpu.VMEM)] * 4,
        scratch_shapes=SCRATCH + COMPUTE_SCRATCH,
        compiler_params=pltpu.CompilerParams(
            collective_id=0, has_side_effects=True, vmem_limit_bytes=20 * 1024 * 1024
        ),
    )(*[
        pltpu.with_memory_space_constraint(value, pltpu.HBM)
        for value in (
            pool, counts.reshape(1, 256), crop_ids.T, crop_corners.transpose(1, 2, 0),
            conv_first, conv_second, norm_gain.reshape(1, CH), head_weight.reshape(1, CH),
            *[value.reshape(-1, CH) for value in small],
            *large,
        )
    ])


beta_first = 0.9
beta_second = 0.999


def adam_update(gradient, momentum, variance):
    next_momentum = beta_first * momentum + (1.0 - beta_first) * gradient
    next_variance = beta_second * variance + (1.0 - beta_second) * gradient * gradient
    return next_momentum / (jnp.sqrt(next_variance) + 1e-08), next_momentum


def adam_kernel(inverse_batch, total, small, moment, variance, *refs):
    updates, nexts = refs[0:4], refs[4:8]
    gradient = total[:, 0:16].astype(jnp.float32).reshape(256, 128) * inverse_batch
    small_gradient = added(total[:, 16:32])
    small_gradient = (small_gradient[0:8] + small_gradient[8:16]) * inverse_batch
    for dx in range(3):
        j = 2 - dx
        part = jnp.concatenate(
            [gradient[0:216, CH * j : CH * j + CH], gradient[72 * j : 72 * j + 72, 96:128]], axis=0
        ).reshape(9, CH, CH)
        taps = slice(9 * dx, 9 * dx + 9)
        updates[1][taps], nexts[1][taps] = adam_update(part, moment[taps], variance[taps])
        part = jnp.concatenate([small_gradient[:, CH * dx : CH * dx + CH], small_gradient[2 + dx : 3 + dx, 96:128]], axis=0)
        updates[0][taps], nexts[0][taps] = adam_update(part, small[0, taps], small[3, taps])
    for k in (1, 2):
        part = small_gradient[k - 1 : k, 96:128]
        updates[k + 1][...], nexts[k + 1][...] = adam_update(part, small[k, 0:1], small[k + 3, 0:1])


def adam(batch_size, total, small, moment, variance):
    shapes = [jax.ShapeDtypeStruct(shape, jnp.float32) for shape in ((27, CH), (27, CH, CH), (1, CH), (1, CH))]
    results = pl.pallas_call(
        functools.partial(adam_kernel, 1.0 / batch_size),
        out_shape=shapes + shapes,
        in_specs=[pl.BlockSpec(memory_space=pltpu.VMEM)] * 4,
        out_specs=[pl.BlockSpec(memory_space=pltpu.VMEM)] * 8,
        compiler_params=pltpu.CompilerParams(vmem_limit_bytes=8 * 1024 * 1024),
    )(total, small, moment, variance)
    return tuple(value.reshape(CH) if value.shape == (1, CH) else value for value in results)


SHARE = 2


def shards(
    pool, crop_ids, crop_corners, counts, conv_first, conv_second, norm_gain, head_weight,
    momentum_first, momentum_second, momentum_gain, momentum_head,
    variance_first, variance_second, variance_gain, variance_head,
):
    moved_on = summed_gradients(
        pool, crop_ids, crop_corners, counts, conv_first, conv_second, norm_gain, head_weight,
        (momentum_first, momentum_gain, momentum_head, variance_first, variance_gain, variance_head),
        (momentum_second, variance_second),
    )
    return adam(counts.shape[0] * SHARE, *moved_on)


def solution(mesh):
    in_specs = (P(None, None, "dp"),) + (P(),) * 15
    return jax.shard_map(shards, mesh=mesh, in_specs=in_specs, out_specs=(P(),) * 8, check_vma=False)
```

```python
import functools

import jax
import jax.numpy as jnp
from jax import lax
from jax.experimental import pallas as pl
from jax.experimental.pallas import tpu as pltpu
from jax.sharding import PartitionSpec as P

CH = 32
CROP = 12
BLOCK = 32
MOST = 3


SIDE = 16
PLANE = CROP * CROP
PITCH = PLANE + 2 * CROP
PART = 384
LANES = 2 * PART
VOXELS = CROP * CROP * CROP
BAND = 6 * CH
TAPS = 9 * BAND


def iota(shape, axis):
    return lax.broadcasted_iota(jnp.int32, shape, axis)


def nt(a, b):
    return lax.dot_general(a, b, (((1,), (1,)), ((), ())), preferred_element_type=jnp.float32)


def nn(a, b):
    return jnp.dot(a, b, preferred_element_type=jnp.float32)


def onehot(condition):
    return jnp.where(condition, 1.0, 0.0).astype(jnp.bfloat16)


def in_crop():
    lane = iota((1, PART), 1)
    return (lane < 2 * PITCH) & (lane % PITCH < PLANE)


def edges(reach):
    z = iota((1, PART), 1) % PITCH % CROP
    return z < CROP - reach, None, z >= reach


def sources(value, masks):
    value = value.astype(jnp.bfloat16)
    return [value if mask is None else jnp.where(mask, value, jnp.zeros_like(value)) for mask in masks]


def moved(source, dy, dz):
    amount = (-(CROP * dy + dz)) % PART
    return (pltpu.roll(source, amount, 1) if amount else source).astype(jnp.bfloat16)


def by_crop(columns):
    return jnp.where(iota((1, PART), 1) < PITCH, columns[0], columns[1])


def crop_sums(value):
    lane = iota((1, PART), 1)
    value = jnp.where(in_crop(), value, 0.0)
    first = jnp.sum(jnp.where(lane < PITCH, value, 0.0), axis=1, keepdims=True)
    return first, jnp.sum(jnp.where(lane >= PITCH, value, 0.0), axis=1, keepdims=True)


def expand_first(conv_first, toeplitz_first):
    weights = conv_first[...].astype(jnp.bfloat16)
    repeat = onehot(iota((12 * CH, CH), 0) % CH == iota((12 * CH, CH), 1))
    row, column = iota((12 * CH, 144), 0), iota((12 * CH, 144), 1)
    place = row // CH
    step = column % 16 - (2 * (place % 6) + place // 6) + 1
    total = jnp.zeros((12 * CH, 144), jnp.float32)
    for dx in range(3):
        tap = onehot(iota((144, 27), 0) // 16 + 9 * dx == iota((144, 27), 1))
        spread = nn(tap, weights).astype(jnp.bfloat16)
        total = jnp.where(step == dx, nt(repeat, spread), total)
    toeplitz_first[...] = total.astype(jnp.bfloat16)


def expand_second(conv_second, forward, backward):
    eye = onehot(iota((CH, CH), 0) == iota((CH, CH), 1))
    zero = jnp.zeros((CH, 256 - 3 * CH), jnp.float32)
    plain, turned = [], []
    for tap in range(9):
        blocks = [conv_second[9 * dx + tap] for dx in range(3)]
        plain.append(jnp.concatenate([blocks[2], blocks[1], blocks[0], zero], axis=1))
        stacked = jnp.concatenate(blocks, axis=0).astype(jnp.bfloat16)
        turned.append(jnp.concatenate([nt(eye, stacked), zero], axis=1))
    for i in range(6):
        rows = slice(i * CH, i * CH + CH)
        amount = (CH * (i - 1)) % 256
        for strips, matrix in ((plain, backward), (turned, forward)):
            bands = [(pltpu.roll(strip, amount, 1) if amount else strip)[:, 0:BAND] for strip in strips]
            matrix[rows, :] = jnp.concatenate(bands, axis=1).astype(jnp.bfloat16)


def crop_gradients(
    image, target, gain, head, packed,
    toeplitz_first, forward, backward, patches, hidden, hidden_stack, second, logits, cotangent, cotangent_stack,
):
    halves = (slice(0, PART), slice(PART, LANES))
    places = [(parity, i) for parity in range(2) for i in range(6)]
    steps = [(tap // 3 - 1, tap % 3 - 1) for tap in range(9)]
    valid = in_crop()
    image = sources(image, edges(1))
    for tap, (dy, dz) in enumerate(steps):
        patches[tap * 16 : tap * 16 + 16, :] = moved(image[dz + 1], dy, dz)
    masks = edges(2)
    for parity, half in enumerate(halves):
        first_map = nn(toeplitz_first[parity * BAND : parity * BAND + BAND, :], patches[...])
        value = jnp.where(valid, jnp.maximum(first_map, 0.0), 0.0)
        hidden[:, half] = value.astype(jnp.bfloat16)
        value = sources(value, masks)
        for tap, (dy, dz) in enumerate(steps):
            hidden_stack[tap * BAND : tap * BAND + BAND, half] = moved(value[dz + 1], 2 * dy, 2 * dz)
    second[...] = nn(forward[...], hidden_stack[...])
    scale = 1.0 / VOXELS
    total = jnp.zeros((CH, PART), jnp.float32)
    for parity, i in places:
        total = total + second[i * CH : i * CH + CH, halves[parity]]
    center = by_crop([value * scale for value in crop_sums(total)])
    total = jnp.zeros((CH, PART), jnp.float32)
    for parity, i in places:
        away = second[i * CH : i * CH + CH, halves[parity]] - center
        total = total + away * away
    inverse = by_crop([lax.rsqrt(value * scale + 1e-05) for value in crop_sums(total)])
    for parity, i in places:
        rows, half, plane = slice(i * CH, i * CH + CH), halves[parity], 2 * i + parity
        hat = (second[rows, half] - center) * inverse
        second[rows, half] = hat
        joined = (jnp.maximum(hat * gain, 0.0) + hidden[rows, half].astype(jnp.float32)).astype(jnp.bfloat16)
        logits[plane : plane + 1, :] = jnp.sum(joined.astype(jnp.float32) * head, axis=0, keepdims=True)
    slope = 1.0 / (1.0 + jnp.exp(-logits[0:12, :])) - target
    logits[0:12, :] = jnp.where(valid, slope * scale, 0.0)
    sum_plain = jnp.zeros((CH, PART), jnp.float32)
    sum_hat = jnp.zeros((CH, PART), jnp.float32)
    for parity, i in places:
        rows, half, plane = slice(i * CH, i * CH + CH), halves[parity], 2 * i + parity
        hat = second[rows, half]
        normed = hat * gain
        slope = logits[plane : plane + 1, :]
        passed = jnp.where(normed > 0.0, slope, 0.0)
        sum_plain = sum_plain + passed
        sum_hat = sum_hat + passed * hat
    sums_plain = [head * value for value in crop_sums(sum_plain)]
    sums_hat = [head * value for value in crop_sums(sum_hat)]
    grad_gain = sum(sums_hat)
    mean_plain = by_crop([value * scale for value in sums_plain])
    mean_hat = by_crop([value * scale for value in sums_hat])
    factor = jnp.where(valid, inverse * gain, 0.0)
    for parity, i in places:
        rows, half, plane = slice(i * CH, i * CH + CH), halves[parity], 2 * i + parity
        hat = second[rows, half]
        slope = logits[plane : plane + 1, :]
        passed = jnp.where(hat * gain > 0.0, head * slope, 0.0)
        cotangent[rows, half] = (factor * (passed - mean_plain - hat * mean_hat)).astype(jnp.bfloat16)
    cotangent[BAND:256, :] = jnp.zeros((256 - BAND, LANES), jnp.bfloat16)
    turned = cotangent[...].T
    lane = iota((CH, 128), 1)
    for tap in range(9):
        if tap % 3 == 0:
            three = nn(hidden_stack[tap * BAND : tap * BAND + 3 * BAND, :], turned)
        products = three[tap % 3 * BAND : tap % 3 * BAND + BAND]
        low, high = products[:, 0:128], products[:, 128:256]
        band = [slice(i * CH, i * CH + CH) for i in range(6)]
        total = low[band[1]] + high[band[5]] + jnp.where(lane >= CH, pltpu.roll(low[band[0]], CH, 1), 0.0)
        total = total + pltpu.roll(low[band[2]], 96, 1)
        for i, amount in ((3, 64), (4, 32)):
            total = total + pltpu.roll(jnp.where(lane < 128 - amount, high[band[i]], low[band[i]]), amount, 1)
        at = tap * CH
        if at < 216:
            count = min(CH, 216 - at)
            packed[at : at + count, :] = jnp.where(lane < 96, total, 0.0)[0:count]
        if at + CH > 216:
            skip = max(0, 216 - at)
            for j in range(3):
                shifted = pltpu.roll(total, 96 - CH * j, 1)
                shifted = jnp.where(lane >= 96, shifted, 0.0)[skip:CH]
                to = 72 * j + at + skip - 216
                packed[to : to + CH - skip, :] = packed[to : to + CH - skip, :] + shifted
    return lambda small: first_gradients(
        small, gain, head, grad_gain, backward, patches, hidden, second, logits, cotangent, cotangent_stack,
    )


def first_gradients(
    small_sums, gain, head, grad_gain, backward, patches, hidden, second, logits, cotangent, cotangent_stack,
):
    halves = (slice(0, PART), slice(PART, LANES))
    places = [(parity, i) for parity in range(2) for i in range(6)]
    masks = edges(2)
    for half in halves:
        value = sources(cotangent[0:BAND, half], masks)
        for tap in range(9):
            dy, dz = tap // 3 - 1, tap % 3 - 1
            cotangent_stack[tap * BAND : tap * BAND + BAND, half] = moved(value[1 - dz], -2 * dy, -2 * dz)
    back = nn(backward[...], cotangent_stack[...])
    sum_head = jnp.zeros((CH, PART), jnp.float32)
    for parity, i in places:
        rows, half, plane = slice(i * CH, i * CH + CH), halves[parity], 2 * i + parity
        slope = logits[plane : plane + 1, :]
        normed = second[rows, half] * gain
        joined = (jnp.maximum(normed, 0.0) + hidden[rows, half].astype(jnp.float32)).astype(jnp.bfloat16)
        sum_head = sum_head + joined.astype(jnp.float32) * slope
        whole = back[rows, half] + head * slope
        alive = hidden[rows, half].astype(jnp.float32) > 0.0
        second[rows, half] = jnp.where(alive, whole, 0.0)
    grad_head = sum(crop_sums(sum_head))
    lane = iota((9, 128), 1)
    small = jnp.zeros((9, 128), jnp.float32)
    products = jnp.concatenate([nt(patches[...], second[:, half].astype(jnp.bfloat16)) for half in halves], axis=1)
    row, column = iota((144, 2 * BAND), 0), iota((144, 2 * BAND), 1)
    place = column // CH
    step = row % 16 - (2 * (place % 6) + place // 6) + 1
    for dx in range(3):
        part = jnp.where(step == dx, products, 0.0)
        part = jnp.sum(part.reshape(9, 16, 2 * BAND), axis=1)
        part = part[:, 0:128] + part[:, 128:256] + part[:, 256:384]
        part = part + pltpu.roll(part, 64, 1)
        part = part + pltpu.roll(part, 32, 1)
        small = jnp.where(lane // CH == dx, part, small)
    pick = iota((CH, 128), 0) + 96 == iota((CH, 128), 1)
    small = small + jnp.concatenate(
        [jnp.sum(jnp.where(pick, value, 0.0), axis=0, keepdims=True) for value in (grad_gain, grad_head)]
        + [jnp.where(lane[0:1] >= 96, pltpu.roll(small[8:9], 96 - CH * dx, 1), 0.0) for dx in range(3)]
        + [jnp.zeros((4, 128), jnp.float32)],
        axis=0,
    )
    small_sums[...] = small[0:8]


COMPUTE_SCRATCH = [
    pltpu.VMEM((12 * CH, 144), jnp.bfloat16),
    pltpu.VMEM((BAND, TAPS), jnp.bfloat16),
    pltpu.VMEM((BAND, TAPS), jnp.bfloat16),
    pltpu.VMEM((144, PART), jnp.bfloat16),
    pltpu.VMEM((BAND, LANES), jnp.bfloat16),
    pltpu.VMEM((TAPS, LANES), jnp.bfloat16),
    pltpu.VMEM((BAND, LANES), jnp.float32),
    pltpu.VMEM((16, PART), jnp.float32),
    pltpu.VMEM((256, LANES), jnp.bfloat16),
    pltpu.VMEM((TAPS, LANES), jnp.bfloat16),
]


MESH = pl.DeviceIdType.MESH


def plane_peer(k):
    dp = lax.axis_index("dp")
    x = lax.rem(dp // 32 + k // 4, 4)
    y = lax.rem(lax.rem(dp, 4) + k % 4, 4)
    z = lax.rem(dp // 4, 8)
    return (x * 32 + z * 4 + y, lax.axis_index("pair")), x * 4 + y


def z_peer(k):
    dp = lax.axis_index("dp")
    z = lax.rem(lax.rem(dp // 4, 8) + k, 8)
    return ((dp // 32) * 32 + z * 4 + lax.rem(dp, 4), lax.axis_index("pair")), z


def column_peer(k):
    (dp, _), z = z_peer(k // 2)
    core = lax.rem(lax.axis_index("pair") + k % 2, 2)
    return (dp, core), z * 2 + core


PLANE_STEPS = (10, 6, 9, 11, 14, 2, 5, 7, 8, 13, 15, 1, 3, 4, 12)
Z_STEPS = (4, 3, 5, 2, 6, 1, 7)
COLUMN_STEPS = (9, 8, 7, 6, 11, 10, 5, 4, 13, 12, 3, 2, 15, 14, 1)
CHIPS, DEPTH, COLUMN = (plane_peer, PLANE_STEPS), (z_peer, Z_STEPS), (column_peer, COLUMN_STEPS)
GROUPS = (COLUMN, CHIPS)


def rows_at(place, count):
    return pl.ds(pl.multiple_of(place * count, count), count)


def greet():
    barrier = pltpu.get_barrier_semaphore()
    for peer, steps in GROUPS:
        for k in steps:
            pl.semaphore_signal(barrier, inc=1, device_id=peer(k)[0], device_id_type=MESH)
    return lambda: pl.semaphore_wait(barrier, sum(len(steps) for _, steps in GROUPS))


def exchange(stage, group, source, target, send, recv):
    peer, steps = group
    copies = []
    for k in steps:
        device, place = peer(k)
        copy = pltpu.make_async_remote_copy(
            src_ref=source(place), dst_ref=target, send_sem=send.at[stage, k], recv_sem=recv.at[stage, k],
            device_id=device, device_id_type=MESH,
        )
        copy.start()
        copies.append(copy)
    return copies


def receive(copies, started):
    for copy in copies:
        copy.wait_recv()
    started.extend(copies)


def added(slots):
    total = slots[0].astype(jnp.float32)
    for k in range(1, 16):
        total = total + slots[k].astype(jnp.float32)
    return total


def in_two(value):
    high = value.astype(jnp.bfloat16)
    return jnp.concatenate([high, (value - high.astype(jnp.float32)).astype(jnp.bfloat16)], axis=0)


def reduce_everywhere(packed, finish_gradients, out, leaving, first, second, small, send, recv, started):
    _, place = plane_peer(0)
    _, column = column_peer(0)
    leaving[...] = packed[...].astype(jnp.bfloat16)
    copies = exchange(2, CHIPS, lambda other: leaving.at[rows_at(other, 16)], first.at[place], send, recv)
    first[place] = leaving[rows_at(place, 16)]
    finish_gradients(small)
    second[column, 16:32] = in_two(small[...])
    receive(copies, started)
    second[column, 0:16] = added(first).astype(jnp.bfloat16)
    copies = exchange(3, COLUMN, lambda other: second.at[column], second.at[column], send, recv)
    receive(copies, started)
    total = added(second)
    out[place, 0:16] = total[0:16].astype(jnp.bfloat16)
    out[place, 16:32] = in_two(total[16:24] + total[24:32])
    copies = exchange(4, CHIPS, lambda other: out.at[place], out.at[place], send, recv)
    receive(copies, started)


def crop_table(counts, ids, corners):
    shape = (256, 256)
    count = counts[...].astype(jnp.float32)
    before = onehot(iota(shape, 0) < iota(shape, 1))
    starts = nn(count.astype(jnp.bfloat16), before)
    number = (iota(shape, 0) + 256 * lax.axis_index("pair")).astype(jnp.float32)
    total = jnp.zeros((256, 4), jnp.float32)
    for s in range(MOST):
        chosen = onehot((number == starts + s) & (count > s))
        table = jnp.concatenate([ids[s : s + 1, :], corners[s]], axis=0)
        total = total + nt(chosen, table.astype(jnp.bfloat16))
    return total


def as_number(condition_shape, axis):
    return iota(condition_shape, axis).astype(jnp.float32)


def column(ref):
    eye = iota((CH, CH), 0) == iota((CH, CH), 1)
    return jnp.sum(jnp.where(eye, ref[...], 0.0), axis=1, keepdims=True)


def step_kernel(
    pool_at, counts_at, ids_at, corners_at, conv_first_at, conv_second_at, gain_at, head_at, *refs
):
    small_at, moments_at, (out, small, *moments), refs = refs[0:6], refs[6:8], refs[8:12], refs[12:]
    (
    pool, counts, ids, corners, conv_first, conv_second, gain_ref, head_ref, loaded,
    gathered, arrived, leaving, landed, spots, packed, summands, first, second_sums, small_sums, send, recv,
    toeplitz_first, forward, backward, patches, hidden, hidden_stack, second, logits, cotangent, cotangent_stack,
    ) = refs
    wait_for_all, started = greet(), []
    pairs = (
        (counts_at, counts), (ids_at, ids), (corners_at, corners), (pool_at, pool),
        (conv_first_at, conv_first), (conv_second_at, conv_second), (gain_at, gain_ref), (head_at, head_ref),
    ) + tuple((source, small.at[k, 0 : source.shape[0]]) for k, source in enumerate(small_at)) + tuple(zip(moments_at, moments))
    loads = [pltpu.make_async_copy(*pair, loaded.at[k]) for k, pair in enumerate(pairs)]
    for load in loads[0:4]:
        load.start()
    _, place = plane_peer(0)
    _, z = z_peer(0)
    for load in loads[0:3]:
        load.wait()
    table = crop_table(counts, ids, corners)
    loads[3].wait()
    blocks = pool[...].reshape(512, 256)
    depth = table[:, 3:4].astype(jnp.int32)
    narrow = onehot(
        (iota((256, 128), 0) // BLOCK == iota((256, 128), 1) // SIDE)
        & (iota((256, 128), 0) % BLOCK == iota((256, 128), 1) % SIDE)
    )
    for c in range(2):
        chosen = onehot(2.0 * table[:, 0:1] + c == as_number((256, 512), 1))
        slab = nn(chosen, blocks)
        parts = []
        for part in (slab[:, 0:128], slab[:, 128:256]):
            for bit in (16, 8, 4, 2, 1):
                part = jnp.where((depth & bit) != 0, pltpu.roll(part, 128 - bit, 1), part)
            parts.append(part)
        cut = jnp.concatenate(parts, axis=1).astype(jnp.bfloat16)
        gathered[:, 128 * c : 128 * c + 128] = nn(cut, narrow).astype(jnp.bfloat16)
    wait_for_all()
    copies = exchange(0, CHIPS, lambda other: gathered.at[rows_at(other, 16)], arrived.at[rows_at(place, 16)], send, recv)
    for load in loads[4:]:
        load.start()
    arrived[rows_at(place, 16)] = gathered[rows_at(place, 16)]
    for load in loads[4:]:
        load.wait()
    expand_first(conv_first, toeplitz_first)
    expand_second(conv_second, forward, backward)
    table = table.astype(jnp.bfloat16)
    row = iota((128, 1), 0)
    crop = row // 16 * 2 + row % 16 // 8
    about = nn(onehot(iota((128, 256), 1) == place * 16 + crop), table)
    x = jnp.floor((about[:, 1:2] - z.astype(jnp.float32) + 7.0) * 0.125) + (row % 8 // 4).astype(jnp.float32)
    wanted = (x * 4.0 + (row % 4).astype(jnp.float32)) * 16.0 + crop.astype(jnp.float32)
    chosen = onehot(wanted == as_number((128, 256), 1))
    receive(copies, started)
    leaving[...] = nn(chosen, arrived[...]).astype(jnp.bfloat16)
    copies = exchange(1, DEPTH, lambda other: leaving.at[rows_at(other, 16)], landed.at[rows_at(z, 16)], send, recv)
    landed[rows_at(z, 16)] = leaving[rows_at(z, 16)]
    gain = column(gain_ref)
    head = column(head_ref).astype(jnp.bfloat16).astype(jnp.float32)
    row = iota((128, 1), 0)
    s, p = row % 32 // 16, row % 16
    about = nn(onehot(iota((128, 256), 1) == place * 16 + z * 2 + s), table)
    x = about[:, 1:2] + p.astype(jnp.float32)
    wanted = (x - 8.0 * jnp.floor(x * 0.125)) * 16.0 + (s * 8 + p // 8 * 4 + row // 32).astype(jnp.float32)
    chosen = onehot((wanted == as_number((128, 128), 1)) & (p < CROP))
    lane = iota((1, PART), 1)
    for s in range(2):
        y = about[16 * s : 16 * s + 1, 2:3] + (lane % PITCH // CROP).astype(jnp.float32)
        spot = y * SIDE + (lane % PITCH % CROP).astype(jnp.float32)
        inside = in_crop() & (lane // PITCH == s)
        spots[s] = onehot(jnp.where(inside, spot, -1.0) == as_number((512, PART), 0))
    receive(copies, started)
    planes = nn(chosen, landed[...]).astype(jnp.bfloat16)
    window = jnp.zeros((32, PART), jnp.float32)
    for s in range(2):
        whole = jnp.concatenate(
            [
                jnp.concatenate([planes[32 * q + 16 * s : 32 * q + 16 * s + 16, 128 * c : 128 * c + 128] for q in range(4)], axis=1)
                for c in range(2)
            ],
            axis=0,
        )
        window = window + nn(whole, spots[s])
    packed[216:256, :] = jnp.zeros((40, 128), jnp.float32)
    finish_gradients = crop_gradients(
        window[0:16], window[16:28], gain, head, packed,
        toeplitz_first, forward, backward, patches, hidden, hidden_stack, second, logits, cotangent, cotangent_stack,
    )
    reduce_everywhere(
        packed, finish_gradients, out, summands, first, second_sums, small_sums, send, recv, started
    )
    for copy in started:
        copy.wait_send()


SCRATCH = [
    pltpu.VMEM((256, 2, 256), jnp.bfloat16),
    pltpu.VMEM((1, 256), jnp.int32),
    pltpu.VMEM((MOST, 256), jnp.int32),
    pltpu.VMEM((MOST, 3, 256), jnp.int32),
    pltpu.VMEM((27, CH), jnp.float32),
    pltpu.VMEM((27, CH, CH), jnp.float32),
    pltpu.VMEM((1, CH), jnp.float32),
    pltpu.VMEM((1, CH), jnp.float32),
    pltpu.SemaphoreType.DMA((16,)),
    pltpu.VMEM((256, 256), jnp.bfloat16),
    pltpu.VMEM((256, 256), jnp.bfloat16),
    pltpu.VMEM((128, 256), jnp.bfloat16),
    pltpu.VMEM((128, 256), jnp.bfloat16),
    pltpu.VMEM((2, 512, PART), jnp.bfloat16),
    pltpu.VMEM((256, 128), jnp.float32),
    pltpu.VMEM((256, 128), jnp.bfloat16),
    pltpu.VMEM((16, 16, 128), jnp.bfloat16),
    pltpu.VMEM((16, 32, 128), jnp.bfloat16),
    pltpu.VMEM((8, 128), jnp.float32),
    pltpu.SemaphoreType.DMA((5, 16)),
    pltpu.SemaphoreType.DMA((5, 16)),
]


def summed_gradients(pool, crop_ids, crop_corners, counts, conv_first, conv_second, norm_gain, head_weight, small, large):
    return pl.pallas_call(
        step_kernel,
        out_shape=[jax.ShapeDtypeStruct((16, 32, 128), jnp.bfloat16), jax.ShapeDtypeStruct((6, 32, CH), jnp.float32)]
        + [jax.ShapeDtypeStruct((27, CH, CH), jnp.float32)] * 2,
        in_specs=[pl.BlockSpec(memory_space=pltpu.HBM)] * 16,
        out_specs=[pl.BlockSpec(memory_space=pltpu.VMEM)] * 4,
        scratch_shapes=SCRATCH + COMPUTE_SCRATCH,
        compiler_params=pltpu.CompilerParams(
            collective_id=0, has_side_effects=True, vmem_limit_bytes=20 * 1024 * 1024
        ),
    )(*[
        pltpu.with_memory_space_constraint(value, pltpu.HBM)
        for value in (
            pool, counts.reshape(1, 256), crop_ids.T, crop_corners.transpose(1, 2, 0),
            conv_first, conv_second, norm_gain.reshape(1, CH), head_weight.reshape(1, CH),
            *[value.reshape(-1, CH) for value in small],
            *large,
        )
    ])


beta_first = 0.9
beta_second = 0.999


def adam_update(gradient, momentum, variance):
    next_momentum = beta_first * momentum + (1.0 - beta_first) * gradient
    next_variance = beta_second * variance + (1.0 - beta_second) * gradient * gradient
    return next_momentum / (jnp.sqrt(next_variance) + 1e-08), next_momentum


def adam_kernel(inverse_batch, total, small, moment, variance, *refs):
    updates, nexts = refs[0:4], refs[4:8]
    gradient = total[:, 0:16].astype(jnp.float32).reshape(256, 128) * inverse_batch
    small_gradient = added(total[:, 16:32])
    small_gradient = (small_gradient[0:8] + small_gradient[8:16]) * inverse_batch
    for dx in range(3):
        j = 2 - dx
        part = jnp.concatenate(
            [gradient[0:216, CH * j : CH * j + CH], gradient[72 * j : 72 * j + 72, 96:128]], axis=0
        ).reshape(9, CH, CH)
        taps = slice(9 * dx, 9 * dx + 9)
        updates[1][taps], nexts[1][taps] = adam_update(part, moment[taps], variance[taps])
        part = jnp.concatenate([small_gradient[:, CH * dx : CH * dx + CH], small_gradient[2 + dx : 3 + dx, 96:128]], axis=0)
        updates[0][taps], nexts[0][taps] = adam_update(part, small[0, taps], small[3, taps])
    for k in (1, 2):
        part = small_gradient[k - 1 : k, 96:128]
        updates[k + 1][...], nexts[k + 1][...] = adam_update(part, small[k, 0:1], small[k + 3, 0:1])


def adam(batch_size, total, small, moment, variance):
    shapes = [jax.ShapeDtypeStruct(shape, jnp.float32) for shape in ((27, CH), (27, CH, CH), (1, CH), (1, CH))]
    results = pl.pallas_call(
        functools.partial(adam_kernel, 1.0 / batch_size),
        out_shape=shapes + shapes,
        in_specs=[pl.BlockSpec(memory_space=pltpu.VMEM)] * 4,
        out_specs=[pl.BlockSpec(memory_space=pltpu.VMEM)] * 8,
        compiler_params=pltpu.CompilerParams(vmem_limit_bytes=8 * 1024 * 1024),
    )(total, small, moment, variance)
    return tuple(value.reshape(CH) if value.shape == (1, CH) else value for value in results)


SHARE = 2


def shards(
    pool, crop_ids, crop_corners, counts, conv_first, conv_second, norm_gain, head_weight,
    momentum_first, momentum_second, momentum_gain, momentum_head,
    variance_first, variance_second, variance_gain, variance_head,
):
    moved_on = summed_gradients(
        pool, crop_ids, crop_corners, counts, conv_first, conv_second, norm_gain, head_weight,
        (momentum_first, momentum_gain, momentum_head, variance_first, variance_gain, variance_head),
        (momentum_second, variance_second),
    )
    return adam(counts.shape[0] * SHARE, *moved_on)


def solution(mesh):
    in_specs = (P(None, None, "dp"),) + (P(),) * 15
    return jax.shard_map(shards, mesh=mesh, in_specs=in_specs, out_specs=(P(),) * 8, check_vma=False)
```

```python
import functools

import jax
import jax.numpy as jnp
from jax import lax
from jax.experimental import pallas as pl
from jax.experimental.pallas import tpu as pltpu
from jax.sharding import PartitionSpec as P

CH = 32
CROP = 12
BLOCK = 32
MOST = 3


SIDE = 16
PLANE = CROP * CROP
PITCH = PLANE + 2 * CROP
PART = 384
LANES = 2 * PART
VOXELS = CROP * CROP * CROP
BAND = 6 * CH
TAPS = 9 * BAND


def iota(shape, axis):
    return lax.broadcasted_iota(jnp.int32, shape, axis)


def nt(a, b):
    return lax.dot_general(a, b, (((1,), (1,)), ((), ())), preferred_element_type=jnp.float32)


def nn(a, b):
    return jnp.dot(a, b, preferred_element_type=jnp.float32)


def onehot(condition):
    return jnp.where(condition, 1.0, 0.0).astype(jnp.bfloat16)


def in_crop():
    lane = iota((1, PART), 1)
    return (lane < 2 * PITCH) & (lane % PITCH < PLANE)


def edges(reach):
    z = iota((1, PART), 1) % PITCH % CROP
    return z < CROP - reach, None, z >= reach


def sources(value, masks):
    value = value.astype(jnp.bfloat16)
    return [value if mask is None else jnp.where(mask, value, jnp.zeros_like(value)) for mask in masks]


def moved(source, dy, dz):
    amount = (-(CROP * dy + dz)) % PART
    return (pltpu.roll(source, amount, 1) if amount else source).astype(jnp.bfloat16)


def by_crop(columns):
    return jnp.where(iota((1, PART), 1) < PITCH, columns[0], columns[1])


def crop_sums(value):
    lane = iota((1, PART), 1)
    value = jnp.where(in_crop(), value, 0.0)
    first = jnp.sum(jnp.where(lane < PITCH, value, 0.0), axis=1, keepdims=True)
    return first, jnp.sum(jnp.where(lane >= PITCH, value, 0.0), axis=1, keepdims=True)


def expand_first(conv_first, toeplitz_first):
    weights = conv_first[...].astype(jnp.bfloat16)
    repeat = onehot(iota((12 * CH, CH), 0) % CH == iota((12 * CH, CH), 1))
    row, column = iota((12 * CH, 144), 0), iota((12 * CH, 144), 1)
    place = row // CH
    step = column % 16 - (2 * (place % 6) + place // 6) + 1
    total = jnp.zeros((12 * CH, 144), jnp.float32)
    for dx in range(3):
        tap = onehot(iota((144, 27), 0) // 16 + 9 * dx == iota((144, 27), 1))
        spread = nn(tap, weights).astype(jnp.bfloat16)
        total = jnp.where(step == dx, nt(repeat, spread), total)
    toeplitz_first[...] = total.astype(jnp.bfloat16)


def expand_second(conv_second, forward, backward):
    eye = onehot(iota((CH, CH), 0) == iota((CH, CH), 1))
    zero = jnp.zeros((CH, 256 - 3 * CH), jnp.float32)
    plain, turned = [], []
    for tap in range(9):
        blocks = [conv_second[9 * dx + tap] for dx in range(3)]
        plain.append(jnp.concatenate([blocks[2], blocks[1], blocks[0], zero], axis=1))
        stacked = jnp.concatenate(blocks, axis=0).astype(jnp.bfloat16)
        turned.append(jnp.concatenate([nt(eye, stacked), zero], axis=1))
    for i in range(6):
        rows = slice(i * CH, i * CH + CH)
        amount = (CH * (i - 1)) % 256
        for strips, matrix in ((plain, backward), (turned, forward)):
            bands = [(pltpu.roll(strip, amount, 1) if amount else strip)[:, 0:BAND] for strip in strips]
            matrix[rows, :] = jnp.concatenate(bands, axis=1).astype(jnp.bfloat16)


def crop_gradients(
    image, target, gain, head, packed,
    toeplitz_first, forward, backward, patches, hidden, hidden_stack, second, logits, cotangent, cotangent_stack,
):
    halves = (slice(0, PART), slice(PART, LANES))
    places = [(parity, i) for parity in range(2) for i in range(6)]
    steps = [(tap // 3 - 1, tap % 3 - 1) for tap in range(9)]
    valid = in_crop()
    image = sources(image, edges(1))
    for tap, (dy, dz) in enumerate(steps):
        patches[tap * 16 : tap * 16 + 16, :] = moved(image[dz + 1], dy, dz)
    masks = edges(2)
    for parity, half in enumerate(halves):
        first_map = nn(toeplitz_first[parity * BAND : parity * BAND + BAND, :], patches[...])
        value = jnp.where(valid, jnp.maximum(first_map, 0.0), 0.0)
        hidden[:, half] = value.astype(jnp.bfloat16)
        value = sources(value, masks)
        for tap, (dy, dz) in enumerate(steps):
            hidden_stack[tap * BAND : tap * BAND + BAND, half] = moved(value[dz + 1], 2 * dy, 2 * dz)
    second[...] = nn(forward[...], hidden_stack[...])
    scale = 1.0 / VOXELS
    total = jnp.zeros((CH, PART), jnp.float32)
    for parity, i in places:
        total = total + second[i * CH : i * CH + CH, halves[parity]]
    center = by_crop([value * scale for value in crop_sums(total)])
    total = jnp.zeros((CH, PART), jnp.float32)
    for parity, i in places:
        away = second[i * CH : i * CH + CH, halves[parity]] - center
        total = total + away * away
    inverse = by_crop([lax.rsqrt(value * scale + 1e-05) for value in crop_sums(total)])
    for parity, i in places:
        rows, half, plane = slice(i * CH, i * CH + CH), halves[parity], 2 * i + parity
        hat = (second[rows, half] - center) * inverse
        second[rows, half] = hat
        joined = (jnp.maximum(hat * gain, 0.0) + hidden[rows, half].astype(jnp.float32)).astype(jnp.bfloat16)
        logits[plane : plane + 1, :] = jnp.sum(joined.astype(jnp.float32) * head, axis=0, keepdims=True)
    slope = 1.0 / (1.0 + jnp.exp(-logits[0:12, :])) - target
    logits[0:12, :] = jnp.where(valid, slope * scale, 0.0)
    sum_plain = jnp.zeros((CH, PART), jnp.float32)
    sum_hat = jnp.zeros((CH, PART), jnp.float32)
    for parity, i in places:
        rows, half, plane = slice(i * CH, i * CH + CH), halves[parity], 2 * i + parity
        hat = second[rows, half]
        normed = hat * gain
        slope = logits[plane : plane + 1, :]
        passed = jnp.where(normed > 0.0, slope, 0.0)
        sum_plain = sum_plain + passed
        sum_hat = sum_hat + passed * hat
    sums_plain = [head * value for value in crop_sums(sum_plain)]
    sums_hat = [head * value for value in crop_sums(sum_hat)]
    grad_gain = sum(sums_hat)
    mean_plain = by_crop([value * scale for value in sums_plain])
    mean_hat = by_crop([value * scale for value in sums_hat])
    factor = jnp.where(valid, inverse * gain, 0.0)
    for parity, i in places:
        rows, half, plane = slice(i * CH, i * CH + CH), halves[parity], 2 * i + parity
        hat = second[rows, half]
        slope = logits[plane : plane + 1, :]
        passed = jnp.where(hat * gain > 0.0, head * slope, 0.0)
        cotangent[rows, half] = (factor * (passed - mean_plain - hat * mean_hat)).astype(jnp.bfloat16)
    cotangent[BAND:256, :] = jnp.zeros((256 - BAND, LANES), jnp.bfloat16)
    turned = cotangent[...].T
    lane = iota((CH, 128), 1)
    for tap in range(9):
        if tap % 3 == 0:
            three = nn(hidden_stack[tap * BAND : tap * BAND + 3 * BAND, :], turned)
        products = three[tap % 3 * BAND : tap % 3 * BAND + BAND]
        low, high = products[:, 0:128], products[:, 128:256]
        band = [slice(i * CH, i * CH + CH) for i in range(6)]
        total = low[band[1]] + high[band[5]] + jnp.where(lane >= CH, pltpu.roll(low[band[0]], CH, 1), 0.0)
        total = total + pltpu.roll(low[band[2]], 96, 1)
        for i, amount in ((3, 64), (4, 32)):
            total = total + pltpu.roll(jnp.where(lane < 128 - amount, high[band[i]], low[band[i]]), amount, 1)
        at = tap * CH
        if at < 216:
            count = min(CH, 216 - at)
            packed[at : at + count, :] = jnp.where(lane < 96, total, 0.0)[0:count]
        if at + CH > 216:
            skip = max(0, 216 - at)
            for j in range(3):
                shifted = pltpu.roll(total, 96 - CH * j, 1)
                shifted = jnp.where(lane >= 96, shifted, 0.0)[skip:CH]
                to = 72 * j + at + skip - 216
                packed[to : to + CH - skip, :] = packed[to : to + CH - skip, :] + shifted
    return lambda small: first_gradients(
        small, gain, head, grad_gain, backward, patches, hidden, second, logits, cotangent, cotangent_stack,
    )


def first_gradients(
    small_sums, gain, head, grad_gain, backward, patches, hidden, second, logits, cotangent, cotangent_stack,
):
    halves = (slice(0, PART), slice(PART, LANES))
    places = [(parity, i) for parity in range(2) for i in range(6)]
    masks = edges(2)
    for half in halves:
        value = sources(cotangent[0:BAND, half], masks)
        for tap in range(9):
            dy, dz = tap // 3 - 1, tap % 3 - 1
            cotangent_stack[tap * BAND : tap * BAND + BAND, half] = moved(value[1 - dz], -2 * dy, -2 * dz)
    back = nn(backward[...], cotangent_stack[...])
    sum_head = jnp.zeros((CH, PART), jnp.float32)
    for parity, i in places:
        rows, half, plane = slice(i * CH, i * CH + CH), halves[parity], 2 * i + parity
        slope = logits[plane : plane + 1, :]
        normed = second[rows, half] * gain
        joined = (jnp.maximum(normed, 0.0) + hidden[rows, half].astype(jnp.float32)).astype(jnp.bfloat16)
        sum_head = sum_head + joined.astype(jnp.float32) * slope
        whole = back[rows, half] + head * slope
        alive = hidden[rows, half].astype(jnp.float32) > 0.0
        second[rows, half] = jnp.where(alive, whole, 0.0)
    grad_head = sum(crop_sums(sum_head))
    lane = iota((9, 128), 1)
    small = jnp.zeros((9, 128), jnp.float32)
    products = jnp.concatenate([nt(patches[...], second[:, half].astype(jnp.bfloat16)) for half in halves], axis=1)
    row, column = iota((144, 2 * BAND), 0), iota((144, 2 * BAND), 1)
    place = column // CH
    step = row % 16 - (2 * (place % 6) + place // 6) + 1
    for dx in range(3):
        part = jnp.where(step == dx, products, 0.0)
        part = jnp.sum(part.reshape(9, 16, 2 * BAND), axis=1)
        part = part[:, 0:128] + part[:, 128:256] + part[:, 256:384]
        part = part + pltpu.roll(part, 64, 1)
        part = part + pltpu.roll(part, 32, 1)
        small = jnp.where(lane // CH == dx, part, small)
    pick = iota((CH, 128), 0) + 96 == iota((CH, 128), 1)
    small = small + jnp.concatenate(
        [jnp.sum(jnp.where(pick, value, 0.0), axis=0, keepdims=True) for value in (grad_gain, grad_head)]
        + [jnp.where(lane[0:1] >= 96, pltpu.roll(small[8:9], 96 - CH * dx, 1), 0.0) for dx in range(3)]
        + [jnp.zeros((4, 128), jnp.float32)],
        axis=0,
    )
    small_sums[...] = small[0:8]


COMPUTE_SCRATCH = [
    pltpu.VMEM((12 * CH, 144), jnp.bfloat16),
    pltpu.VMEM((BAND, TAPS), jnp.bfloat16),
    pltpu.VMEM((BAND, TAPS), jnp.bfloat16),
    pltpu.VMEM((144, PART), jnp.bfloat16),
    pltpu.VMEM((BAND, LANES), jnp.bfloat16),
    pltpu.VMEM((TAPS, LANES), jnp.bfloat16),
    pltpu.VMEM((BAND, LANES), jnp.float32),
    pltpu.VMEM((16, PART), jnp.float32),
    pltpu.VMEM((256, LANES), jnp.bfloat16),
    pltpu.VMEM((TAPS, LANES), jnp.bfloat16),
]


MESH = pl.DeviceIdType.MESH


def plane_peer(k):
    dp = lax.axis_index("dp")
    x = lax.rem(dp // 32 + k // 4, 4)
    y = lax.rem(lax.rem(dp, 4) + k % 4, 4)
    z = lax.rem(dp // 4, 8)
    return (x * 32 + z * 4 + y, lax.axis_index("pair")), x * 4 + y


def z_peer(k):
    dp = lax.axis_index("dp")
    z = lax.rem(lax.rem(dp // 4, 8) + k, 8)
    return ((dp // 32) * 32 + z * 4 + lax.rem(dp, 4), lax.axis_index("pair")), z


def column_peer(k):
    (dp, _), z = z_peer(k // 2)
    core = lax.rem(lax.axis_index("pair") + k % 2, 2)
    return (dp, core), z * 2 + core


PLANE_STEPS = (10, 6, 9, 11, 14, 2, 5, 7, 8, 13, 15, 1, 3, 4, 12)
Z_STEPS = (4, 3, 5, 2, 6, 1, 7)
COLUMN_STEPS = (9, 8, 7, 6, 11, 10, 5, 4, 13, 12, 3, 2, 15, 14, 1)
CHIPS, DEPTH, COLUMN = (plane_peer, PLANE_STEPS), (z_peer, Z_STEPS), (column_peer, COLUMN_STEPS)
GROUPS = (COLUMN, CHIPS)


def rows_at(place, count):
    return pl.ds(pl.multiple_of(place * count, count), count)


def greet():
    barrier = pltpu.get_barrier_semaphore()
    for peer, steps in GROUPS:
        for k in steps:
            pl.semaphore_signal(barrier, inc=1, device_id=peer(k)[0], device_id_type=MESH)
    return lambda: pl.semaphore_wait(barrier, sum(len(steps) for _, steps in GROUPS))


def exchange(stage, group, source, target, send, recv):
    peer, steps = group
    copies = []
    for k in steps:
        device, place = peer(k)
        copy = pltpu.make_async_remote_copy(
            src_ref=source(place), dst_ref=target, send_sem=send.at[stage, k], recv_sem=recv.at[stage, k],
            device_id=device, device_id_type=MESH,
        )
        copy.start()
        copies.append(copy)
    return copies


def finish(copies):
    for copy in copies:
        copy.wait()


def added(slots):
    total = slots[0].astype(jnp.float32)
    for k in range(1, 16):
        total = total + slots[k].astype(jnp.float32)
    return total


def in_two(value):
    high = value.astype(jnp.bfloat16)
    return jnp.concatenate([high, (value - high.astype(jnp.float32)).astype(jnp.bfloat16)], axis=0)


FILLED = 14


def reduce_everywhere(packed, finish_gradients, out, leaving, first, second, small, send, recv):
    _, place = plane_peer(0)
    _, column = column_peer(0)
    leaving[...] = packed[...].astype(jnp.bfloat16)
    peer, steps = CHIPS
    copies = []
    for k in steps:
        device, other = peer(k)
        copy = pltpu.make_async_remote_copy(
            src_ref=leaving.at[rows_at(other, 16)], dst_ref=first.at[place], send_sem=send.at[2, k], recv_sem=recv.at[2, k],
            device_id=device, device_id_type=MESH,
        )
        pl.when(other < FILLED)(copy.start)
        copies.append((copy, other))
    first[place] = leaving[rows_at(place, 16)]
    finish_gradients(small)
    second[column, 16:32] = in_two(small[...])
    for copy, other in copies:
        pl.when(other < FILLED)(copy.wait_send)

    @pl.when(place < FILLED)
    def _():
        for copy, _ in copies:
            copy.wait_recv()
        second[column, 0:16] = added(first).astype(jnp.bfloat16)

    @pl.when(place >= FILLED)
    def _():
        second[column, 0:16] = jnp.zeros((16, 128), jnp.bfloat16)

    copies = exchange(3, COLUMN, lambda other: second.at[column], second.at[column], send, recv)
    finish(copies)
    total = added(second)
    out[place, 0:16] = total[0:16].astype(jnp.bfloat16)
    out[place, 16:32] = in_two(total[16:24] + total[24:32])
    copies = exchange(4, CHIPS, lambda other: out.at[place], out.at[place], send, recv)
    finish(copies)


def crop_table(counts, ids, corners):
    shape = (256, 256)
    count = counts[...].astype(jnp.float32)
    before = onehot(iota(shape, 0) < iota(shape, 1))
    starts = nn(count.astype(jnp.bfloat16), before)
    number = (iota(shape, 0) + 256 * lax.axis_index("pair")).astype(jnp.float32)
    total = jnp.zeros((256, 4), jnp.float32)
    for s in range(MOST):
        chosen = onehot((number == starts + s) & (count > s))
        table = jnp.concatenate([ids[s : s + 1, :], corners[s]], axis=0)
        total = total + nt(chosen, table.astype(jnp.bfloat16))
    return total


def as_number(condition_shape, axis):
    return iota(condition_shape, axis).astype(jnp.float32)


def column(ref):
    eye = iota((CH, CH), 0) == iota((CH, CH), 1)
    return jnp.sum(jnp.where(eye, ref[...], 0.0), axis=1, keepdims=True)


def step_kernel(
    pool_at, counts_at, ids_at, corners_at, conv_first_at, conv_second_at, gain_at, head_at, *refs
):
    small_at, moments_at, (out, small, *moments), refs = refs[0:6], refs[6:8], refs[8:12], refs[12:]
    (
    pool, counts, ids, corners, conv_first, conv_second, gain_ref, head_ref, loaded,
    gathered, arrived, leaving, landed, spots, packed, summands, first, second_sums, small_sums, send, recv,
    toeplitz_first, forward, backward, patches, hidden, hidden_stack, second, logits, cotangent, cotangent_stack,
    ) = refs
    wait_for_all = greet()
    pairs = (
        (counts_at, counts), (ids_at, ids), (corners_at, corners), (pool_at, pool),
        (conv_first_at, conv_first), (conv_second_at, conv_second), (gain_at, gain_ref), (head_at, head_ref),
    ) + tuple((source, small.at[k, 0 : source.shape[0]]) for k, source in enumerate(small_at)) + tuple(zip(moments_at, moments))
    loads = [pltpu.make_async_copy(*pair, loaded.at[k]) for k, pair in enumerate(pairs)]
    for load in loads:
        load.start()
    _, place = plane_peer(0)
    _, z = z_peer(0)
    for load in loads[0:3]:
        load.wait()
    table = crop_table(counts, ids, corners)
    loads[3].wait()
    blocks = pool[...].reshape(512, 256)
    depth = table[:, 3:4].astype(jnp.int32)
    narrow = onehot(
        (iota((256, 128), 0) // BLOCK == iota((256, 128), 1) // SIDE)
        & (iota((256, 128), 0) % BLOCK == iota((256, 128), 1) % SIDE)
    )
    for c in range(2):
        chosen = onehot(2.0 * table[:, 0:1] + c == as_number((256, 512), 1))
        slab = nn(chosen, blocks)
        parts = []
        for part in (slab[:, 0:128], slab[:, 128:256]):
            for bit in (16, 8, 4, 2, 1):
                part = jnp.where((depth & bit) != 0, pltpu.roll(part, 128 - bit, 1), part)
            parts.append(part)
        cut = jnp.concatenate(parts, axis=1).astype(jnp.bfloat16)
        gathered[:, 128 * c : 128 * c + 128] = nn(cut, narrow).astype(jnp.bfloat16)
    wait_for_all()
    copies = exchange(0, CHIPS, lambda other: gathered.at[rows_at(other, 16)], arrived.at[rows_at(place, 16)], send, recv)
    arrived[rows_at(place, 16)] = gathered[rows_at(place, 16)]
    for load in loads[4:]:
        load.wait()
    expand_first(conv_first, toeplitz_first)
    expand_second(conv_second, forward, backward)
    table = table.astype(jnp.bfloat16)
    row = iota((128, 1), 0)
    crop = row // 16 * 2 + row % 16 // 8
    about = nn(onehot(iota((128, 256), 1) == place * 16 + crop), table)
    x = jnp.floor((about[:, 1:2] - z.astype(jnp.float32) + 7.0) * 0.125) + (row % 8 // 4).astype(jnp.float32)
    wanted = (x * 4.0 + (row % 4).astype(jnp.float32)) * 16.0 + crop.astype(jnp.float32)
    chosen = onehot(wanted == as_number((128, 256), 1))
    finish(copies)
    leaving[...] = nn(chosen, arrived[...]).astype(jnp.bfloat16)
    copies = exchange(1, DEPTH, lambda other: leaving.at[rows_at(other, 16)], landed.at[rows_at(z, 16)], send, recv)
    landed[rows_at(z, 16)] = leaving[rows_at(z, 16)]
    gain = column(gain_ref)
    head = column(head_ref).astype(jnp.bfloat16).astype(jnp.float32)
    row = iota((128, 1), 0)
    s, p = row % 32 // 16, row % 16
    about = nn(onehot(iota((128, 256), 1) == place * 16 + z * 2 + s), table)
    x = about[:, 1:2] + p.astype(jnp.float32)
    wanted = (x - 8.0 * jnp.floor(x * 0.125)) * 16.0 + (s * 8 + p // 8 * 4 + row // 32).astype(jnp.float32)
    chosen = onehot((wanted == as_number((128, 128), 1)) & (p < CROP))
    lane = iota((1, PART), 1)
    for s in range(2):
        y = about[16 * s : 16 * s + 1, 2:3] + (lane % PITCH // CROP).astype(jnp.float32)
        spot = y * SIDE + (lane % PITCH % CROP).astype(jnp.float32)
        inside = in_crop() & (lane // PITCH == s)
        spots[s] = onehot(jnp.where(inside, spot, -1.0) == as_number((512, PART), 0))
    finish(copies)
    planes = nn(chosen, landed[...]).astype(jnp.bfloat16)
    window = jnp.zeros((32, PART), jnp.float32)
    for s in range(2):
        whole = jnp.concatenate(
            [
                jnp.concatenate([planes[32 * q + 16 * s : 32 * q + 16 * s + 16, 128 * c : 128 * c + 128] for q in range(4)], axis=1)
                for c in range(2)
            ],
            axis=0,
        )
        window = window + nn(whole, spots[s])
    packed[216:256, :] = jnp.zeros((40, 128), jnp.float32)
    finish_gradients = crop_gradients(
        window[0:16], window[16:28], gain, head, packed,
        toeplitz_first, forward, backward, patches, hidden, hidden_stack, second, logits, cotangent, cotangent_stack,
    )
    reduce_everywhere(
        packed, finish_gradients, out, summands, first, second_sums, small_sums, send, recv
    )


SCRATCH = [
    pltpu.VMEM((256, 2, 256), jnp.bfloat16),
    pltpu.VMEM((1, 256), jnp.int32),
    pltpu.VMEM((MOST, 256), jnp.int32),
    pltpu.VMEM((MOST, 3, 256), jnp.int32),
    pltpu.VMEM((27, CH), jnp.float32),
    pltpu.VMEM((27, CH, CH), jnp.float32),
    pltpu.VMEM((1, CH), jnp.float32),
    pltpu.VMEM((1, CH), jnp.float32),
    pltpu.SemaphoreType.DMA((16,)),
    pltpu.VMEM((256, 256), jnp.bfloat16),
    pltpu.VMEM((256, 256), jnp.bfloat16),
    pltpu.VMEM((128, 256), jnp.bfloat16),
    pltpu.VMEM((128, 256), jnp.bfloat16),
    pltpu.VMEM((2, 512, PART), jnp.bfloat16),
    pltpu.VMEM((256, 128), jnp.float32),
    pltpu.VMEM((256, 128), jnp.bfloat16),
    pltpu.VMEM((16, 16, 128), jnp.bfloat16),
    pltpu.VMEM((16, 32, 128), jnp.bfloat16),
    pltpu.VMEM((8, 128), jnp.float32),
    pltpu.SemaphoreType.DMA((5, 16)),
    pltpu.SemaphoreType.DMA((5, 16)),
]


def summed_gradients(pool, crop_ids, crop_corners, counts, conv_first, conv_second, norm_gain, head_weight, small, large):
    return pl.pallas_call(
        step_kernel,
        out_shape=[jax.ShapeDtypeStruct((16, 32, 128), jnp.bfloat16), jax.ShapeDtypeStruct((6, 32, CH), jnp.float32)]
        + [jax.ShapeDtypeStruct((27, CH, CH), jnp.float32)] * 2,
        in_specs=[pl.BlockSpec(memory_space=pltpu.HBM)] * 16,
        out_specs=[pl.BlockSpec(memory_space=pltpu.VMEM)] * 4,
        scratch_shapes=SCRATCH + COMPUTE_SCRATCH,
        compiler_params=pltpu.CompilerParams(
            collective_id=0, has_side_effects=True, vmem_limit_bytes=20 * 1024 * 1024
        ),
    )(*[
        pltpu.with_memory_space_constraint(value, pltpu.HBM)
        for value in (
            pool, counts.reshape(1, 256), crop_ids.T, crop_corners.transpose(1, 2, 0),
            conv_first, conv_second, norm_gain.reshape(1, CH), head_weight.reshape(1, CH),
            *[value.reshape(-1, CH) for value in small],
            *large,
        )
    ])


beta_first = 0.9
beta_second = 0.999


def adam_update(gradient, momentum, variance):
    next_momentum = beta_first * momentum + (1.0 - beta_first) * gradient
    next_variance = beta_second * variance + (1.0 - beta_second) * gradient * gradient
    return next_momentum / (jnp.sqrt(next_variance) + 1e-08), next_momentum


def adam_kernel(inverse_batch, total, small, moment, variance, *refs):
    updates, nexts = refs[0:4], refs[4:8]
    gradient = total[:, 0:16].astype(jnp.float32).reshape(256, 128) * inverse_batch
    small_gradient = added(total[:, 16:32])
    small_gradient = (small_gradient[0:8] + small_gradient[8:16]) * inverse_batch
    for dx in range(3):
        j = 2 - dx
        part = jnp.concatenate(
            [gradient[0:216, CH * j : CH * j + CH], gradient[72 * j : 72 * j + 72, 96:128]], axis=0
        ).reshape(9, CH, CH)
        taps = slice(9 * dx, 9 * dx + 9)
        updates[1][taps], nexts[1][taps] = adam_update(part, moment[taps], variance[taps])
        part = jnp.concatenate([small_gradient[:, CH * dx : CH * dx + CH], small_gradient[2 + dx : 3 + dx, 96:128]], axis=0)
        updates[0][taps], nexts[0][taps] = adam_update(part, small[0, taps], small[3, taps])
    for k in (1, 2):
        part = small_gradient[k - 1 : k, 96:128]
        updates[k + 1][...], nexts[k + 1][...] = adam_update(part, small[k, 0:1], small[k + 3, 0:1])


def adam(batch_size, total, small, moment, variance):
    shapes = [jax.ShapeDtypeStruct(shape, jnp.float32) for shape in ((27, CH), (27, CH, CH), (1, CH), (1, CH))]
    results = pl.pallas_call(
        functools.partial(adam_kernel, 1.0 / batch_size),
        out_shape=shapes + shapes,
        in_specs=[pl.BlockSpec(memory_space=pltpu.VMEM)] * 4,
        out_specs=[pl.BlockSpec(memory_space=pltpu.VMEM)] * 8,
        compiler_params=pltpu.CompilerParams(vmem_limit_bytes=8 * 1024 * 1024),
    )(total, small, moment, variance)
    return tuple(value.reshape(CH) if value.shape == (1, CH) else value for value in results)


SHARE = 2


def shards(
    pool, crop_ids, crop_corners, counts, conv_first, conv_second, norm_gain, head_weight,
    momentum_first, momentum_second, momentum_gain, momentum_head,
    variance_first, variance_second, variance_gain, variance_head,
):
    moved_on = summed_gradients(
        pool, crop_ids, crop_corners, counts, conv_first, conv_second, norm_gain, head_weight,
        (momentum_first, momentum_gain, momentum_head, variance_first, variance_gain, variance_head),
        (momentum_second, variance_second),
    )
    return adam(counts.shape[0] * SHARE, *moved_on)


def solution(mesh):
    in_specs = (P(None, None, "dp"),) + (P(),) * 15
    return jax.shard_map(shards, mesh=mesh, in_specs=in_specs, out_specs=(P(),) * 8, check_vma=False)
```
